32 devices in a mesh: gx: 4 (over z), gy: 8 (over y, x, core).
Axes of the slice: x: 2, y: 2, z: 4, core: 2. Of those that a mesh axis runs over, the one named last changes fastest.
Arguments:
- adjoint_guess: float32 [16, 128, 256], P('gx', 'gy'), may hold values from -80 to 80, as said below
- velocity: float32 [3, 16, 4096], P(None, 'gx', 'gy'), may hold values from -1 to 1
- leaf_rate: float32 [16, 4096], P('gx', 'gy'), may hold values from 0.2 to 5
- canopy: int32 [16, 4096], P('gx', 'gy'), may hold values from 0 to 1, as said below
- solid: int32 [16, 4096], P('gx', 'gy'), may hold values from 0 to 1, as said below
- receptors: int32 [8], replicated, may hold values from 0 to 2047
Outputs:
- adjoint_field: float32 [16, 128, 256], P('gx', 'gy')
- residual: float32 [16, 128, 256], P('gx', 'gy')
The draws below stay inside these ranges and needn't reach their ends.
Inputs may be any that keep to these rules, and one draw needn't show every extreme that they name: `adjoint_guess`: finite values. 1 marks building cells; every horizontal column is solid from the ground up to its building's height. `canopy`: 1 marks tree-crown cells; none is solid.
All inputs are finite; a program needn't handle non-finite values.
Results may differ from the reference program's by a relative error of at most 0.0003.
Values sent between devices are 32-bit elements; how exact they have to be, the bound alone decides.
No kernel may reach another device: no remote copies, remote signals or barrier semaphores. Data moves between devices by JAX's collectives and lax.ppermute only.
A program may use at most 64 MiB of HBM per device.

```python
import math
import jax
import jax.numpy as jnp

NZ = 32
R = 8
CYCLES = 3
NX = 16
NY = 128


def street_columns(key):
    base_key = jax.random.fold_in(key, 11)
    keys = jax.random.split(base_key, 5)
    building = (jax.random.randint(keys[0], (NX, NY), 0, 4) == 0).astype(jnp.int32)
    height = jax.random.randint(keys[1], (NX, NY), 3, NZ // 2 + 1) * building
    tree = (jax.random.randint(keys[2], (NX, NY), 0, 3) == 0).astype(jnp.int32) * (1 - building)
    crown_top = jax.random.randint(keys[3], (NX, NY), 4, NZ // 2 + 1)
    crown_base = jax.random.randint(keys[4], (NX, NY), 1, 3)
    levels = jnp.arange(NZ, dtype=jnp.int32)
    solid_cells = (levels[None, None, :] < height[:, :, None]).astype(jnp.int32)
    crown = (levels[None, None, :] >= crown_base[:, :, None]) & (levels[None, None, :] < crown_top[:, :, None])
    canopy_cells = crown.astype(jnp.int32) * tree[:, :, None]
    return (solid_cells.reshape(NX, NY * NZ), canopy_cells.reshape(NX, NY * NZ))


def draw_solid(key, part):
    return street_columns(key)[0]


def draw_canopy(key, part):
    return street_columns(key)[1]


def draw_adjoint_guess(key, part):
    row_pos = jnp.arange(NX, dtype=jnp.float32) / max(NX - 1, 1)
    col_pos = jnp.arange(NY, dtype=jnp.float32) / max(NY - 1, 1)
    lane_pos = (jnp.arange(NZ * R) % R).astype(jnp.float32) / R
    base = jnp.clip(jax.random.normal(key, (NX, NY, NZ * R), jnp.float32), -4.0, 4.0)
    scale = jnp.exp(jnp.log(3.0) * row_pos)[:, None, None] * jnp.exp(jnp.log(3.0) * col_pos)[None, :, None]
    return (base * scale * (1.0 + lane_pos)[None, None, :]).astype(jnp.float32)


def place_ends(entries, rng, least, largest):
    longest = entries.shape.index(max(entries.shape))
    spots = []
    for shift in (0, 1):
        where = [jax.random.randint(jax.random.fold_in(rng, axis), (), 0, length) for axis, length in enumerate(entries.shape)]
        where[longest] = (where[longest] + shift) % entries.shape[longest]
        spots.append(tuple(where))
    return entries.at[spots[0]].set(least).at[spots[1]].set(largest)


def block_levels(rng, shape, cuts, least, largest):
    factor_of, own = 1.0, jax.random.fold_in(rng, 6)
    for position, blocks in cuts:
        draws = jnp.exp(jax.random.uniform(jax.random.fold_in(own, position), (blocks,), jnp.float32, least / len(cuts), largest / len(cuts)))
        factor_of = factor_of * jnp.repeat(draws, shape[position] // blocks).reshape([-1 if axis == position else 1 for axis in range(len(shape))])
    return factor_of


def setup_inputs(seed: int = 0) -> dict:
    streams_of = jax.random.split(jax.random.key(seed), 7)
    adjoint_guess = draw_adjoint_guess(jax.random.fold_in(streams_of[6], 71), 0)
    velocity = jnp.clip(jax.random.uniform(streams_of[1], (3, NX, NY * NZ), jnp.float32, -1.0, 1.0) * block_levels(streams_of[1], (3, NX, NY * NZ), ((1, 4), (2, 8)), -0.4, 0.0), -1.0, 1.0)
    leaf_rate = jnp.clip(jnp.exp(math.log(5.0) - 3.218876 * jax.random.uniform(streams_of[2], (NX, NY * NZ), jnp.float32) ** block_levels(streams_of[2], (NX, NY * NZ), ((0, 4), (1, 8)), -0.2, 0.2)), 0.2, 5.0)
    canopy = draw_canopy(jax.random.fold_in(streams_of[6], 71), 0)
    solid = draw_solid(jax.random.fold_in(streams_of[6], 71), 0)
    receptors = place_ends(jax.random.randint(streams_of[5], (R,), 0, NX * NY), jax.random.fold_in(streams_of[5], 1), 0, (NX * NY) - 1).astype(jnp.int32)
    return {"adjoint_guess": adjoint_guess, "velocity": velocity, "leaf_rate": leaf_rate, "canopy": canopy, "solid": solid, "receptors": receptors}


horiz_diff = 4.0
vert_diff = 2.0
decay_rate = 3.5
penalty = 40.0
leaf_gain = 4.0
source_gain = 32.0


def coefficient_fields(flows, reaction):
    east_flow = flows[0]
    north_flow = flows[1]
    rise_flow = flows[2]
    couplings = [horiz_diff + jax.nn.relu(east_flow), horiz_diff + jax.nn.relu(-east_flow),
                 horiz_diff + jax.nn.relu(north_flow), horiz_diff + jax.nn.relu(-north_flow),
                 vert_diff + jax.nn.relu(rise_flow), vert_diff + jax.nn.relu(-rise_flow)]
    diagonal = decay_rate + reaction + couplings[0] + couplings[1] + couplings[2] + couplings[3] + couplings[4] + couplings[5]
    return [jnp.repeat(piece, R, axis=-1) for piece in [diagonal] + couplings]


def apply_operator(padded, coefficients):
    centre = padded[1:-1, 1:-1]
    zero_lane = jnp.zeros(centre.shape[:-1] + (R,), jnp.float32)
    upper_cells = jnp.concatenate([centre[..., R:], zero_lane], axis=-1)
    lower_cells = jnp.concatenate([zero_lane, centre[..., :-R]], axis=-1)
    diagonal, east_c, west_c, north_c, south_c, upper_c, lower_c = coefficients
    return (diagonal * centre - east_c * padded[2:, 1:-1] - west_c * padded[:-2, 1:-1]
            - north_c * padded[1:-1, 2:] - south_c * padded[1:-1, :-2]
            - upper_c * upper_cells - lower_c * lower_cells)


def per_receptor(first, second):
    return jnp.sum((first * second).reshape(-1, R), axis=0)


def spread_lanes(values):
    return jnp.tile(values, NZ)


def reference(adjoint_guess, velocity, leaf_rate, canopy, solid, receptors):
    flows = velocity.reshape(3, NX, NY, NZ)
    reaction = (penalty * solid.astype(jnp.float32) + leaf_gain * leaf_rate * canopy.astype(jnp.float32)).reshape(NX, NY, NZ)
    coefficients = coefficient_fields(flows, reaction)

    def operate(values):
        return apply_operator(jnp.pad(values, ((1, 1), (1, 1), (0, 0))), coefficients)

    rec_rows = (receptors // NY).astype(jnp.int32)
    rec_cols = (receptors % NY).astype(jnp.int32)
    lanes = (R + jnp.arange(R)).astype(jnp.int32)
    source = jnp.zeros((NX, NY, NZ * R), jnp.float32).at[rec_rows, rec_cols, lanes].add(source_gain)
    iterate = adjoint_guess
    residual = source - operate(iterate)
    for cycle_index in range(CYCLES):
        image_dir = operate(residual)
        alpha_step = per_receptor(residual, residual) / per_receptor(residual, image_dir)
        halfway = residual - spread_lanes(alpha_step) * image_dir
        turned = operate(halfway)
        omega_step = per_receptor(turned, halfway) / per_receptor(turned, turned)
        iterate = iterate + spread_lanes(alpha_step) * residual + spread_lanes(omega_step) * halfway
        residual = halfway - spread_lanes(omega_step) * turned
    return iterate, residual
```

```python
import functools
import math

import jax
import jax.numpy as jnp
from jax import lax
from jax.experimental import pallas as pl
from jax.experimental.pallas import tpu as pltpu
from jax.sharding import PartitionSpec as P

NZ = 32
R = 8
CYCLES = 3
DEPTH = 2 * CYCLES + 1
VECS = DEPTH
HALO = 8
SCALE = 16.0
SHIFT = 2.0
LANES = 128

horiz_diff = 4.0
vert_diff = 2.0
decay_rate = 3.5
penalty = 40.0
leaf_gain = 4.0
source_gain = 32.0


def two_sum(a, b):
    s = a + b
    t = s - a
    return s, (a - (s - t)) + (b - t)


def quick_sum(a, b):
    s = a + b
    return s, b - (s - a)


def split(a):
    c = a * 4097.0
    hi = c - (c - a)
    return hi, a - hi


def two_prod(a, b):
    p = a * b
    ah, al = split(a)
    bh, bl = split(b)
    return p, (((ah * bh - p) + ah * bl) + al * bh) + al * bl


def krylov_kernel(
    rows, cols, rec_ref, left_ref, own_ref, right_ref, ex_ref, gram_ref, vec_ref,
    f_ref, coef_ref, raw_ref, wide_ref, hi_ref, lo_ref,
):
    win = rows + 2 * DEPTH
    crows = win - 2
    width = cols + 2 * HALO
    tiles = width // 8
    total_rows = left_ref.shape[0]
    total_cols = cols * lax.axis_size("gy")
    row0 = lax.axis_index("gx") * rows - DEPTH
    col0 = lax.axis_index("gy") * cols - HALO
    lane = lax.broadcasted_iota(jnp.int32, (8, LANES), 1)
    sub = lax.broadcasted_iota(jnp.int32, (8, LANES), 0)

    def inside_row(i):
        at = row0 + i
        ok = jnp.logical_and(at >= 0, at < total_rows)
        return jnp.where(ok, 1.0, 0.0), jnp.clip(at, 0, total_rows - 1)

    def parts(at, lo):
        return (
            left_ref[at, :, lo : lo + LANES],
            own_ref[at, :, lo : lo + LANES],
            right_ref[at, :, lo : lo + LANES],
        )

    spans = ((0, HALO), (HALO, HALO + cols), (HALO + cols, width))

    @pl.loop(0, win)
    def _(i):
        ok, at = inside_row(i)
        for h in range(2):
            for (c0, c1), piece in zip(spans, parts(at, h * LANES)):
                f_ref[0, h, i, 8 + c0 : 8 + c1] = piece * ok

    @pl.loop(0, crows)
    def _(i):
        _, at = inside_row(i + 1)
        base = pl.multiple_of(i * width, 8)
        for (c0, c1), piece in zip(spans, parts(at, 2 * LANES)):
            raw_ref[pl.ds(base + c0, c1 - c0), :] = piece

    raw = raw_ref[...]
    first = raw.astype(jnp.bfloat16)
    rest = raw - first.astype(jnp.float32)
    second = rest.astype(jnp.bfloat16)
    third = (rest - second.astype(jnp.float32)).astype(jnp.bfloat16)
    wide_ref[...] = jnp.dot(
        jnp.concatenate([first, second, third], axis=1),
        ex_ref[...],
        preferred_element_type=jnp.float32,
    )

    @pl.loop(0, crows)
    def _(i):
        ok, _ = inside_row(i + 1)
        base = pl.multiple_of(i * width, 8)
        for t in range(tiles):
            at_col = col0 + 8 * t + sub
            seen = jnp.logical_and(at_col >= 0, at_col < total_cols)
            keep = jnp.where(seen, ok * (1.0 / SCALE), 0.0)
            for h in range(2):
                u, v, w, reaction = [
                    wide_ref[pl.ds(base + 8 * t, 8), pl.ds((2 * c + h) * LANES, LANES)]
                    for c in range(4)
                ]
                side = [
                    horiz_diff + jnp.maximum(u, 0.0),
                    horiz_diff + jnp.maximum(-u, 0.0),
                    horiz_diff + jnp.maximum(v, 0.0),
                    horiz_diff + jnp.maximum(-v, 0.0),
                    vert_diff + jnp.maximum(w, 0.0),
                    vert_diff + jnp.maximum(-w, 0.0),
                ]
                diag = decay_rate + reaction
                for one in side:
                    diag = diag + one
                if h == 1:
                    side[4] = jnp.where(lane < LANES - R, side[4], 0.0)
                else:
                    side[5] = jnp.where(lane >= R, side[5], 0.0)
                for c, one in enumerate([diag] + side):
                    coef_ref[c, h, i, 8 * t : 8 * t + 8] = one * keep

    def apply(step, finish):
        src, dst = step - 1, step
        shown = range(tiles) if step < DEPTH else range(HALO // 8, tiles - HALO // 8)

        @pl.loop(step, win - step)
        def _(i):
            for t in shown:
                c0 = 8 + 8 * t
                mid = [f_ref[src, h, i, c0 : c0 + 8] for h in range(2)]
                up = [pltpu.roll(m, LANES - R, 1) for m in mid]
                down = [pltpu.roll(m, R, 1) for m in mid]
                above = [jnp.where(lane < LANES - R, up[0], up[1]), up[1]]
                below = [down[0], jnp.where(lane >= R, down[1], down[0])]
                for h in range(2):
                    near = [
                        mid[h],
                        f_ref[src, h, i + 1, c0 : c0 + 8],
                        f_ref[src, h, i - 1, c0 : c0 + 8],
                        f_ref[src, h, i, c0 + 1 : c0 + 9],
                        f_ref[src, h, i, c0 - 1 : c0 + 7],
                        above[h],
                        below[h],
                    ]
                    terms = [
                        coef_ref[c, h, i - 1, 8 * t : 8 * t + 8] * near[c] for c in range(7)
                    ]
                    image = (terms[0] - terms[1]) - (terms[2] + terms[3])
                    image = image - ((terms[4] + terms[5]) + terms[6])
                    f_ref[dst, h, i, c0 : c0 + 8] = finish(image, mid[h])

    apply(1, lambda image, mid: -SCALE * image)
    for q in range(R):
        cell = rec_ref[q]
        i = cell // total_cols - row0
        c = cell % total_cols - col0
        seen = (i >= 1) & (i < win - 1) & (c >= 0) & (c < width)
        i = jnp.clip(i, 1, win - 2)
        c = jnp.clip(c, 0, width - 1)
        base = pl.multiple_of(8 + (c // 8) * 8, 8)
        gain = jnp.where(seen, source_gain, 0.0)
        spot = jnp.where((sub == c % 8) & (lane == R + q), gain, 0.0)
        f_ref[1, 0, i, pl.ds(base, 8)] += spot
    for step in range(2, DEPTH + 1):
        apply(step, lambda image, mid: image - SHIFT * mid)

    pieces = [
        (h, i, t) for h in range(2) for i in range(rows) for t in range(cols // 8)
    ]
    count = len(pieces)
    for k in range(VECS):
        for m, (h, i, t) in enumerate(pieces):
            c0 = 8 + HALO + 8 * t
            x = f_ref[k + 1, h, DEPTH + i, c0 : c0 + 8]
            vec_ref[k, h, i, 8 * t : 8 * t + 8] = x
            hi_ref[k, m], lo_ref[k, m] = split(x)

    zero = jnp.zeros((8, LANES), jnp.float32)
    sums = {}
    for group in ([0, 1, 2, 3], [4, 5], [6]):
        pairs = [(i, j) for j in group for i in range(j + 1)]

        def add(m, carry, pairs=pairs):
            need = sorted({i for pair in pairs for i in pair})
            hi = {k: hi_ref[k, m] for k in need}
            lo = {k: lo_ref[k, m] for k in need}
            out = []
            for (i, j), (s, e) in zip(pairs, carry):
                s, miss = two_sum(s, hi[i] * hi[j])
                if i == j:
                    cross = 2.0 * (hi[i] * lo[j])
                else:
                    cross = hi[i] * lo[j] + lo[i] * hi[j]
                out.append((s, e + ((cross + lo[i] * lo[j]) + miss)))
            return tuple(out)

        done = lax.fori_loop(0, count, add, tuple((zero, zero) for _ in pairs))
        for pair, value in zip(pairs, done):
            sums[pair] = value

    def merge(a, b, axis, step):
        where = (sub if axis == 0 else lane) & step
        first = where == 0
        size = 8 if axis == 0 else LANES
        out = []
        for x, y in zip(a, b):
            kept = jnp.where(first, x, y)
            moved = jnp.where(first, y, x)
            if 2 * step == size:
                moved = pltpu.roll(moved, step, axis)
            else:
                moved = jnp.where(
                    first, pltpu.roll(moved, size - step, axis), pltpu.roll(moved, step, axis)
                )
            out.append((kept, moved))
        (s0, s1), (e0, e1) = out
        s, miss = two_sum(s0, s1)
        return s, (e0 + e1) + miss

    def tree(items, axis, steps):
        for step in steps:
            half = len(items) // 2
            items = [merge(items[n], items[n + half], axis, step) for n in range(half)]
        return items[0]

    columns = []
    for j in range(8):
        i_list = [sums.get((min(i, j), max(i, j)), (zero, zero)) for i in range(8)]
        columns.append(tree(i_list, 0, (4, 2, 1)) if j < VECS else (zero, zero))
    s, e = tree(columns, 1, (64, 32, 16))
    low = (lane & R) == 0
    s1 = jnp.where(low, pltpu.roll(s, LANES - R, 1), pltpu.roll(s, R, 1))
    e1 = jnp.where(low, pltpu.roll(e, LANES - R, 1), pltpu.roll(e, R, 1))
    s, miss = two_sum(s, s1)
    e = (e + e1) + miss
    s, e = quick_sum(s, e)
    chunk = jnp.where(low, s, e)
    for n in range(gram_ref.shape[0] // 8):
        gram_ref[8 * n : 8 * n + 8] = chunk


def finish_kernel(gram_ref, guess_ref, vec_ref, x_ref, r_ref):
    lane = lax.broadcasted_iota(jnp.int32, (8, LANES), 1)
    sub = lax.broadcasted_iota(jnp.int32, (8, LANES), 0)
    devices = gram_ref.shape[0] // 8
    ways = math.gcd(devices, 8)
    zero = jnp.zeros((8, LANES), jnp.float32)

    def gather(n, carry):
        out = []
        for w, (s, e) in enumerate(carry):
            at = pl.multiple_of((n * ways + w) * 8, 8)
            s, miss = two_sum(s, gram_ref[pl.ds(at, 8), :])
            out.append((s, e + miss))
        return tuple(out)

    items = list(lax.fori_loop(0, devices // ways, gather, ((zero, zero),) * ways))
    while len(items) > 1:
        half = len(items) // 2
        merged = []
        for n in range(half):
            s, miss = two_sum(items[n][0], items[n + half][0])
            merged.append((s, (items[n][1] + items[n + half][1]) + miss))
        items = merged
    s, e = items[0]
    low = (lane & R) == 0
    g_hi = jnp.where(low, s, pltpu.roll(s, R, 1))
    g_lo = jnp.where(low, pltpu.roll(s, LANES - R, 1) + e, s + pltpu.roll(e, R, 1))
    g_hi, g_lo = quick_sum(g_hi, g_lo)

    def reduced(p, e, axis, steps):
        for step in steps:
            p, miss = two_sum(p, pltpu.roll(p, step, axis))
            e = (e + pltpu.roll(e, step, axis)) + miss
        return quick_sum(p, e)

    def product(a, b):
        p, e = two_prod(a[0], b[0])
        return p, e + (a[0] * b[1] + a[1] * b[0])

    def image_of(p, axis):
        step = 1 if axis == 0 else 2 * R
        s, miss = two_sum(SHIFT * p[0], pltpu.roll(p[0], step, axis))
        return quick_sum(s, (SHIFT * p[1] + pltpu.roll(p[1], step, axis)) + miss)

    def minus(a, factor, b):
        p, e = two_prod(factor, b[0])
        s, miss = two_sum(a[0], -p)
        return quick_sum(s, (a[1] - (e + factor * b[1])) + miss)

    def ratio(p_row, top, bottom):
        y = reduced(*product((g_hi, g_lo), p_row), 1, (16, 32, 64))
        a = reduced(*product(top, y), 0, (4, 2, 1))
        b = reduced(*product(bottom, y), 0, (4, 2, 1))
        return a[0] / b[0]

    row = (jnp.where(lane < 2 * R, 1.0, 0.0), zero)
    col = (jnp.where(sub == 0, 1.0, 0.0), zero)
    gained = zero
    for _ in range(CYCLES):
        row_image, col_image = image_of(row, 1), image_of(col, 0)
        alpha = ratio(row, col, col_image)
        row_half = minus(row, alpha, row_image)
        col_half = minus(col, alpha, col_image)
        row_turned, col_turned = image_of(row_half, 1), image_of(col_half, 0)
        omega = ratio(row_turned, col_half, col_turned)
        gained = gained + ((alpha / SCALE) * col[0] + (omega / SCALE) * col_half[0])
        row = minus(row_half, omega, row_turned)
        col = minus(col_half, omega, col_turned)

    def spread(x, k):
        return jnp.broadcast_to(x[k : k + 1], (8, LANES))

    r_factor = [spread(col[0], k) for k in range(VECS)]
    x_factor = [spread(gained, k) for k in range(VECS - 1)]
    rows, cols = guess_ref.shape[:2]
    for i in range(rows):
        for t in range(cols // 8):
            for h in range(2):
                c, l = slice(8 * t, 8 * t + 8), slice(h * LANES, (h + 1) * LANES)
                v = [vec_ref[k, h, i, c] for k in range(VECS)]
                x, r = x_factor[0] * v[0], r_factor[0] * v[0]
                for k in range(1, VECS):
                    r = r + r_factor[k] * v[k]
                    if k < VECS - 1:
                        x = x + x_factor[k] * v[k]
                x_ref[i, c, l] = guess_ref[i, c, l] + x
                r_ref[i, c, l] = r


def body(adjoint_guess, velocity, leaf_rate, canopy, solid, receptors):
    rows, cols, lanes = adjoint_guess.shape
    ngx, ngy = lax.axis_size("gx"), lax.axis_size("gy")
    devices = ngx * ngy
    width = cols + 2 * HALO
    win = rows + 2 * DEPTH
    reaction = penalty * solid.astype(jnp.float32) + leaf_gain * leaf_rate * canopy.astype(
        jnp.float32
    )
    fields = jnp.concatenate([velocity, reaction[None]], axis=0).reshape(4, rows, cols, NZ)
    fields = jnp.transpose(fields, (1, 2, 0, 3)).reshape(rows, cols, 4 * NZ)
    payload = jnp.concatenate([adjoint_guess, fields], axis=-1)
    own = lax.all_gather(payload, "gx", axis=0, tiled=True)
    up = [(j, j + 1) for j in range(ngy - 1)]
    down = [(j + 1, j) for j in range(ngy - 1)]
    left = lax.ppermute(own[:, cols - HALO :], "gy", up)
    right = lax.ppermute(own[:, :HALO], "gy", down)

    source_lane = jnp.arange(4 * NZ)[:, None]
    wide_lane = jnp.arange(4 * NZ * R)[None, :]
    spread = (source_lane == wide_lane // R).astype(jnp.bfloat16)
    spread = jnp.concatenate([spread] * 3, axis=0)

    vmem = pl.BlockSpec(memory_space=pltpu.VMEM)
    smem = pl.BlockSpec(memory_space=pltpu.SMEM)
    gram, vectors = pl.pallas_call(
        functools.partial(krylov_kernel, rows, cols),
        out_shape=(
            jax.ShapeDtypeStruct((devices * 8, LANES), jnp.float32),
            jax.ShapeDtypeStruct((VECS, 2, rows, cols, LANES), jnp.float32),
        ),
        in_specs=[smem, vmem, vmem, vmem, vmem],
        out_specs=(vmem, vmem),
        scratch_shapes=[
            pltpu.VMEM((DEPTH + 1, 2, win, width + 16, LANES), jnp.float32),
            pltpu.VMEM((7, 2, win - 2, width, LANES), jnp.float32),
            pltpu.VMEM(((win - 2) * width, LANES), jnp.float32),
            pltpu.VMEM(((win - 2) * width, 8 * LANES), jnp.float32),
            pltpu.VMEM((VECS, 2 * rows * cols // 8, 8, LANES), jnp.float32),
            pltpu.VMEM((VECS, 2 * rows * cols // 8, 8, LANES), jnp.float32),
        ],
        compiler_params=pltpu.CompilerParams(vmem_limit_bytes=40 * 1024 * 1024),
        name="krylov",
    )(receptors, left, own, right, spread)
    everyone = lax.all_to_all(gram, ("gx", "gy"), 0, 0, tiled=True)
    out = jax.ShapeDtypeStruct((rows, cols, lanes), jnp.float32)
    return pl.pallas_call(
        finish_kernel,
        out_shape=(out, out),
        in_specs=[vmem, vmem, vmem],
        out_specs=(vmem, vmem),
        compiler_params=pltpu.CompilerParams(vmem_limit_bytes=16 * 1024 * 1024),
        name="finish",
    )(everyone, adjoint_guess, vectors)


def solution(mesh):
    return jax.shard_map(
        body,
        mesh=mesh,
        in_specs=(
            P("gx", "gy", None),
            P(None, "gx", "gy"),
            P("gx", "gy"),
            P("gx", "gy"),
            P("gx", "gy"),
            P(),
        ),
        out_specs=(P("gx", "gy", None), P("gx", "gy", None)),
        check_vma=False,
    )
```

```python
import functools
import math

import jax
import jax.numpy as jnp
from jax import lax
from jax.experimental import pallas as pl
from jax.experimental.pallas import tpu as pltpu
from jax.sharding import PartitionSpec as P

NZ = 32
R = 8
CYCLES = 3
DEPTH = 2 * CYCLES + 1
VECS = DEPTH
HALO = 8
SCALE = 16.0
SHIFT = 2.0
LANES = 128

horiz_diff = 4.0
vert_diff = 2.0
decay_rate = 3.5
penalty = 40.0
leaf_gain = 4.0
source_gain = 32.0


def two_sum(a, b):
    s = a + b
    t = s - a
    return s, (a - (s - t)) + (b - t)


def quick_sum(a, b):
    s = a + b
    return s, b - (s - a)


def split(a):
    c = a * 4097.0
    hi = c - (c - a)
    return hi, a - hi


def two_prod(a, b):
    p = a * b
    ah, al = split(a)
    bh, bl = split(b)
    return p, (((ah * bh - p) + ah * bl) + al * bh) + al * bl


def krylov_kernel(
    rows, cols, rec_ref, left_ref, own_ref, right_ref, ex_ref, gram_ref, vec_ref,
    f_ref, coef_ref, raw_ref, wide_ref, hi_ref, lo_ref,
):
    win = rows + 2 * DEPTH
    crows = win - 2
    width = cols + 2 * HALO
    tiles = width // 8
    total_rows = left_ref.shape[0]
    total_cols = cols * lax.axis_size("gy")
    row0 = lax.axis_index("gx") * rows - DEPTH
    col0 = lax.axis_index("gy") * cols - HALO
    lane = lax.broadcasted_iota(jnp.int32, (8, LANES), 1)
    sub = lax.broadcasted_iota(jnp.int32, (8, LANES), 0)

    def inside_row(i):
        at = row0 + i
        ok = jnp.logical_and(at >= 0, at < total_rows)
        return jnp.where(ok, 1.0, 0.0), jnp.clip(at, 0, total_rows - 1)

    def parts(at, lo):
        return (
            left_ref[at, :, lo : lo + LANES],
            own_ref[at, :, lo : lo + LANES],
            right_ref[at, :, lo : lo + LANES],
        )

    spans = ((0, HALO), (HALO, HALO + cols), (HALO + cols, width))

    @pl.loop(0, win, unroll=True)
    def _(i):
        ok, at = inside_row(i)
        for h in range(2):
            for (c0, c1), piece in zip(spans, parts(at, h * LANES)):
                f_ref[0, h, i, 8 + c0 : 8 + c1] = piece * ok

    @pl.loop(0, crows, unroll=True)
    def _(i):
        _, at = inside_row(i + 1)
        base = pl.multiple_of(i * width, 8)
        for (c0, c1), piece in zip(spans, parts(at, 2 * LANES)):
            raw_ref[pl.ds(base + c0, c1 - c0), :] = piece

    raw = raw_ref[...]
    first = raw.astype(jnp.bfloat16)
    rest = raw - first.astype(jnp.float32)
    second = rest.astype(jnp.bfloat16)
    third = (rest - second.astype(jnp.float32)).astype(jnp.bfloat16)
    wide_ref[...] = jnp.dot(
        jnp.concatenate([first, second, third], axis=1),
        ex_ref[...],
        preferred_element_type=jnp.float32,
    )

    @pl.loop(0, crows, unroll=True)
    def _(i):
        ok, _ = inside_row(i + 1)
        base = pl.multiple_of(i * width, 8)
        for t in range(tiles):
            at_col = col0 + 8 * t + sub
            seen = jnp.logical_and(at_col >= 0, at_col < total_cols)
            keep = jnp.where(seen, ok * (1.0 / SCALE), 0.0)
            for h in range(2):
                u, v, w, reaction = [
                    wide_ref[pl.ds(base + 8 * t, 8), pl.ds((2 * c + h) * LANES, LANES)]
                    for c in range(4)
                ]
                side = [
                    horiz_diff + jnp.maximum(u, 0.0),
                    horiz_diff + jnp.maximum(-u, 0.0),
                    horiz_diff + jnp.maximum(v, 0.0),
                    horiz_diff + jnp.maximum(-v, 0.0),
                    vert_diff + jnp.maximum(w, 0.0),
                    vert_diff + jnp.maximum(-w, 0.0),
                ]
                diag = decay_rate + reaction
                for one in side:
                    diag = diag + one
                if h == 1:
                    side[4] = jnp.where(lane < LANES - R, side[4], 0.0)
                else:
                    side[5] = jnp.where(lane >= R, side[5], 0.0)
                for c, one in enumerate([diag] + side):
                    coef_ref[c, h, i, 8 * t : 8 * t + 8] = one * keep

    def apply(step, finish):
        src, dst = step - 1, step
        shown = range(tiles) if step < DEPTH else range(HALO // 8, tiles - HALO // 8)

        def load(i):
            return [[f_ref[src, h, i, 8 + 8 * t : 16 + 8 * t] for t in range(tiles)] for h in range(2)]

        def one_row(i, carry):
            west, mid = carry
            east = load(i + 1)
            ahead = [[pltpu.roll(m, 7, 0) for m in mid[h]] for h in range(2)]
            behind = [[pltpu.roll(m, 1, 0) for m in mid[h]] for h in range(2)]
            for t in shown:
                up = [pltpu.roll(mid[h][t], LANES - R, 1) for h in range(2)]
                down = [pltpu.roll(mid[h][t], R, 1) for h in range(2)]
                above = [jnp.where(lane < LANES - R, up[0], up[1]), up[1]]
                below = [down[0], jnp.where(lane >= R, down[1], down[0])]
                for h in range(2):
                    north, south = ahead[h][t], behind[h][t]
                    if t + 1 < tiles:
                        north = jnp.where(sub < 7, north, ahead[h][t + 1])
                    if t > 0:
                        south = jnp.where(sub > 0, south, behind[h][t - 1])
                    near = [mid[h][t], east[h][t], west[h][t], north, south, above[h], below[h]]
                    terms = [
                        coef_ref[c, h, i - 1, 8 * t : 8 * t + 8] * near[c] for c in range(7)
                    ]
                    image = (terms[0] - terms[1]) - (terms[2] + terms[3])
                    image = image - ((terms[4] + terms[5]) + terms[6])
                    f_ref[dst, h, i, 8 + 8 * t : 16 + 8 * t] = finish(image, mid[h][t])
            return mid, east

        carry = load(step - 1), load(step)
        for i in range(step, win - step):
            carry = one_row(i, carry)

    apply(1, lambda image, mid: -SCALE * image)
    for q in range(R):
        cell = rec_ref[q]
        i = cell // total_cols - row0
        c = cell % total_cols - col0
        seen = (i >= 1) & (i < win - 1) & (c >= 0) & (c < width)
        i = jnp.clip(i, 1, win - 2)
        c = jnp.clip(c, 0, width - 1)
        base = pl.multiple_of(8 + (c // 8) * 8, 8)
        gain = jnp.where(seen, source_gain, 0.0)
        spot = jnp.where((sub == c % 8) & (lane == R + q), gain, 0.0)
        f_ref[1, 0, i, pl.ds(base, 8)] += spot
    for step in range(2, DEPTH + 1):
        apply(step, lambda image, mid: image - SHIFT * mid)

    pieces = [
        (h, i, t) for h in range(2) for i in range(rows) for t in range(cols // 8)
    ]
    count = len(pieces)
    for k in range(VECS):
        for m, (h, i, t) in enumerate(pieces):
            c0 = 8 + HALO + 8 * t
            x = f_ref[k + 1, h, DEPTH + i, c0 : c0 + 8]
            vec_ref[k, h, i, 8 * t : 8 * t + 8] = x
            hi_ref[k, m], lo_ref[k, m] = split(x)

    zero = jnp.zeros((8, LANES), jnp.float32)
    sums = {}
    for group in ([0, 1, 2, 3], [4, 5], [6]):
        pairs = [(i, j) for j in group for i in range(j + 1)]

        def add(m, carry, pairs=pairs):
            need = sorted({i for pair in pairs for i in pair})
            hi = {k: hi_ref[k, m] for k in need}
            lo = {k: lo_ref[k, m] for k in need}
            out = []
            for (i, j), (s, e) in zip(pairs, carry):
                s, miss = two_sum(s, hi[i] * hi[j])
                if i == j:
                    cross = 2.0 * (hi[i] * lo[j])
                else:
                    cross = hi[i] * lo[j] + lo[i] * hi[j]
                out.append((s, e + ((cross + lo[i] * lo[j]) + miss)))
            return tuple(out)

        done = lax.fori_loop(0, count, add, tuple((zero, zero) for _ in pairs), unroll=True)
        for pair, value in zip(pairs, done):
            sums[pair] = value

    def merge(a, b, axis, step):
        where = (sub if axis == 0 else lane) & step
        first = where == 0
        size = 8 if axis == 0 else LANES
        out = []
        for x, y in zip(a, b):
            kept = jnp.where(first, x, y)
            moved = jnp.where(first, y, x)
            if 2 * step == size:
                moved = pltpu.roll(moved, step, axis)
            else:
                moved = jnp.where(
                    first, pltpu.roll(moved, size - step, axis), pltpu.roll(moved, step, axis)
                )
            out.append((kept, moved))
        (s0, s1), (e0, e1) = out
        s, miss = two_sum(s0, s1)
        return s, (e0 + e1) + miss

    def tree(items, axis, steps):
        for step in steps:
            half = len(items) // 2
            items = [merge(items[n], items[n + half], axis, step) for n in range(half)]
        return items[0]

    columns = []
    for j in range(8):
        i_list = [sums.get((min(i, j), max(i, j)), (zero, zero)) for i in range(8)]
        columns.append(tree(i_list, 0, (4, 2, 1)) if j < VECS else (zero, zero))
    s, e = tree(columns, 1, (64, 32, 16))
    low = (lane & R) == 0
    s1 = jnp.where(low, pltpu.roll(s, LANES - R, 1), pltpu.roll(s, R, 1))
    e1 = jnp.where(low, pltpu.roll(e, LANES - R, 1), pltpu.roll(e, R, 1))
    s, miss = two_sum(s, s1)
    e = (e + e1) + miss
    s, e = quick_sum(s, e)
    chunk = jnp.where(low, s, e)
    for n in range(gram_ref.shape[0] // 8):
        gram_ref[8 * n : 8 * n + 8] = chunk


def finish_kernel(gram_ref, guess_ref, vec_ref, x_ref, r_ref):
    lane = lax.broadcasted_iota(jnp.int32, (8, LANES), 1)
    sub = lax.broadcasted_iota(jnp.int32, (8, LANES), 0)
    devices = gram_ref.shape[0] // 8
    ways = math.gcd(devices, 8)
    zero = jnp.zeros((8, LANES), jnp.float32)

    def gather(n, carry):
        out = []
        for w, (s, e) in enumerate(carry):
            at = pl.multiple_of((n * ways + w) * 8, 8)
            s, miss = two_sum(s, gram_ref[pl.ds(at, 8), :])
            out.append((s, e + miss))
        return tuple(out)

    items = list(lax.fori_loop(0, devices // ways, gather, ((zero, zero),) * ways))
    while len(items) > 1:
        half = len(items) // 2
        merged = []
        for n in range(half):
            s, miss = two_sum(items[n][0], items[n + half][0])
            merged.append((s, (items[n][1] + items[n + half][1]) + miss))
        items = merged
    s, e = items[0]
    low = (lane & R) == 0
    g_hi = jnp.where(low, s, pltpu.roll(s, R, 1))
    g_lo = jnp.where(low, pltpu.roll(s, LANES - R, 1) + e, s + pltpu.roll(e, R, 1))
    g_hi, g_lo = quick_sum(g_hi, g_lo)

    def reduced(p, e, axis, steps):
        for step in steps:
            p, miss = two_sum(p, pltpu.roll(p, step, axis))
            e = (e + pltpu.roll(e, step, axis)) + miss
        return quick_sum(p, e)

    def product(a, b):
        p, e = two_prod(a[0], b[0])
        return p, e + (a[0] * b[1] + a[1] * b[0])

    def image_of(p, axis):
        step = 1 if axis == 0 else 2 * R
        s, miss = two_sum(SHIFT * p[0], pltpu.roll(p[0], step, axis))
        return quick_sum(s, (SHIFT * p[1] + pltpu.roll(p[1], step, axis)) + miss)

    def minus(a, factor, b):
        p, e = two_prod(factor, b[0])
        s, miss = two_sum(a[0], -p)
        return quick_sum(s, (a[1] - (e + factor * b[1])) + miss)

    def ratio(p_row, top, bottom):
        y = reduced(*product((g_hi, g_lo), p_row), 1, (16, 32, 64))
        a = reduced(*product(top, y), 0, (4, 2, 1))
        b = reduced(*product(bottom, y), 0, (4, 2, 1))
        return a[0] / b[0]

    row = (jnp.where(lane < 2 * R, 1.0, 0.0), zero)
    col = (jnp.where(sub == 0, 1.0, 0.0), zero)
    gained = zero
    for _ in range(CYCLES):
        row_image, col_image = image_of(row, 1), image_of(col, 0)
        alpha = ratio(row, col, col_image)
        row_half = minus(row, alpha, row_image)
        col_half = minus(col, alpha, col_image)
        row_turned, col_turned = image_of(row_half, 1), image_of(col_half, 0)
        omega = ratio(row_turned, col_half, col_turned)
        gained = gained + ((alpha / SCALE) * col[0] + (omega / SCALE) * col_half[0])
        row = minus(row_half, omega, row_turned)
        col = minus(col_half, omega, col_turned)

    def spread(x, k):
        return jnp.broadcast_to(x[k : k + 1], (8, LANES))

    r_factor = [spread(col[0], k) for k in range(VECS)]
    x_factor = [spread(gained, k) for k in range(VECS - 1)]
    rows, cols = guess_ref.shape[:2]
    for i in range(rows):
        for t in range(cols // 8):
            for h in range(2):
                c, l = slice(8 * t, 8 * t + 8), slice(h * LANES, (h + 1) * LANES)
                v = [vec_ref[k, h, i, c] for k in range(VECS)]
                x, r = x_factor[0] * v[0], r_factor[0] * v[0]
                for k in range(1, VECS):
                    r = r + r_factor[k] * v[k]
                    if k < VECS - 1:
                        x = x + x_factor[k] * v[k]
                x_ref[i, c, l] = guess_ref[i, c, l] + x
                r_ref[i, c, l] = r


def body(adjoint_guess, velocity, leaf_rate, canopy, solid, receptors):
    rows, cols, lanes = adjoint_guess.shape
    ngx, ngy = lax.axis_size("gx"), lax.axis_size("gy")
    devices = ngx * ngy
    width = cols + 2 * HALO
    win = rows + 2 * DEPTH
    reaction = penalty * solid.astype(jnp.float32) + leaf_gain * leaf_rate * canopy.astype(
        jnp.float32
    )
    fields = jnp.concatenate([velocity, reaction[None]], axis=0).reshape(4, rows, cols, NZ)
    fields = jnp.transpose(fields, (1, 2, 0, 3)).reshape(rows, cols, 4 * NZ)
    payload = jnp.concatenate([adjoint_guess, fields], axis=-1)
    own = lax.all_gather(payload, "gx", axis=0, tiled=True)
    up = [(j, j + 1) for j in range(ngy - 1)]
    down = [(j + 1, j) for j in range(ngy - 1)]
    left = lax.ppermute(own[:, cols - HALO :], "gy", up)
    right = lax.ppermute(own[:, :HALO], "gy", down)

    source_lane = jnp.arange(4 * NZ)[:, None]
    wide_lane = jnp.arange(4 * NZ * R)[None, :]
    spread = (source_lane == wide_lane // R).astype(jnp.bfloat16)
    spread = jnp.concatenate([spread] * 3, axis=0)

    vmem = pl.BlockSpec(memory_space=pltpu.VMEM)
    smem = pl.BlockSpec(memory_space=pltpu.SMEM)
    gram, vectors = pl.pallas_call(
        functools.partial(krylov_kernel, rows, cols),
        out_shape=(
            jax.ShapeDtypeStruct((devices * 8, LANES), jnp.float32),
            jax.ShapeDtypeStruct((VECS, 2, rows, cols, LANES), jnp.float32),
        ),
        in_specs=[smem, vmem, vmem, vmem, vmem],
        out_specs=(vmem, vmem),
        scratch_shapes=[
            pltpu.VMEM((DEPTH + 1, 2, win, width + 16, LANES), jnp.float32),
            pltpu.VMEM((7, 2, win - 2, width, LANES), jnp.float32),
            pltpu.VMEM(((win - 2) * width, LANES), jnp.float32),
            pltpu.VMEM(((win - 2) * width, 8 * LANES), jnp.float32),
            pltpu.VMEM((VECS, 2 * rows * cols // 8, 8, LANES), jnp.float32),
            pltpu.VMEM((VECS, 2 * rows * cols // 8, 8, LANES), jnp.float32),
        ],
        compiler_params=pltpu.CompilerParams(vmem_limit_bytes=40 * 1024 * 1024),
        name="krylov",
    )(receptors, left, own, right, spread)
    everyone = lax.all_to_all(gram, ("gx", "gy"), 0, 0, tiled=True)
    out = jax.ShapeDtypeStruct((rows, cols, lanes), jnp.float32)
    return pl.pallas_call(
        finish_kernel,
        out_shape=(out, out),
        in_specs=[vmem, vmem, vmem],
        out_specs=(vmem, vmem),
        compiler_params=pltpu.CompilerParams(vmem_limit_bytes=16 * 1024 * 1024),
        name="finish",
    )(everyone, adjoint_guess, vectors)


def solution(mesh):
    return jax.shard_map(
        body,
        mesh=mesh,
        in_specs=(
            P("gx", "gy", None),
            P(None, "gx", "gy"),
            P("gx", "gy"),
            P("gx", "gy"),
            P("gx", "gy"),
            P(),
        ),
        out_specs=(P("gx", "gy", None), P("gx", "gy", None)),
        check_vma=False,
    )
```

```python
import functools
import math

import jax
import jax.numpy as jnp
from jax import lax
from jax.experimental import pallas as pl
from jax.experimental.pallas import tpu as pltpu
from jax.sharding import PartitionSpec as P

NZ = 32
R = 8
CYCLES = 3
DEPTH = 2 * CYCLES + 1
VECS = DEPTH
HALO = 8
SCALE = 16.0
SHIFT = 2.0
LANES = 128

horiz_diff = 4.0
vert_diff = 2.0
decay_rate = 3.5
penalty = 40.0
leaf_gain = 4.0
source_gain = 32.0


def two_sum(a, b):
    s = a + b
    t = s - a
    return s, (a - (s - t)) + (b - t)


def quick_sum(a, b):
    s = a + b
    return s, b - (s - a)


def split(a):
    c = a * 4097.0
    hi = c - (c - a)
    return hi, a - hi


def two_prod(a, b):
    p = a * b
    ah, al = split(a)
    bh, bl = split(b)
    return p, (((ah * bh - p) + ah * bl) + al * bh) + al * bl


def pack_kernel(
    guess_ref, velocity_ref, leaf_ref, canopy_ref, solid_ref, out_ref,
    v_ref, l_ref, c_ref, s_ref, sem,
):
    copies = [
        pltpu.make_async_copy(velocity_ref, v_ref, sem.at[0]),
        pltpu.make_async_copy(leaf_ref, l_ref, sem.at[1]),
        pltpu.make_async_copy(canopy_ref, c_ref, sem.at[2]),
        pltpu.make_async_copy(solid_ref, s_ref, sem.at[3]),
    ]
    rows, cols = guess_ref.shape[:2]
    times = out_ref.shape[0] // rows
    for n in range(times):
        place = out_ref.at[pl.ds(n * rows, rows), :, pl.ds(0, NZ * R)]
        copies.append(pltpu.make_async_copy(guess_ref, place, sem.at[4 + n]))
    for copy in copies:
        copy.start()
    for copy in copies[:4]:
        copy.wait()
    lane = lax.broadcasted_iota(jnp.int32, (8, LANES), 1)
    sub = lax.broadcasted_iota(jnp.int32, (8, LANES), 0)
    reaction = penalty * s_ref[...].astype(jnp.float32) + leaf_gain * l_ref[...] * c_ref[
        ...
    ].astype(jnp.float32)
    fields = [v_ref[0], v_ref[1], v_ref[2], reaction]
    for x in range(rows):
        for t in range(cols // 8):
            base = 8 * t * NZ
            spread = []
            for field in fields:
                near = field[x : x + 1, base : base + LANES]
                far = field[x : x + 1, base + LANES : base + 2 * LANES]
                spread.append(
                    jnp.where(
                        sub < 4,
                        jnp.broadcast_to(near, (8, LANES)),
                        jnp.broadcast_to(far, (8, LANES)),
                    )
                )
            whole = None
            for d in range(4):
                mixed = spread[d]
                for s in range(1, 4):
                    mixed = jnp.where(sub % 4 == s, spread[(s + d) % 4], mixed)
                if d == 0:
                    whole = mixed
                else:
                    here = (lane // NZ - sub) % 4 == d
                    whole = jnp.where(here, pltpu.roll(mixed, NZ * d, 1), whole)
            for n in range(times):
                out_ref[n * rows + x, 8 * t : 8 * t + 8, NZ * R :] = whole
    for copy in copies[4:]:
        copy.wait()


def krylov_kernel(
    rows, cols, rec_ref, left_ref, own_ref, right_ref, ex_ref, gram_ref, vec_ref,
    f_ref, coef_ref, raw_ref, wide_ref, hi_ref, lo_ref,
):
    win = rows + 2 * DEPTH
    crows = win - 2
    width = cols + 2 * HALO
    tiles = width // 8
    total_rows = left_ref.shape[0]
    total_cols = cols * lax.axis_size("gy")
    row0 = lax.axis_index("gx") * rows - DEPTH
    col0 = lax.axis_index("gy") * cols - HALO
    lane = lax.broadcasted_iota(jnp.int32, (8, LANES), 1)
    sub = lax.broadcasted_iota(jnp.int32, (8, LANES), 0)

    def inside_row(i):
        at = row0 + i
        ok = jnp.logical_and(at >= 0, at < total_rows)
        return jnp.where(ok, 1.0, 0.0), jnp.clip(at, 0, total_rows - 1)

    def parts(at, lo):
        return (
            left_ref[at, :, lo : lo + LANES],
            own_ref[at, :, lo : lo + LANES],
            right_ref[at, :, lo : lo + LANES],
        )

    spans = ((0, HALO), (HALO, HALO + cols), (HALO + cols, width))

    @pl.loop(0, win, unroll=True)
    def _(i):
        ok, at = inside_row(i)
        for h in range(2):
            for (c0, c1), piece in zip(spans, parts(at, h * LANES)):
                f_ref[0, h, i, 8 + c0 : 8 + c1] = piece * ok

    @pl.loop(0, crows, unroll=True)
    def _(i):
        _, at = inside_row(i + 1)
        base = pl.multiple_of(i * width, 8)
        for (c0, c1), piece in zip(spans, parts(at, 2 * LANES)):
            raw_ref[pl.ds(base + c0, c1 - c0), :] = piece

    raw = raw_ref[...]
    first = raw.astype(jnp.bfloat16)
    rest = raw - first.astype(jnp.float32)
    second = rest.astype(jnp.bfloat16)
    third = (rest - second.astype(jnp.float32)).astype(jnp.bfloat16)
    wide_ref[...] = jnp.dot(
        jnp.concatenate([first, second, third], axis=1),
        ex_ref[...],
        preferred_element_type=jnp.float32,
    )

    @pl.loop(0, crows, unroll=True)
    def _(i):
        ok, _ = inside_row(i + 1)
        base = pl.multiple_of(i * width, 8)
        for t in range(tiles):
            at_col = col0 + 8 * t + sub
            seen = jnp.logical_and(at_col >= 0, at_col < total_cols)
            keep = jnp.where(seen, ok * (1.0 / SCALE), 0.0)
            for h in range(2):
                u, v, w, reaction = [
                    wide_ref[pl.ds(base + 8 * t, 8), pl.ds((2 * c + h) * LANES, LANES)]
                    for c in range(4)
                ]
                side = [
                    horiz_diff + jnp.maximum(u, 0.0),
                    horiz_diff + jnp.maximum(-u, 0.0),
                    horiz_diff + jnp.maximum(v, 0.0),
                    horiz_diff + jnp.maximum(-v, 0.0),
                    vert_diff + jnp.maximum(w, 0.0),
                    vert_diff + jnp.maximum(-w, 0.0),
                ]
                diag = decay_rate + reaction
                for one in side:
                    diag = diag + one
                if h == 1:
                    side[4] = jnp.where(lane < LANES - R, side[4], 0.0)
                else:
                    side[5] = jnp.where(lane >= R, side[5], 0.0)
                for c, one in enumerate([diag] + side):
                    coef_ref[c, h, i, 8 * t : 8 * t + 8] = one * keep

    def apply(step, finish):
        src, dst = step - 1, step
        shown = range(tiles) if step < DEPTH else range(HALO // 8, tiles - HALO // 8)

        def load(i):
            return [[f_ref[src, h, i, 8 + 8 * t : 16 + 8 * t] for t in range(tiles)] for h in range(2)]

        def one_row(i, carry):
            west, mid = carry
            east = load(i + 1)
            ahead = [[pltpu.roll(m, 7, 0) for m in mid[h]] for h in range(2)]
            behind = [[pltpu.roll(m, 1, 0) for m in mid[h]] for h in range(2)]
            for t in shown:
                up = [pltpu.roll(mid[h][t], LANES - R, 1) for h in range(2)]
                down = [pltpu.roll(mid[h][t], R, 1) for h in range(2)]
                above = [jnp.where(lane < LANES - R, up[0], up[1]), up[1]]
                below = [down[0], jnp.where(lane >= R, down[1], down[0])]
                for h in range(2):
                    north, south = ahead[h][t], behind[h][t]
                    if t + 1 < tiles:
                        north = jnp.where(sub < 7, north, ahead[h][t + 1])
                    if t > 0:
                        south = jnp.where(sub > 0, south, behind[h][t - 1])
                    near = [mid[h][t], east[h][t], west[h][t], north, south, above[h], below[h]]
                    terms = [
                        coef_ref[c, h, i - 1, 8 * t : 8 * t + 8] * near[c] for c in range(7)
                    ]
                    image = (terms[0] - terms[1]) - (terms[2] + terms[3])
                    image = image - ((terms[4] + terms[5]) + terms[6])
                    f_ref[dst, h, i, 8 + 8 * t : 16 + 8 * t] = finish(image, mid[h][t])
            return mid, east

        carry = load(step - 1), load(step)
        for i in range(step, win - step):
            carry = one_row(i, carry)

    apply(1, lambda image, mid: -SCALE * image)
    for q in range(R):
        cell = rec_ref[q]
        i = cell // total_cols - row0
        c = cell % total_cols - col0
        seen = (i >= 1) & (i < win - 1) & (c >= 0) & (c < width)
        i = jnp.clip(i, 1, win - 2)
        c = jnp.clip(c, 0, width - 1)
        base = pl.multiple_of(8 + (c // 8) * 8, 8)
        gain = jnp.where(seen, source_gain, 0.0)
        spot = jnp.where((sub == c % 8) & (lane == R + q), gain, 0.0)
        f_ref[1, 0, i, pl.ds(base, 8)] += spot
    for step in range(2, DEPTH + 1):
        apply(step, lambda image, mid: image - SHIFT * mid)

    pieces = [
        (h, i, t) for h in range(2) for i in range(rows) for t in range(cols // 8)
    ]
    count = len(pieces)
    for k in range(VECS):
        for m, (h, i, t) in enumerate(pieces):
            c0 = 8 + HALO + 8 * t
            x = f_ref[k + 1, h, DEPTH + i, c0 : c0 + 8]
            vec_ref[k, h, i, 8 * t : 8 * t + 8] = x
            hi_ref[k, m], lo_ref[k, m] = split(x)

    zero = jnp.zeros((8, LANES), jnp.float32)
    sums = {}
    for group in ([0, 1, 2, 3], [4, 5], [6]):
        pairs = [(i, j) for j in group for i in range(j + 1)]

        def add(m, carry, pairs=pairs):
            need = sorted({i for pair in pairs for i in pair})
            hi = {k: hi_ref[k, m] for k in need}
            lo = {k: lo_ref[k, m] for k in need}
            out = []
            for (i, j), (s, e) in zip(pairs, carry):
                s, miss = two_sum(s, hi[i] * hi[j])
                if i == j:
                    cross = 2.0 * (hi[i] * lo[j])
                else:
                    cross = hi[i] * lo[j] + lo[i] * hi[j]
                out.append((s, e + ((cross + lo[i] * lo[j]) + miss)))
            return tuple(out)

        done = lax.fori_loop(0, count, add, tuple((zero, zero) for _ in pairs), unroll=True)
        for pair, value in zip(pairs, done):
            sums[pair] = value

    def merge(a, b, axis, step):
        where = (sub if axis == 0 else lane) & step
        first = where == 0
        size = 8 if axis == 0 else LANES
        out = []
        for x, y in zip(a, b):
            kept = jnp.where(first, x, y)
            moved = jnp.where(first, y, x)
            if 2 * step == size:
                moved = pltpu.roll(moved, step, axis)
            else:
                moved = jnp.where(
                    first, pltpu.roll(moved, size - step, axis), pltpu.roll(moved, step, axis)
                )
            out.append((kept, moved))
        (s0, s1), (e0, e1) = out
        s, miss = two_sum(s0, s1)
        return s, (e0 + e1) + miss

    def tree(items, axis, steps):
        for step in steps:
            half = len(items) // 2
            items = [merge(items[n], items[n + half], axis, step) for n in range(half)]
        return items[0]

    columns = []
    for j in range(8):
        i_list = [sums.get((min(i, j), max(i, j)), (zero, zero)) for i in range(8)]
        columns.append(tree(i_list, 0, (4, 2, 1)) if j < VECS else (zero, zero))
    s, e = tree(columns, 1, (64, 32, 16))
    low = (lane & R) == 0
    s1 = jnp.where(low, pltpu.roll(s, LANES - R, 1), pltpu.roll(s, R, 1))
    e1 = jnp.where(low, pltpu.roll(e, LANES - R, 1), pltpu.roll(e, R, 1))
    s, miss = two_sum(s, s1)
    e = (e + e1) + miss
    s, e = quick_sum(s, e)
    chunk = jnp.where(low, s, e)
    for n in range(gram_ref.shape[0] // 8):
        gram_ref[8 * n : 8 * n + 8] = chunk


def finish_kernel(gram_ref, guess_ref, vec_ref, x_ref, r_ref):
    lane = lax.broadcasted_iota(jnp.int32, (8, LANES), 1)
    sub = lax.broadcasted_iota(jnp.int32, (8, LANES), 0)
    devices = gram_ref.shape[0] // 8
    ways = math.gcd(devices, 8)
    zero = jnp.zeros((8, LANES), jnp.float32)

    def gather(n, carry):
        out = []
        for w, (s, e) in enumerate(carry):
            at = pl.multiple_of((n * ways + w) * 8, 8)
            s, miss = two_sum(s, gram_ref[pl.ds(at, 8), :])
            out.append((s, e + miss))
        return tuple(out)

    items = list(lax.fori_loop(0, devices // ways, gather, ((zero, zero),) * ways))
    while len(items) > 1:
        half = len(items) // 2
        merged = []
        for n in range(half):
            s, miss = two_sum(items[n][0], items[n + half][0])
            merged.append((s, (items[n][1] + items[n + half][1]) + miss))
        items = merged
    s, e = items[0]
    low = (lane & R) == 0
    g_hi = jnp.where(low, s, pltpu.roll(s, R, 1))
    g_lo = jnp.where(low, pltpu.roll(s, LANES - R, 1) + e, s + pltpu.roll(e, R, 1))
    g_hi, g_lo = quick_sum(g_hi, g_lo)

    def reduced(p, e, axis, steps):
        for step in steps:
            p, miss = two_sum(p, pltpu.roll(p, step, axis))
            e = (e + pltpu.roll(e, step, axis)) + miss
        return quick_sum(p, e)

    def product(a, b):
        p, e = two_prod(a[0], b[0])
        return p, e + (a[0] * b[1] + a[1] * b[0])

    def image_of(p, axis):
        step = 1 if axis == 0 else 2 * R
        s, miss = two_sum(SHIFT * p[0], pltpu.roll(p[0], step, axis))
        return quick_sum(s, (SHIFT * p[1] + pltpu.roll(p[1], step, axis)) + miss)

    def minus(a, factor, b):
        p, e = two_prod(factor, b[0])
        s, miss = two_sum(a[0], -p)
        return quick_sum(s, (a[1] - (e + factor * b[1])) + miss)

    def ratio(p_row, top, bottom):
        y = reduced(*product((g_hi, g_lo), p_row), 1, (16, 32, 64))
        a = reduced(*product(top, y), 0, (4, 2, 1))
        b = reduced(*product(bottom, y), 0, (4, 2, 1))
        return a[0] / b[0]

    row = (jnp.where(lane < 2 * R, 1.0, 0.0), zero)
    col = (jnp.where(sub == 0, 1.0, 0.0), zero)
    gained = zero
    for _ in range(CYCLES):
        row_image, col_image = image_of(row, 1), image_of(col, 0)
        alpha = ratio(row, col, col_image)
        row_half = minus(row, alpha, row_image)
        col_half = minus(col, alpha, col_image)
        row_turned, col_turned = image_of(row_half, 1), image_of(col_half, 0)
        omega = ratio(row_turned, col_half, col_turned)
        gained = gained + ((alpha / SCALE) * col[0] + (omega / SCALE) * col_half[0])
        row = minus(row_half, omega, row_turned)
        col = minus(col_half, omega, col_turned)

    def spread(x, k):
        return jnp.broadcast_to(x[k : k + 1], (8, LANES))

    r_factor = [spread(col[0], k) for k in range(VECS)]
    x_factor = [spread(gained, k) for k in range(VECS - 1)]
    rows, cols = guess_ref.shape[:2]
    for i in range(rows):
        for t in range(cols // 8):
            for h in range(2):
                c, l = slice(8 * t, 8 * t + 8), slice(h * LANES, (h + 1) * LANES)
                v = [vec_ref[k, h, i, c] for k in range(VECS)]
                x, r = x_factor[0] * v[0], r_factor[0] * v[0]
                for k in range(1, VECS):
                    r = r + r_factor[k] * v[k]
                    if k < VECS - 1:
                        x = x + x_factor[k] * v[k]
                x_ref[i, c, l] = guess_ref[i, c, l] + x
                r_ref[i, c, l] = r


def body(adjoint_guess, velocity, leaf_rate, canopy, solid, receptors):
    rows, cols, lanes = adjoint_guess.shape
    ngx, ngy = lax.axis_size("gx"), lax.axis_size("gy")
    devices = ngx * ngy
    width = cols + 2 * HALO
    win = rows + 2 * DEPTH
    vmem = pl.BlockSpec(memory_space=pltpu.VMEM)
    smem = pl.BlockSpec(memory_space=pltpu.SMEM)
    hbm = pl.BlockSpec(memory_space=pl.ANY)
    payload = pl.pallas_call(
        pack_kernel,
        out_shape=jax.ShapeDtypeStruct((ngx * rows, cols, lanes + 4 * NZ), jnp.float32),
        in_specs=[hbm] * 5,
        out_specs=vmem,
        scratch_shapes=[
            pltpu.VMEM(velocity.shape, jnp.float32),
            pltpu.VMEM(leaf_rate.shape, jnp.float32),
            pltpu.VMEM(canopy.shape, jnp.int32),
            pltpu.VMEM(solid.shape, jnp.int32),
            pltpu.SemaphoreType.DMA((4 + ngx,)),
        ],
        name="pack",
    )(adjoint_guess, velocity, leaf_rate, canopy, solid)
    own = lax.all_to_all(payload, "gx", 0, 0, tiled=True)
    up = [(j, j + 1) for j in range(ngy - 1)]
    down = [(j + 1, j) for j in range(ngy - 1)]
    left = lax.ppermute(own[:, cols - HALO :], "gy", up)
    right = lax.ppermute(own[:, :HALO], "gy", down)

    source_lane = jnp.arange(4 * NZ)[:, None]
    wide_lane = jnp.arange(4 * NZ * R)[None, :]
    spread = (source_lane == wide_lane // R).astype(jnp.bfloat16)
    spread = jnp.concatenate([spread] * 3, axis=0)

    gram, vectors = pl.pallas_call(
        functools.partial(krylov_kernel, rows, cols),
        out_shape=(
            jax.ShapeDtypeStruct((devices * 8, LANES), jnp.float32),
            jax.ShapeDtypeStruct((VECS, 2, rows, cols, LANES), jnp.float32),
        ),
        in_specs=[smem, vmem, vmem, vmem, vmem],
        out_specs=(vmem, vmem),
        scratch_shapes=[
            pltpu.VMEM((DEPTH + 1, 2, win, width + 16, LANES), jnp.float32),
            pltpu.VMEM((7, 2, win - 2, width, LANES), jnp.float32),
            pltpu.VMEM(((win - 2) * width, LANES), jnp.float32),
            pltpu.VMEM(((win - 2) * width, 8 * LANES), jnp.float32),
            pltpu.VMEM((VECS, 2 * rows * cols // 8, 8, LANES), jnp.float32),
            pltpu.VMEM((VECS, 2 * rows * cols // 8, 8, LANES), jnp.float32),
        ],
        compiler_params=pltpu.CompilerParams(vmem_limit_bytes=40 * 1024 * 1024),
        name="krylov",
    )(receptors, left, own, right, spread)
    everyone = lax.all_to_all(gram, ("gx", "gy"), 0, 0, tiled=True)
    out = jax.ShapeDtypeStruct((rows, cols, lanes), jnp.float32)
    return pl.pallas_call(
        finish_kernel,
        out_shape=(out, out),
        in_specs=[vmem, vmem, vmem],
        out_specs=(vmem, vmem),
        compiler_params=pltpu.CompilerParams(vmem_limit_bytes=16 * 1024 * 1024),
        name="finish",
    )(everyone, adjoint_guess, vectors)


def solution(mesh):
    return jax.shard_map(
        body,
        mesh=mesh,
        in_specs=(
            P("gx", "gy", None),
            P(None, "gx", "gy"),
            P("gx", "gy"),
            P("gx", "gy"),
            P("gx", "gy"),
            P(),
        ),
        out_specs=(P("gx", "gy", None), P("gx", "gy", None)),
        check_vma=False,
    )
```

```python
import functools
import math

import jax
import jax.numpy as jnp
from jax import lax
from jax.experimental import pallas as pl
from jax.experimental.pallas import tpu as pltpu
from jax.sharding import PartitionSpec as P

NZ = 32
R = 8
CYCLES = 3
DEPTH = 2 * CYCLES + 1
VECS = DEPTH
HALO = 8
SCALE = 16.0
SHIFT = 2.0
LANES = 128

horiz_diff = 4.0
vert_diff = 2.0
decay_rate = 3.5
penalty = 40.0
leaf_gain = 4.0
source_gain = 32.0


def two_sum(a, b):
    s = a + b
    t = s - a
    return s, (a - (s - t)) + (b - t)


def quick_sum(a, b):
    s = a + b
    return s, b - (s - a)


def split(a):
    c = a * 4097.0
    hi = c - (c - a)
    return hi, a - hi


def two_prod(a, b):
    p = a * b
    ah, al = split(a)
    bh, bl = split(b)
    return p, (((ah * bh - p) + ah * bl) + al * bh) + al * bl


def pack_kernel(
    guess_ref, velocity_ref, leaf_ref, canopy_ref, solid_ref, out_ref,
    v_ref, l_ref, c_ref, s_ref, sem,
):
    copies = [
        pltpu.make_async_copy(velocity_ref, v_ref, sem.at[0]),
        pltpu.make_async_copy(leaf_ref, l_ref, sem.at[1]),
        pltpu.make_async_copy(canopy_ref, c_ref, sem.at[2]),
        pltpu.make_async_copy(solid_ref, s_ref, sem.at[3]),
    ]
    rows, cols = guess_ref.shape[:2]
    times = out_ref.shape[0] // rows
    for n in range(times):
        place = out_ref.at[pl.ds(n * rows, rows), :, pl.ds(0, NZ * R)]
        copies.append(pltpu.make_async_copy(guess_ref, place, sem.at[4 + n]))
    for copy in copies:
        copy.start()
    for copy in copies[:4]:
        copy.wait()
    lane = lax.broadcasted_iota(jnp.int32, (8, LANES), 1)
    sub = lax.broadcasted_iota(jnp.int32, (8, LANES), 0)
    reaction = penalty * s_ref[...].astype(jnp.float32) + leaf_gain * l_ref[...] * c_ref[
        ...
    ].astype(jnp.float32)
    fields = [v_ref[0], v_ref[1], v_ref[2], reaction]
    for x in range(rows):
        for t in range(cols // 8):
            base = 8 * t * NZ
            spread = []
            for field in fields:
                near = field[x : x + 1, base : base + LANES]
                far = field[x : x + 1, base + LANES : base + 2 * LANES]
                spread.append(
                    jnp.where(
                        sub < 4,
                        jnp.broadcast_to(near, (8, LANES)),
                        jnp.broadcast_to(far, (8, LANES)),
                    )
                )
            whole = None
            for d in range(4):
                mixed = spread[d]
                for s in range(1, 4):
                    mixed = jnp.where(sub % 4 == s, spread[(s + d) % 4], mixed)
                if d == 0:
                    whole = mixed
                else:
                    here = (lane // NZ - sub) % 4 == d
                    whole = jnp.where(here, pltpu.roll(mixed, NZ * d, 1), whole)
            for n in range(times):
                out_ref[n * rows + x, 8 * t : 8 * t + 8, NZ * R :] = whole
    for copy in copies[4:]:
        copy.wait()


def reach_of(i, rows):
    return max(DEPTH - i, i - (DEPTH + rows - 1), 0)


def tiles_within(reach, cols):
    shown = []
    for t in range((cols + 2 * HALO) // 8):
        away = max(HALO - (8 * t + 7), 8 * t - (HALO + cols) + 1, 0)
        if away <= reach:
            shown.append(t)
    return shown


def stencil_row(west, mid, east, coef_ref, at, shown):
    lane = lax.broadcasted_iota(jnp.int32, (8, LANES), 1)
    sub = lax.broadcasted_iota(jnp.int32, (8, LANES), 0)
    tiles = len(mid[0])
    ahead = [[pltpu.roll(m, 7, 0) for m in mid[h]] for h in range(2)]
    behind = [[pltpu.roll(m, 1, 0) for m in mid[h]] for h in range(2)]
    images = {}
    for t in shown:
        up = [pltpu.roll(mid[h][t], LANES - R, 1) for h in range(2)]
        down = [pltpu.roll(mid[h][t], R, 1) for h in range(2)]
        above = [jnp.where(lane < LANES - R, up[0], up[1]), up[1]]
        below = [down[0], jnp.where(lane >= R, down[1], down[0])]
        for h in range(2):
            north, south = ahead[h][t], behind[h][t]
            if t + 1 < tiles:
                north = jnp.where(sub < 7, north, ahead[h][t + 1])
            if t > 0:
                south = jnp.where(sub > 0, south, behind[h][t - 1])
            near = [mid[h][t], east[h][t], west[h][t], north, south, above[h], below[h]]
            terms = [coef_ref[c, h, at, 8 * t : 8 * t + 8] * near[c] for c in range(7)]
            image = (terms[0] - terms[1]) - (terms[2] + terms[3])
            images[h, t] = image - ((terms[4] + terms[5]) + terms[6])
    return images


def krylov_kernel(
    rows, cols, rec_ref, left_ref, own_ref, right_ref, ex_ref, gram_ref, f_ref, coef_ref,
    raw_ref, wide_ref, hi_ref, lo_ref, cell_ref, cell_sem,
):
    fetch = pltpu.make_async_copy(rec_ref, cell_ref, cell_sem)
    fetch.start()
    win = rows + 2 * DEPTH
    crows = win - 2
    width = cols + 2 * HALO
    tiles = width // 8
    total_rows = left_ref.shape[0]
    total_cols = cols * lax.axis_size("gy")
    row0 = lax.axis_index("gx") * rows - DEPTH
    col0 = lax.axis_index("gy") * cols - HALO
    lane = lax.broadcasted_iota(jnp.int32, (8, LANES), 1)
    sub = lax.broadcasted_iota(jnp.int32, (8, LANES), 0)

    def inside_row(i):
        at = row0 + i
        ok = jnp.logical_and(at >= 0, at < total_rows)
        return jnp.where(ok, 1.0, 0.0), jnp.clip(at, 0, total_rows - 1)

    def parts(at, lo):
        return (
            left_ref[at, :, lo : lo + LANES],
            own_ref[at, :, lo : lo + LANES],
            right_ref[at, :, lo : lo + LANES],
        )

    spans = ((0, HALO), (HALO, HALO + cols), (HALO + cols, width))

    for i in range(win):
        ok, at = inside_row(i)
        for h in range(2):
            for (c0, c1), piece in zip(spans, parts(at, h * LANES)):
                f_ref[0, h, i, c0:c1] = piece * ok

    for i in range(crows):
        _, at = inside_row(i + 1)
        for (c0, c1), piece in zip(spans, parts(at, 2 * LANES)):
            raw_ref[i * width + c0 : i * width + c1, :] = piece

    raw = raw_ref[...]
    first = raw.astype(jnp.bfloat16)
    rest = raw - first.astype(jnp.float32)
    second = rest.astype(jnp.bfloat16)
    third = (rest - second.astype(jnp.float32)).astype(jnp.bfloat16)
    wide_ref[...] = jnp.dot(
        jnp.concatenate([first, second, third], axis=1),
        ex_ref[...],
        preferred_element_type=jnp.float32,
    )

    for i in range(crows):
        ok, _ = inside_row(i + 1)
        for t in tiles_within(DEPTH - 1 - reach_of(i + 1, rows), cols):
            at = i * width + 8 * t
            at_col = col0 + 8 * t + sub
            seen = jnp.logical_and(at_col >= 0, at_col < total_cols)
            keep = jnp.where(seen, ok * (1.0 / SCALE), 0.0)
            for h in range(2):
                u, v, w, reaction = [
                    wide_ref[at : at + 8, (2 * c + h) * LANES : (2 * c + h + 1) * LANES]
                    for c in range(4)
                ]
                side = [
                    horiz_diff + jnp.maximum(u, 0.0),
                    horiz_diff + jnp.maximum(-u, 0.0),
                    horiz_diff + jnp.maximum(v, 0.0),
                    horiz_diff + jnp.maximum(-v, 0.0),
                    vert_diff + jnp.maximum(w, 0.0),
                    vert_diff + jnp.maximum(-w, 0.0),
                ]
                diag = decay_rate + reaction
                for one in side:
                    diag = diag + one
                if h == 1:
                    side[4] = jnp.where(lane < LANES - R, side[4], 0.0)
                else:
                    side[5] = jnp.where(lane >= R, side[5], 0.0)
                for c, one in enumerate([diag] + side):
                    coef_ref[c, h, i, 8 * t : 8 * t + 8] = one * keep

    def load(k, i):
        return [[f_ref[k, h, i, 8 * t : 8 * t + 8] for t in range(tiles)] for h in range(2)]

    def apply(step, finish):
        west, mid = load(step - 1, step - 1), load(step - 1, step)
        for i in range(step, win - step):
            east = load(step - 1, i + 1)
            shown = tiles_within(DEPTH - step - reach_of(i, rows), cols)
            images = stencil_row(west, mid, east, coef_ref, i - 1, shown)
            for (h, t), image in images.items():
                f_ref[step, h, i, 8 * t : 8 * t + 8] = finish(image, mid[h][t])
            west, mid = mid, east

    apply(1, lambda image, mid: -SCALE * image)
    fetch.wait()
    for q in range(R):
        i = cell_ref[0, q] - row0
        c = cell_ref[1, q] - col0
        seen = (i >= 1) & (i < win - 1) & (c >= 0) & (c < width)
        i = jnp.clip(i, 1, win - 2)
        c = jnp.clip(c, 0, width - 1)
        base = pl.multiple_of((c // 8) * 8, 8)
        gain = jnp.where(seen, source_gain, 0.0)
        spot = jnp.where((sub == c % 8) & (lane == R + q), gain, 0.0)
        f_ref[1, 0, i, pl.ds(base, 8)] += spot
    for step in range(2, DEPTH + 1):
        apply(step, lambda image, mid: image - SHIFT * mid)

    pieces = [
        (h, i, t) for h in range(2) for i in range(rows) for t in range(cols // 8)
    ]
    count = len(pieces)
    for k in range(VECS):
        for m, (h, i, t) in enumerate(pieces):
            c0 = HALO + 8 * t
            hi_ref[k, m], lo_ref[k, m] = split(f_ref[k + 1, h, DEPTH + i, c0 : c0 + 8])

    zero = jnp.zeros((8, LANES), jnp.float32)
    sums = {}
    for group in ([0, 1, 2, 3], [4, 5], [6]):
        pairs = [(i, j) for j in group for i in range(j + 1)]

        def add(m, carry, pairs=pairs):
            need = sorted({i for pair in pairs for i in pair})
            hi = {k: hi_ref[k, m] for k in need}
            lo = {k: lo_ref[k, m] for k in need}
            out = []
            for (i, j), (s, e) in zip(pairs, carry):
                s, miss = two_sum(s, hi[i] * hi[j])
                if i == j:
                    cross = 2.0 * (hi[i] * lo[j])
                else:
                    cross = hi[i] * lo[j] + lo[i] * hi[j]
                out.append((s, e + ((cross + lo[i] * lo[j]) + miss)))
            return tuple(out)

        done = lax.fori_loop(0, count, add, tuple((zero, zero) for _ in pairs), unroll=True)
        for pair, value in zip(pairs, done):
            sums[pair] = value

    def merge(a, b, axis, step):
        where = (sub if axis == 0 else lane) & step
        first = where == 0
        size = 8 if axis == 0 else LANES
        out = []
        for x, y in zip(a, b):
            kept = jnp.where(first, x, y)
            moved = jnp.where(first, y, x)
            if 2 * step == size:
                moved = pltpu.roll(moved, step, axis)
            else:
                moved = jnp.where(
                    first, pltpu.roll(moved, size - step, axis), pltpu.roll(moved, step, axis)
                )
            out.append((kept, moved))
        (s0, s1), (e0, e1) = out
        s, miss = two_sum(s0, s1)
        return s, (e0 + e1) + miss

    def tree(items, axis, steps):
        for step in steps:
            half = len(items) // 2
            items = [merge(items[n], items[n + half], axis, step) for n in range(half)]
        return items[0]

    columns = []
    for j in range(8):
        i_list = [sums.get((min(i, j), max(i, j)), (zero, zero)) for i in range(8)]
        columns.append(tree(i_list, 0, (4, 2, 1)) if j < VECS else (zero, zero))
    s, e = tree(columns, 1, (64, 32, 16))
    low = (lane & R) == 0
    s1 = jnp.where(low, pltpu.roll(s, LANES - R, 1), pltpu.roll(s, R, 1))
    e1 = jnp.where(low, pltpu.roll(e, LANES - R, 1), pltpu.roll(e, R, 1))
    s, miss = two_sum(s, s1)
    e = (e + e1) + miss
    s, e = quick_sum(s, e)
    chunk = jnp.where(low, s, e)
    for n in range(gram_ref.shape[0] // 8):
        gram_ref[8 * n : 8 * n + 8] = chunk


def finish_kernel(gram_ref, f_ref, coef_ref, x_ref, r_ref):
    rows, cols = x_ref.shape[:2]
    tiles = (cols + 2 * HALO) // 8
    lane = lax.broadcasted_iota(jnp.int32, (8, LANES), 1)
    sub = lax.broadcasted_iota(jnp.int32, (8, LANES), 0)
    devices = gram_ref.shape[0] // 8
    ways = math.gcd(devices, 8)
    zero = jnp.zeros((8, LANES), jnp.float32)

    def plus(a, b):
        s, miss = two_sum(a[0], b[0])
        return s, (a[1] + b[1]) + miss

    def total(items):
        while len(items) > 1:
            half = len(items) // 2
            pairs = [plus(items[2 * n], items[2 * n + 1]) for n in range(half)]
            items = pairs + items[2 * half :]
        return items[0]

    def gather(n, carry):
        out = []
        for w, (s, e) in enumerate(carry):
            at = pl.multiple_of((n * ways + w) * 8, 8)
            s, miss = two_sum(s, gram_ref[pl.ds(at, 8), :])
            out.append((s, e + miss))
        return tuple(out)

    steps = devices // ways
    s, e = total(
        list(lax.fori_loop(0, steps, gather, ((zero, zero),) * ways, unroll=steps <= 8))
    )
    low = (lane & R) == 0
    g_hi = jnp.where(low, s, pltpu.roll(s, R, 1))
    g_lo = jnp.where(low, pltpu.roll(s, LANES - R, 1) + e, s + pltpu.roll(e, R, 1))
    g_hi, g_lo = quick_sum(g_hi, g_lo)

    def column(x, j):
        x = jnp.where(lane // (2 * R) == j, x, 0.0)
        for step in (64, 32, 16):
            x = x + pltpu.roll(x, step, 1)
        return x

    grams = [(column(g_hi, j), column(g_lo, j)) for j in range(VECS)]
    gram_splits = [split(g[0]) for g in grams]

    def product(a, b, a_split, b_split):
        p = a[0] * b[0]
        (ah, al), (bh, bl) = a_split, b_split
        e = (((ah * bh - p) + ah * bl) + al * bh) + al * bl
        return p, e + (a[0] * b[1] + a[1] * b[0])

    def minus(a, factor, b):
        p, e = two_prod(factor, b[0])
        s, miss = two_sum(a[0], -p)
        return quick_sum(s, (a[1] - (e + factor * b[1])) + miss)


    def list_image(p):
        out = [(SHIFT * p[0][0], SHIFT * p[0][1])]
        for k in range(1, len(p)):
            out.append(quick_sum(*plus((SHIFT * p[k][0], SHIFT * p[k][1]), p[k - 1])))
        return out + [p[-1]]

    def sub_image(p):
        moved = pltpu.roll(p[0], 1, 0), pltpu.roll(p[1], 1, 0)
        return quick_sum(*plus((SHIFT * p[0], SHIFT * p[1]), moved))

    def list_minus(a, factor, b):
        a = a + [(zero, zero)] * (len(b) - len(a))
        return [minus(x, factor, y) for x, y in zip(a, b)]

    def apply_gram(p):
        return quick_sum(
            *total([product(g, x, gs, split(x[0])) for g, gs, x in zip(grams, gram_splits, p)])
        )

    def dot(a, b):
        p, e = product(a, b, split(a[0]), split(b[0]))
        for step in (4, 2, 1):
            p, e = plus((p, e), (pltpu.roll(p, step, 0), pltpu.roll(e, step, 0)))
        return quick_sum(p, e)

    as_list = [(zero + 1.0, zero)]
    as_sub = (jnp.where(sub == 0, 1.0, 0.0), zero)
    gained = []
    for cycle in range(CYCLES):
        list1 = list_image(as_list)
        list2 = list_image(list1)
        sub1 = sub_image(as_sub)
        sub2 = sub_image(sub1)
        y0, y1, y2 = apply_gram(as_list), apply_gram(list1), apply_gram(list2)
        m00, m01, m02 = dot(as_sub, y0), dot(sub1, y0), dot(sub2, y0)
        m11, m12, m22 = dot(sub1, y1), dot(sub2, y1), dot(sub2, y2)
        alpha = m00[0] / m01[0]
        along = minus(m01, alpha, minus(plus(m02, m11), alpha, m12))
        power = minus(m11, alpha, minus((2.0 * m12[0], 2.0 * m12[1]), alpha, m22))
        omega = along[0] / power[0]
        if cycle + 1 < CYCLES:
            half_list = list_minus(as_list, alpha, list1)
            turn_list = list_minus(list1, alpha, list2)
            gained = gained + [zero] * (len(half_list) - len(gained))
            for k, one in enumerate(half_list):
                gained[k] = gained[k] + (omega / SCALE) * one[0]
            for k, one in enumerate(as_list):
                gained[k] = gained[k] + (alpha / SCALE) * one[0]
            as_list = list_minus(half_list, omega, turn_list)
            as_sub = minus(minus(as_sub, alpha, sub1), omega, minus(sub1, alpha, sub2))

    def combine(i, t, h):
        at = slice(8 * t, 8 * t + 8)
        out = as_list[0][0] * f_ref[1, h, i, at]
        for k in range(1, len(as_list)):
            out = out + as_list[k][0] * f_ref[k + 1, h, i, at]
        return out

    def grid(reach, make):
        out = {}
        for i in range(DEPTH - reach, DEPTH + rows + reach):
            shown = tiles_within(reach - reach_of(i, rows), cols)
            row = make(i, shown)
            out[i] = [[row.get((h, t), zero) for t in range(tiles)] for h in range(2)]
        return out

    residual = grid(
        2, lambda i, shown: {(h, t): combine(i, t, h) for h in range(2) for t in shown}
    )

    def image_row(values, i, shown):
        return stencil_row(values[i - 1], values[i], values[i + 1], coef_ref, i - 1, shown)

    def half_row(i, shown):
        images = image_row(residual, i, shown)
        return {(h, t): residual[i][h][t] - alpha * image for (h, t), image in images.items()}

    half = grid(1, half_row)
    for i in range(DEPTH, DEPTH + rows):
        own = range(HALO // 8, (HALO + cols) // 8)
        for (h, t), turned in image_row(half, i, own).items():
            at = slice(8 * t, 8 * t + 8)
            out = (i - DEPTH, slice(8 * t - HALO, 8 * t - HALO + 8), slice(h * LANES, (h + 1) * LANES))
            x = gained[0] * f_ref[1, h, i, at]
            for k in range(1, len(gained)):
                x = x + gained[k] * f_ref[k + 1, h, i, at]
            x = (f_ref[0, h, i, at] + x) + (alpha / SCALE) * residual[i][h][t]
            x_ref[out] = x + (omega / SCALE) * half[i][h][t]
            r_ref[out] = half[i][h][t] - omega * turned


def body(adjoint_guess, velocity, leaf_rate, canopy, solid, receptors):
    rows, cols, lanes = adjoint_guess.shape
    ngx, ngy = lax.axis_size("gx"), lax.axis_size("gy")
    devices = ngx * ngy
    width = cols + 2 * HALO
    win = rows + 2 * DEPTH
    vmem = pl.BlockSpec(memory_space=pltpu.VMEM)
    hbm = pl.BlockSpec(memory_space=pltpu.HBM)
    payload = pl.pallas_call(
        pack_kernel,
        out_shape=jax.ShapeDtypeStruct((ngx * rows, cols, lanes + 4 * NZ), jnp.float32),
        in_specs=[hbm] * 5,
        out_specs=vmem,
        scratch_shapes=[
            pltpu.VMEM(velocity.shape, jnp.float32),
            pltpu.VMEM(leaf_rate.shape, jnp.float32),
            pltpu.VMEM(canopy.shape, jnp.int32),
            pltpu.VMEM(solid.shape, jnp.int32),
            pltpu.SemaphoreType.DMA((4 + ngx,)),
        ],
        name="pack",
    )(adjoint_guess, velocity, leaf_rate, canopy, solid)
    own = lax.all_to_all(payload, "gx", 0, 0, tiled=True)
    up = [(j, j + 1) for j in range(ngy - 1)]
    down = [(j + 1, j) for j in range(ngy - 1)]
    left = lax.ppermute(own[:, cols - HALO :], "gy", up)
    right = lax.ppermute(own[:, :HALO], "gy", down)

    total_cols = cols * ngy
    cells = jnp.stack([receptors // total_cols, receptors % total_cols])
    source_lane = jnp.arange(4 * NZ)[:, None]
    wide_lane = jnp.arange(4 * NZ * R)[None, :]
    spread = (source_lane == wide_lane // R).astype(jnp.bfloat16)
    spread = jnp.concatenate([spread] * 3, axis=0)
    gram, vectors, coefficients = pl.pallas_call(
        functools.partial(krylov_kernel, rows, cols),
        out_shape=(
            jax.ShapeDtypeStruct((devices * 8, LANES), jnp.float32),
            jax.ShapeDtypeStruct((DEPTH + 1, 2, win, width, LANES), jnp.float32),
            jax.ShapeDtypeStruct((7, 2, win - 2, width, LANES), jnp.float32),
        ),
        in_specs=[pl.BlockSpec(memory_space=pl.ANY), vmem, vmem, vmem, vmem],
        out_specs=(vmem, vmem, vmem),
        scratch_shapes=[
            pltpu.VMEM(((win - 2) * width, LANES), jnp.float32),
            pltpu.VMEM(((win - 2) * width, 8 * LANES), jnp.float32),
            pltpu.VMEM((VECS, 2 * rows * cols // 8, 8, LANES), jnp.float32),
            pltpu.VMEM((VECS, 2 * rows * cols // 8, 8, LANES), jnp.float32),
            pltpu.SMEM((2, R), jnp.int32),
            pltpu.SemaphoreType.DMA(()),
        ],
        compiler_params=pltpu.CompilerParams(vmem_limit_bytes=40 * 1024 * 1024),
        name="krylov",
    )(cells, left, own, right, spread)
    everyone = lax.all_to_all(gram, ("gx", "gy"), 0, 0, tiled=True)
    out = jax.ShapeDtypeStruct((rows, cols, lanes), jnp.float32)
    return pl.pallas_call(
        finish_kernel,
        out_shape=(out, out),
        in_specs=[vmem, vmem, vmem],
        out_specs=(vmem, vmem),
        compiler_params=pltpu.CompilerParams(vmem_limit_bytes=16 * 1024 * 1024),
        name="finish",
    )(everyone, vectors, coefficients)


def solution(mesh):
    return jax.shard_map(
        body,
        mesh=mesh,
        in_specs=(
            P("gx", "gy", None),
            P(None, "gx", "gy"),
            P("gx", "gy"),
            P("gx", "gy"),
            P("gx", "gy"),
            P(),
        ),
        out_specs=(P("gx", "gy", None), P("gx", "gy", None)),
        check_vma=False,
    )
```

```python
import functools
import math

import jax
import jax.numpy as jnp
from jax import lax
from jax.experimental import pallas as pl
from jax.experimental.pallas import tpu as pltpu
from jax.sharding import PartitionSpec as P

NZ = 32
R = 8
CYCLES = 3
DEPTH = 2 * CYCLES + 1
VECS = DEPTH
HALO = 8
SCALE = 16.0
SHIFT = 2.0
LANES = 128

horiz_diff = 4.0
vert_diff = 2.0
decay_rate = 3.5
penalty = 40.0
leaf_gain = 4.0
source_gain = 32.0


def two_sum(a, b):
    s = a + b
    t = s - a
    return s, (a - (s - t)) + (b - t)


def quick_sum(a, b):
    s = a + b
    return s, b - (s - a)


def split(a):
    c = a * 4097.0
    hi = c - (c - a)
    return hi, a - hi


def two_prod(a, b):
    p = a * b
    ah, al = split(a)
    bh, bl = split(b)
    return p, (((ah * bh - p) + ah * bl) + al * bh) + al * bl


def pack_kernel(
    guess_ref, velocity_ref, leaf_ref, canopy_ref, solid_ref, out_ref, far_ref,
    v_ref, l_ref, c_ref, s_ref, sem,
):
    copies = [
        pltpu.make_async_copy(velocity_ref, v_ref, sem.at[0]),
        pltpu.make_async_copy(leaf_ref, l_ref, sem.at[1]),
        pltpu.make_async_copy(canopy_ref, c_ref, sem.at[2]),
        pltpu.make_async_copy(solid_ref, s_ref, sem.at[3]),
        pltpu.make_async_copy(guess_ref, out_ref.at[:, :, pl.ds(0, NZ * R)], sem.at[4]),
    ]
    for copy in copies:
        copy.start()
    for copy in copies[:4]:
        copy.wait()
    rows, cols = guess_ref.shape[:2]
    lane = lax.broadcasted_iota(jnp.int32, (8, LANES), 1)
    sub = lax.broadcasted_iota(jnp.int32, (8, LANES), 0)
    reaction = penalty * s_ref[...].astype(jnp.float32) + leaf_gain * l_ref[...] * c_ref[
        ...
    ].astype(jnp.float32)
    fields = [v_ref[0], v_ref[1], v_ref[2], reaction]
    for x in range(rows):
        for t in range(cols // 8):
            base = 8 * t * NZ
            spread = []
            for field in fields:
                near = field[x : x + 1, base : base + LANES]
                far = field[x : x + 1, base + LANES : base + 2 * LANES]
                spread.append(
                    jnp.where(
                        sub < 4,
                        jnp.broadcast_to(near, (8, LANES)),
                        jnp.broadcast_to(far, (8, LANES)),
                    )
                )
            whole = None
            for d in range(4):
                mixed = spread[d]
                for s in range(1, 4):
                    mixed = jnp.where(sub % 4 == s, spread[(s + d) % 4], mixed)
                if d == 0:
                    whole = mixed
                else:
                    here = (lane // NZ - sub) % 4 == d
                    whole = jnp.where(here, pltpu.roll(mixed, NZ * d, 1), whole)
            out_ref[x, 8 * t : 8 * t + 8, NZ * R :] = whole
    copies[4].wait()
    count = far_ref.shape[0]
    first = jnp.where(lax.axis_index("gx") % 4 < 2, rows - count, 0)
    for x in range(count):
        far_ref[x] = out_ref[first + x]


def window_row(i, rows, a, own, even, odd, far, farther):
    at = i - DEPTH
    if 0 <= at < rows:
        return own(at)
    if -rows <= at < 0:
        return jnp.where(a % 2 == 1, even(at + rows), odd(at + rows))
    if rows <= at < 2 * rows:
        return jnp.where(a % 2 == 1, odd(at - rows), even(at - rows))
    if at < 0:
        return jnp.where(a % 4 >= 2, far(at + DEPTH), farther(at + DEPTH))
    return jnp.where(a % 4 >= 2, farther(at - 2 * rows), far(at - 2 * rows))


def edge_start(a, rows, total_rows, count):
    first = jnp.maximum(DEPTH - a * rows, 1)
    return jnp.minimum(first, rows + 2 * DEPTH - 1 - count)


def reach_of(i, rows):
    return max(DEPTH - i, i - (DEPTH + rows - 1), 0)


def tiles_within(reach, cols):
    shown = []
    for t in range((cols + 2 * HALO) // 8):
        away = max(HALO - (8 * t + 7), 8 * t - (HALO + cols) + 1, 0)
        if away <= reach:
            shown.append(t)
    return shown


def stencil_row(west, mid, east, coef_ref, at, shown):
    lane = lax.broadcasted_iota(jnp.int32, (8, LANES), 1)
    sub = lax.broadcasted_iota(jnp.int32, (8, LANES), 0)
    tiles = len(mid[0])
    ahead = [[pltpu.roll(m, 7, 0) for m in mid[h]] for h in range(2)]
    behind = [[pltpu.roll(m, 1, 0) for m in mid[h]] for h in range(2)]
    images = {}
    for t in shown:
        up = [pltpu.roll(mid[h][t], LANES - R, 1) for h in range(2)]
        down = [pltpu.roll(mid[h][t], R, 1) for h in range(2)]
        above = [jnp.where(lane < LANES - R, up[0], up[1]), up[1]]
        below = [down[0], jnp.where(lane >= R, down[1], down[0])]
        for h in range(2):
            north, south = ahead[h][t], behind[h][t]
            if t + 1 < tiles:
                north = jnp.where(sub < 7, north, ahead[h][t + 1])
            if t > 0:
                south = jnp.where(sub > 0, south, behind[h][t - 1])
            near = [mid[h][t], east[h][t], west[h][t], north, south, above[h], below[h]]
            terms = [coef_ref[c, h, at, 8 * t : 8 * t + 8] * near[c] for c in range(7)]
            image = (terms[0] - terms[1]) - (terms[2] + terms[3])
            images[h, t] = image - ((terms[4] + terms[5]) + terms[6])
    return images


def krylov_kernel(
    rows, cols, rec_ref, outer_ref, inner_ref, own_ref, pair_ref, across_ref, far_ref, farther_ref,
    ex_ref, gram_ref, f_ref, coef_ref,
    raw_ref, wide_ref, hi_ref, lo_ref, cell_ref, cell_sem,
):
    fetch = pltpu.make_async_copy(rec_ref, cell_ref, cell_sem)
    fetch.start()
    win = rows + 2 * DEPTH
    crows = win - 2
    width = cols + 2 * HALO
    tiles = width // 8
    total_rows = rows * lax.axis_size("gx")
    edge_rows = outer_ref.shape[0]
    edge_row0 = edge_start(lax.axis_index("gx"), rows, total_rows, edge_rows)
    place = lax.axis_index("gx")
    odd = lax.axis_index("gy") % 2 == 1
    total_cols = cols * lax.axis_size("gy")
    row0 = lax.axis_index("gx") * rows - DEPTH
    col0 = lax.axis_index("gy") * cols - HALO
    lane = lax.broadcasted_iota(jnp.int32, (8, LANES), 1)
    sub = lax.broadcasted_iota(jnp.int32, (8, LANES), 0)

    def inside_row(i):
        at = row0 + i
        ok = jnp.logical_and(at >= 0, at < total_rows)
        return jnp.where(ok, 1.0, 0.0)

    def parts(i, lo):
        at_edge = jnp.clip(i - edge_row0, 0, edge_rows - 1)
        outer = outer_ref[at_edge, :, lo : lo + LANES]
        inner = inner_ref[at_edge, :, lo : lo + LANES]
        blocks = [
            lambda x, ref=ref: ref[x, :, lo : lo + LANES]
            for ref in (own_ref, pair_ref, across_ref, far_ref, farther_ref)
        ]
        return (
            jnp.where(odd, inner, outer),
            window_row(i, rows, place, *blocks),
            jnp.where(odd, outer, inner),
        )

    spans = ((0, HALO), (HALO, HALO + cols), (HALO + cols, width))

    for i in range(win):
        ok = inside_row(i)
        for h in range(2):
            for (c0, c1), piece in zip(spans, parts(i, h * LANES)):
                f_ref[0, h, i, c0:c1] = piece * ok

    for i in range(crows):
        for (c0, c1), piece in zip(spans, parts(i + 1, 2 * LANES)):
            raw_ref[i * width + c0 : i * width + c1, :] = piece

    raw = raw_ref[...]
    first = raw.astype(jnp.bfloat16)
    rest = raw - first.astype(jnp.float32)
    second = rest.astype(jnp.bfloat16)
    third = (rest - second.astype(jnp.float32)).astype(jnp.bfloat16)
    wide_ref[...] = jnp.dot(
        jnp.concatenate([first, second, third], axis=1),
        ex_ref[...],
        preferred_element_type=jnp.float32,
    )

    for i in range(crows):
        ok = inside_row(i + 1)
        for t in tiles_within(DEPTH - 1 - reach_of(i + 1, rows), cols):
            at = i * width + 8 * t
            at_col = col0 + 8 * t + sub
            seen = jnp.logical_and(at_col >= 0, at_col < total_cols)
            keep = jnp.where(seen, ok * (1.0 / SCALE), 0.0)
            for h in range(2):
                u, v, w, reaction = [
                    wide_ref[at : at + 8, (2 * c + h) * LANES : (2 * c + h + 1) * LANES]
                    for c in range(4)
                ]
                side = [
                    horiz_diff + jnp.maximum(u, 0.0),
                    horiz_diff + jnp.maximum(-u, 0.0),
                    horiz_diff + jnp.maximum(v, 0.0),
                    horiz_diff + jnp.maximum(-v, 0.0),
                    vert_diff + jnp.maximum(w, 0.0),
                    vert_diff + jnp.maximum(-w, 0.0),
                ]
                diag = decay_rate + reaction
                for one in side:
                    diag = diag + one
                if h == 1:
                    side[4] = jnp.where(lane < LANES - R, side[4], 0.0)
                else:
                    side[5] = jnp.where(lane >= R, side[5], 0.0)
                for c, one in enumerate([diag] + side):
                    coef_ref[c, h, i, 8 * t : 8 * t + 8] = one * keep

    def load(k, i):
        return [[f_ref[k, h, i, 8 * t : 8 * t + 8] for t in range(tiles)] for h in range(2)]

    def apply(step, finish):
        west, mid = load(step - 1, step - 1), load(step - 1, step)
        for i in range(step, win - step):
            east = load(step - 1, i + 1)
            shown = tiles_within(DEPTH - step - reach_of(i, rows), cols)
            images = stencil_row(west, mid, east, coef_ref, i - 1, shown)
            for (h, t), image in images.items():
                f_ref[step, h, i, 8 * t : 8 * t + 8] = finish(image, mid[h][t])
            west, mid = mid, east

    apply(1, lambda image, mid: -SCALE * image)
    fetch.wait()
    for q in range(R):
        i = cell_ref[0, q] - row0
        c = cell_ref[1, q] - col0
        seen = (i >= 1) & (i < win - 1) & (c >= 0) & (c < width)
        i = jnp.clip(i, 1, win - 2)
        c = jnp.clip(c, 0, width - 1)
        base = pl.multiple_of((c // 8) * 8, 8)
        gain = jnp.where(seen, source_gain, 0.0)
        spot = jnp.where((sub == c % 8) & (lane == R + q), gain, 0.0)
        f_ref[1, 0, i, pl.ds(base, 8)] += spot
    for step in range(2, DEPTH + 1):
        apply(step, lambda image, mid: image - SHIFT * mid)

    pieces = [
        (h, i, t) for h in range(2) for i in range(rows) for t in range(cols // 8)
    ]
    count = len(pieces)
    for k in range(VECS):
        for m, (h, i, t) in enumerate(pieces):
            c0 = HALO + 8 * t
            hi_ref[k, m], lo_ref[k, m] = split(f_ref[k + 1, h, DEPTH + i, c0 : c0 + 8])

    zero = jnp.zeros((8, LANES), jnp.float32)
    sums = {}
    for group in ([0, 1, 2, 3], [4, 5], [6]):
        pairs = [(i, j) for j in group for i in range(j + 1)]

        def add(m, carry, pairs=pairs):
            need = sorted({i for pair in pairs for i in pair})
            hi = {k: hi_ref[k, m] for k in need}
            lo = {k: lo_ref[k, m] for k in need}
            out = []
            for (i, j), (s, e) in zip(pairs, carry):
                s, miss = two_sum(s, hi[i] * hi[j])
                if i == j:
                    cross = 2.0 * (hi[i] * lo[j])
                else:
                    cross = hi[i] * lo[j] + lo[i] * hi[j]
                out.append((s, e + ((cross + lo[i] * lo[j]) + miss)))
            return tuple(out)

        done = lax.fori_loop(0, count, add, tuple((zero, zero) for _ in pairs), unroll=True)
        for pair, value in zip(pairs, done):
            sums[pair] = value

    def merge(a, b, axis, step):
        where = (sub if axis == 0 else lane) & step
        first = where == 0
        size = 8 if axis == 0 else LANES
        out = []
        for x, y in zip(a, b):
            kept = jnp.where(first, x, y)
            moved = jnp.where(first, y, x)
            if 2 * step == size:
                moved = pltpu.roll(moved, step, axis)
            else:
                moved = jnp.where(
                    first, pltpu.roll(moved, size - step, axis), pltpu.roll(moved, step, axis)
                )
            out.append((kept, moved))
        (s0, s1), (e0, e1) = out
        s, miss = two_sum(s0, s1)
        return s, (e0 + e1) + miss

    def tree(items, axis, steps):
        for step in steps:
            half = len(items) // 2
            items = [merge(items[n], items[n + half], axis, step) for n in range(half)]
        return items[0]

    columns = []
    for j in range(8):
        i_list = [sums.get((min(i, j), max(i, j)), (zero, zero)) for i in range(8)]
        columns.append(tree(i_list, 0, (4, 2, 1)) if j < VECS else (zero, zero))
    s, e = tree(columns, 1, (64, 32, 16))
    low = (lane & R) == 0
    s1 = jnp.where(low, pltpu.roll(s, LANES - R, 1), pltpu.roll(s, R, 1))
    e1 = jnp.where(low, pltpu.roll(e, LANES - R, 1), pltpu.roll(e, R, 1))
    s, miss = two_sum(s, s1)
    e = (e + e1) + miss
    s, e = quick_sum(s, e)
    chunk = jnp.where(low, s, e)
    for n in range(gram_ref.shape[0] // 8):
        gram_ref[8 * n : 8 * n + 8] = chunk


def finish_kernel(gram_ref, f_ref, coef_ref, x_ref, r_ref):
    rows, cols = x_ref.shape[:2]
    tiles = (cols + 2 * HALO) // 8
    lane = lax.broadcasted_iota(jnp.int32, (8, LANES), 1)
    sub = lax.broadcasted_iota(jnp.int32, (8, LANES), 0)
    devices = gram_ref.shape[0] // 8
    ways = math.gcd(devices, 8)
    zero = jnp.zeros((8, LANES), jnp.float32)

    def plus(a, b):
        s, miss = two_sum(a[0], b[0])
        return s, (a[1] + b[1]) + miss

    def total(items):
        while len(items) > 1:
            half = len(items) // 2
            pairs = [plus(items[2 * n], items[2 * n + 1]) for n in range(half)]
            items = pairs + items[2 * half :]
        return items[0]

    def gather(n, carry):
        out = []
        for w, (s, e) in enumerate(carry):
            at = pl.multiple_of((n * ways + w) * 8, 8)
            s, miss = two_sum(s, gram_ref[pl.ds(at, 8), :])
            out.append((s, e + miss))
        return tuple(out)

    steps = devices // ways
    s, e = total(
        list(lax.fori_loop(0, steps, gather, ((zero, zero),) * ways, unroll=steps <= 8))
    )
    low = (lane & R) == 0
    g_hi = jnp.where(low, s, pltpu.roll(s, R, 1))
    g_lo = jnp.where(low, pltpu.roll(s, LANES - R, 1) + e, s + pltpu.roll(e, R, 1))
    g_hi, g_lo = quick_sum(g_hi, g_lo)

    def column(x, j):
        x = jnp.where(lane // (2 * R) == j, x, 0.0)
        for step in (64, 32, 16):
            x = x + pltpu.roll(x, step, 1)
        return x

    grams = [(column(g_hi, j), column(g_lo, j)) for j in range(VECS)]
    gram_splits = [split(g[0]) for g in grams]

    def product(a, b, a_split, b_split):
        p = a[0] * b[0]
        (ah, al), (bh, bl) = a_split, b_split
        e = (((ah * bh - p) + ah * bl) + al * bh) + al * bl
        return p, e + (a[0] * b[1] + a[1] * b[0])

    def minus(a, factor, b):
        p, e = two_prod(factor, b[0])
        s, miss = two_sum(a[0], -p)
        return quick_sum(s, (a[1] - (e + factor * b[1])) + miss)


    def list_image(p):
        out = [(SHIFT * p[0][0], SHIFT * p[0][1])]
        for k in range(1, len(p)):
            out.append(quick_sum(*plus((SHIFT * p[k][0], SHIFT * p[k][1]), p[k - 1])))
        return out + [p[-1]]

    def sub_image(p):
        moved = pltpu.roll(p[0], 1, 0), pltpu.roll(p[1], 1, 0)
        return quick_sum(*plus((SHIFT * p[0], SHIFT * p[1]), moved))

    def list_minus(a, factor, b):
        a = a + [(zero, zero)] * (len(b) - len(a))
        return [minus(x, factor, y) for x, y in zip(a, b)]

    def apply_gram(p):
        return quick_sum(
            *total([product(g, x, gs, split(x[0])) for g, gs, x in zip(grams, gram_splits, p)])
        )

    def dot(a, b):
        p, e = product(a, b, split(a[0]), split(b[0]))
        for step in (4, 2, 1):
            p, e = plus((p, e), (pltpu.roll(p, step, 0), pltpu.roll(e, step, 0)))
        return quick_sum(p, e)

    as_list = [(zero + 1.0, zero)]
    as_sub = (jnp.where(sub == 0, 1.0, 0.0), zero)
    gained = []
    for cycle in range(CYCLES):
        list1 = list_image(as_list)
        list2 = list_image(list1)
        sub1 = sub_image(as_sub)
        sub2 = sub_image(sub1)
        y0, y1, y2 = apply_gram(as_list), apply_gram(list1), apply_gram(list2)
        m00, m01, m02 = dot(as_sub, y0), dot(sub1, y0), dot(sub2, y0)
        m11, m12, m22 = dot(sub1, y1), dot(sub2, y1), dot(sub2, y2)
        alpha = m00[0] / m01[0]
        along = minus(m01, alpha, minus(plus(m02, m11), alpha, m12))
        power = minus(m11, alpha, minus((2.0 * m12[0], 2.0 * m12[1]), alpha, m22))
        omega = along[0] / power[0]
        if cycle + 1 < CYCLES:
            half_list = list_minus(as_list, alpha, list1)
            turn_list = list_minus(list1, alpha, list2)
            gained = gained + [zero] * (len(half_list) - len(gained))
            for k, one in enumerate(half_list):
                gained[k] = gained[k] + (omega / SCALE) * one[0]
            for k, one in enumerate(as_list):
                gained[k] = gained[k] + (alpha / SCALE) * one[0]
            as_list = list_minus(half_list, omega, turn_list)
            as_sub = minus(minus(as_sub, alpha, sub1), omega, minus(sub1, alpha, sub2))

    def combine(i, t, h):
        at = slice(8 * t, 8 * t + 8)
        out = as_list[0][0] * f_ref[1, h, i, at]
        for k in range(1, len(as_list)):
            out = out + as_list[k][0] * f_ref[k + 1, h, i, at]
        return out

    def grid(reach, make):
        out = {}
        for i in range(DEPTH - reach, DEPTH + rows + reach):
            shown = tiles_within(reach - reach_of(i, rows), cols)
            row = make(i, shown)
            out[i] = [[row.get((h, t), zero) for t in range(tiles)] for h in range(2)]
        return out

    residual = grid(
        2, lambda i, shown: {(h, t): combine(i, t, h) for h in range(2) for t in shown}
    )

    def image_row(values, i, shown):
        return stencil_row(values[i - 1], values[i], values[i + 1], coef_ref, i - 1, shown)

    def half_row(i, shown):
        images = image_row(residual, i, shown)
        return {(h, t): residual[i][h][t] - alpha * image for (h, t), image in images.items()}

    half = grid(1, half_row)
    for i in range(DEPTH, DEPTH + rows):
        own = range(HALO // 8, (HALO + cols) // 8)
        for (h, t), turned in image_row(half, i, own).items():
            at = slice(8 * t, 8 * t + 8)
            out = (i - DEPTH, slice(8 * t - HALO, 8 * t - HALO + 8), slice(h * LANES, (h + 1) * LANES))
            x = gained[0] * f_ref[1, h, i, at]
            for k in range(1, len(gained)):
                x = x + gained[k] * f_ref[k + 1, h, i, at]
            x = (f_ref[0, h, i, at] + x) + (alpha / SCALE) * residual[i][h][t]
            x_ref[out] = x + (omega / SCALE) * half[i][h][t]
            r_ref[out] = half[i][h][t] - omega * turned


def body(adjoint_guess, velocity, leaf_rate, canopy, solid, receptors):
    rows, cols, lanes = adjoint_guess.shape
    ngx, ngy = lax.axis_size("gx"), lax.axis_size("gy")
    devices = ngx * ngy
    width = cols + 2 * HALO
    win = rows + 2 * DEPTH
    vmem = pl.BlockSpec(memory_space=pltpu.VMEM)
    hbm = pl.BlockSpec(memory_space=pltpu.HBM)
    wide = lanes + 4 * NZ
    own, far_rows = pl.pallas_call(
        pack_kernel,
        out_shape=(
            pltpu.VMEM((rows, cols, wide), jnp.float32),
            pltpu.VMEM((DEPTH - rows, cols, wide), jnp.float32),
        ),
        in_specs=[hbm] * 5,
        out_specs=(vmem, vmem),
        scratch_shapes=[
            pltpu.VMEM(velocity.shape, jnp.float32),
            pltpu.VMEM(leaf_rate.shape, jnp.float32),
            pltpu.VMEM(canopy.shape, jnp.int32),
            pltpu.VMEM(solid.shape, jnp.int32),
            pltpu.SemaphoreType.DMA((5,)),
        ],
        compiler_params=pltpu.CompilerParams(vmem_limit_bytes=56 * 1024 * 1024),
        name="pack",
    )(adjoint_guess, velocity, leaf_rate, canopy, solid)
    def swap(x, axis, pairs):
        return lax.ppermute(x, axis, pairs + [(j, i) for i, j in pairs])

    place = lax.axis_index("gx")
    far = swap(far_rows, "gx", [(j, j + 2) for j in range(ngx - 2) if j % 4 < 2])
    pair = swap(own, "gx", [(j, j + 1) for j in range(0, ngx - 1, 2)])
    across = swap(own, "gx", [(j, j + 1) for j in range(1, ngx - 1, 2)])
    if ngx > 4:
        other = jnp.where(place % 4 < 2, own[: DEPTH - rows], own[2 * rows - DEPTH :])
        farther = swap(other, "gx", [(j, j + 2) for j in range(ngx - 2) if j % 4 >= 2])
    else:
        farther = jnp.zeros_like(far_rows)

    spans = [
        (max(0, a * rows - DEPTH + 1), min(ngx * rows, (a + 1) * rows + DEPTH - 1))
        for a in range(ngx)
    ]
    count = max(hi - lo for lo, hi in spans)
    odd = lax.axis_index("gy") % 2 == 1

    def edges(left):
        blocks = [
            lambda x, block=jnp.where(left, b[:, :HALO], b[:, cols - HALO :]): block[x]
            for b in (own, pair, across, far, farther)
        ]
        whole = [window_row(i, rows, place, *blocks) for i in range(1, rows + 2 * DEPTH - 1)]
        first = edge_start(place, rows, ngx * rows, count) - 1
        return lax.dynamic_slice_in_dim(jnp.stack(whole), first, count, 0)

    outer = swap(edges(~odd), "gy", [(j, j + 1) for j in range(1, ngy - 1, 2)])
    inner = swap(edges(odd), "gy", [(j, j + 1) for j in range(0, ngy - 1, 2)])

    total_cols = cols * ngy
    cells = jnp.stack([receptors // total_cols, receptors % total_cols])
    source_lane = jnp.arange(4 * NZ)[:, None]
    wide_lane = jnp.arange(4 * NZ * R)[None, :]
    spread = (source_lane == wide_lane // R).astype(jnp.bfloat16)
    spread = jnp.concatenate([spread] * 3, axis=0)
    gram, vectors, coefficients = pl.pallas_call(
        functools.partial(krylov_kernel, rows, cols),
        out_shape=(
            jax.ShapeDtypeStruct((devices * 8, LANES), jnp.float32),
            jax.ShapeDtypeStruct((DEPTH + 1, 2, win, width, LANES), jnp.float32),
            jax.ShapeDtypeStruct((7, 2, win - 2, width, LANES), jnp.float32),
        ),
        in_specs=[pl.BlockSpec(memory_space=pl.ANY)] + [vmem] * 8,
        out_specs=(vmem, vmem, vmem),
        scratch_shapes=[
            pltpu.VMEM(((win - 2) * width, LANES), jnp.float32),
            pltpu.VMEM(((win - 2) * width, 8 * LANES), jnp.float32),
            pltpu.VMEM((VECS, 2 * rows * cols // 8, 8, LANES), jnp.float32),
            pltpu.VMEM((VECS, 2 * rows * cols // 8, 8, LANES), jnp.float32),
            pltpu.SMEM((2, R), jnp.int32),
            pltpu.SemaphoreType.DMA(()),
        ],
        compiler_params=pltpu.CompilerParams(vmem_limit_bytes=40 * 1024 * 1024),
        name="krylov",
    )(cells, outer, inner, own, pair, across, far, farther, spread)
    everyone = lax.all_to_all(gram, ("gx", "gy"), 0, 0, tiled=True)
    out = jax.ShapeDtypeStruct((rows, cols, lanes), jnp.float32)
    return pl.pallas_call(
        finish_kernel,
        out_shape=(out, out),
        in_specs=[vmem, vmem, vmem],
        out_specs=(vmem, vmem),
        compiler_params=pltpu.CompilerParams(vmem_limit_bytes=16 * 1024 * 1024),
        name="finish",
    )(everyone, vectors, coefficients)


def solution(mesh):
    return jax.shard_map(
        body,
        mesh=mesh,
        in_specs=(
            P("gx", "gy", None),
            P(None, "gx", "gy"),
            P("gx", "gy"),
            P("gx", "gy"),
            P("gx", "gy"),
            P(),
        ),
        out_specs=(P("gx", "gy", None), P("gx", "gy", None)),
        check_vma=False,
    )
```

```python
import functools
import math

import jax
import jax.numpy as jnp
from jax import lax
from jax.experimental import pallas as pl
from jax.experimental.pallas import tpu as pltpu
from jax.sharding import PartitionSpec as P

NZ = 32
R = 8
CYCLES = 3
DEPTH = 2 * CYCLES + 1
VECS = DEPTH
HALO = 8
SCALE = 16.0
SHIFT = 2.0
LANES = 128

horiz_diff = 4.0
vert_diff = 2.0
decay_rate = 3.5
penalty = 40.0
leaf_gain = 4.0
source_gain = 32.0


def two_sum(a, b):
    s = a + b
    t = s - a
    return s, (a - (s - t)) + (b - t)


def quick_sum(a, b):
    s = a + b
    return s, b - (s - a)


def split(a):
    c = a * 4097.0
    hi = c - (c - a)
    return hi, a - hi


def two_prod(a, b):
    p = a * b
    ah, al = split(a)
    bh, bl = split(b)
    return p, (((ah * bh - p) + ah * bl) + al * bh) + al * bl


def pack_kernel(
    guess_ref, velocity_ref, leaf_ref, canopy_ref, solid_ref, out_ref, far_ref,
    v_ref, l_ref, c_ref, s_ref, sem,
):
    copies = [
        pltpu.make_async_copy(velocity_ref, v_ref, sem.at[0]),
        pltpu.make_async_copy(leaf_ref, l_ref, sem.at[1]),
        pltpu.make_async_copy(canopy_ref, c_ref, sem.at[2]),
        pltpu.make_async_copy(solid_ref, s_ref, sem.at[3]),
        pltpu.make_async_copy(guess_ref, out_ref.at[:, :, pl.ds(0, NZ * R)], sem.at[4]),
    ]
    for copy in copies:
        copy.start()
    for copy in copies[:4]:
        copy.wait()
    rows, cols = guess_ref.shape[:2]
    lane = lax.broadcasted_iota(jnp.int32, (8, LANES), 1)
    sub = lax.broadcasted_iota(jnp.int32, (8, LANES), 0)
    reaction = penalty * s_ref[...].astype(jnp.float32) + leaf_gain * l_ref[...] * c_ref[
        ...
    ].astype(jnp.float32)
    fields = [v_ref[0], v_ref[1], v_ref[2], reaction]
    for x in range(rows):
        for t in range(cols // 8):
            base = 8 * t * NZ
            spread = []
            for field in fields:
                near = field[x : x + 1, base : base + LANES]
                far = field[x : x + 1, base + LANES : base + 2 * LANES]
                spread.append(
                    jnp.where(
                        sub < 4,
                        jnp.broadcast_to(near, (8, LANES)),
                        jnp.broadcast_to(far, (8, LANES)),
                    )
                )
            whole = None
            for d in range(4):
                mixed = spread[d]
                for s in range(1, 4):
                    mixed = jnp.where(sub % 4 == s, spread[(s + d) % 4], mixed)
                if d == 0:
                    whole = mixed
                else:
                    here = (lane // NZ - sub) % 4 == d
                    whole = jnp.where(here, pltpu.roll(mixed, NZ * d, 1), whole)
            out_ref[x, 8 * t : 8 * t + 8, NZ * R :] = whole
    copies[4].wait()
    count = far_ref.shape[0]
    first = jnp.where(lax.axis_index("gx") % 4 < 2, rows - count, 0)
    for x in range(count):
        far_ref[x] = out_ref[first + x]


def window_row(i, rows, a, own, even, odd, far, farther):
    at = i - DEPTH
    if 0 <= at < rows:
        return own(at)
    if -rows <= at < 0:
        return jnp.where(a % 2 == 1, even(at + rows), odd(at + rows))
    if rows <= at < 2 * rows:
        return jnp.where(a % 2 == 1, odd(at - rows), even(at - rows))
    if at < 0:
        return jnp.where(a % 4 >= 2, far(at + DEPTH), farther(at + DEPTH))
    return jnp.where(a % 4 >= 2, farther(at - 2 * rows), far(at - 2 * rows))


def edges_kernel(
    own_ref, pair_ref, across_ref, far_ref, farther_ref, outer_ref, inner_ref
):
    rows, cols, wide = own_ref.shape
    place = lax.axis_index("gx")
    odd = lax.axis_index("gy") % 2 == 1
    sub = lax.broadcasted_iota(jnp.int32, (8, wide), 0)
    refs = (own_ref, pair_ref, across_ref, far_ref, farther_ref)

    def edge(right):
        c0 = cols - HALO if right else 0
        blocks = [lambda x, ref=ref: ref[x, c0 : c0 + HALO, :] for ref in refs]
        tiles = [window_row(DEPTH + x, rows, place, *blocks) for x in range(rows)]
        for start, way in ((DEPTH, -1), (DEPTH + rows - 1, 1)):
            for d in range(1, DEPTH // 2 + 1):
                close = window_row(start + way * d, rows, place, *blocks)
                distant = window_row(start + way * (DEPTH - d), rows, place, *blocks)
                distant = pltpu.roll(distant, d if right else HALO - d, 0)
                if right:
                    kept = sub >= HALO - DEPTH + d
                else:
                    kept = sub < DEPTH - d
                tiles.append(jnp.where(kept, close, distant))
        return tiles

    for n, (left, right) in enumerate(zip(edge(False), edge(True))):
        outer_ref[n] = jnp.where(odd, right, left)
        inner_ref[n] = jnp.where(odd, left, right)


def reach_of(i, rows):
    return max(DEPTH - i, i - (DEPTH + rows - 1), 0)


def tiles_within(reach, cols):
    shown = []
    for t in range((cols + 2 * HALO) // 8):
        away = max(HALO - (8 * t + 7), 8 * t - (HALO + cols) + 1, 0)
        if away <= reach:
            shown.append(t)
    return shown


def stencil_row(west, mid, east, coef, at, shown):
    lane = lax.broadcasted_iota(jnp.int32, (8, LANES), 1)
    sub = lax.broadcasted_iota(jnp.int32, (8, LANES), 0)
    tiles = len(mid[0])
    ahead = [[pltpu.roll(m, 7, 0) for m in mid[h]] for h in range(2)]
    behind = [[pltpu.roll(m, 1, 0) for m in mid[h]] for h in range(2)]
    images = {}
    for t in shown:
        up = [pltpu.roll(mid[h][t], LANES - R, 1) for h in range(2)]
        down = [pltpu.roll(mid[h][t], R, 1) for h in range(2)]
        above = [jnp.where(lane < LANES - R, up[0], up[1]), up[1]]
        below = [down[0], jnp.where(lane >= R, down[1], down[0])]
        for h in range(2):
            north, south = ahead[h][t], behind[h][t]
            if t + 1 < tiles:
                north = jnp.where(sub < 7, north, ahead[h][t + 1])
            if t > 0:
                south = jnp.where(sub > 0, south, behind[h][t - 1])
            near = [mid[h][t], east[h][t], west[h][t], north, south, above[h], below[h]]
            terms = [coef(c, h, at, t) * near[c] for c in range(7)]
            image = (terms[0] - terms[1]) - (terms[2] + terms[3])
            images[h, t] = image - ((terms[4] + terms[5]) + terms[6])
    return images


def own_tile(t, cols):
    return t - HALO // 8 if HALO <= 8 * t < HALO + cols else None


def coefficients(own_ref, halo_ref, cols):
    def read(c, h, at, t):
        n = own_tile(t, cols)
        if n is not None:
            return own_ref[c, h, at, 8 * n : 8 * n + 8]
        side = 0 if 8 * t < HALO else 8
        return halo_ref[c, h, at, side : side + 8]

    return read


def inside_row(i, rows):
    at = lax.axis_index("gx") * rows - DEPTH + i
    ok = jnp.logical_and(at >= 0, at < rows * lax.axis_size("gx"))
    return jnp.where(ok, 1.0, 0.0)


def widen(raw, spread):
    first = raw.astype(jnp.bfloat16)
    rest = raw - first.astype(jnp.float32)
    second = rest.astype(jnp.bfloat16)
    third = (rest - second.astype(jnp.float32)).astype(jnp.bfloat16)
    pieces = jnp.concatenate([first, second, third], axis=1)
    return jnp.dot(pieces, spread, preferred_element_type=jnp.float32)


def tile_coefficients(wide_ref, at, h, keep):
    lane = lax.broadcasted_iota(jnp.int32, (8, LANES), 1)
    u, v, w, reaction = [
        wide_ref[at : at + 8, (2 * c + h) * LANES : (2 * c + h + 1) * LANES] for c in range(4)
    ]
    side = [
        horiz_diff + jnp.maximum(u, 0.0),
        horiz_diff + jnp.maximum(-u, 0.0),
        horiz_diff + jnp.maximum(v, 0.0),
        horiz_diff + jnp.maximum(-v, 0.0),
        vert_diff + jnp.maximum(w, 0.0),
        vert_diff + jnp.maximum(-w, 0.0),
    ]
    diag = decay_rate + reaction
    for one in side:
        diag = diag + one
    if h == 1:
        side[4] = jnp.where(lane < LANES - R, side[4], 0.0)
    else:
        side[5] = jnp.where(lane >= R, side[5], 0.0)
    return [one * keep for one in [diag] + side]


def central_kernel(
    own_ref, pair_ref, across_ref, far_ref, farther_ref, ex_ref, guess_ref, coef_ref,
    raw_ref, wide_ref,
):
    rows, cols, _ = own_ref.shape
    win = rows + 2 * DEPTH
    place = lax.axis_index("gx")
    refs = (own_ref, pair_ref, across_ref, far_ref, farther_ref)

    def middle(i, lo):
        blocks = [lambda x, ref=ref: ref[x, :, lo : lo + LANES] for ref in refs]
        return window_row(i, rows, place, *blocks)

    for i in range(win):
        for h in range(2):
            guess_ref[h, i] = middle(i, h * LANES) * inside_row(i, rows)
    for i in range(win - 2):
        raw_ref[i * cols : (i + 1) * cols, :] = middle(i + 1, 2 * LANES)
    wide_ref[...] = widen(raw_ref[...], ex_ref[...])
    for i in range(win - 2):
        keep = inside_row(i + 1, rows) * (1.0 / SCALE)
        for t in range(cols // 8):
            for h in range(2):
                values = tile_coefficients(wide_ref, i * cols + 8 * t, h, keep)
                for c, one in enumerate(values):
                    coef_ref[c, h, i, 8 * t : 8 * t + 8] = one


def krylov_kernel(
    rows, cols, rec_ref, outer_ref, inner_ref, guess_ref, mine_ref, ex_ref, gram_ref, f_ref,
    halo_ref, raw_ref, wide_ref, hi_ref, lo_ref, cell_ref, cell_sem,
):
    fetch = pltpu.make_async_copy(rec_ref, cell_ref, cell_sem)
    fetch.start()
    win = rows + 2 * DEPTH
    width = cols + 2 * HALO
    tiles = width // 8
    odd = lax.axis_index("gy") % 2 == 1
    total_cols = cols * lax.axis_size("gy")
    row0 = lax.axis_index("gx") * rows - DEPTH
    col0 = lax.axis_index("gy") * cols - HALO
    lane = lax.broadcasted_iota(jnp.int32, (8, LANES), 1)
    sub = lax.broadcasted_iota(jnp.int32, (8, LANES), 0)
    sides = ((0, True), (HALO + cols, False))

    def edge(i, lo, right):
        away = reach_of(i, rows)
        if away == 0:
            n, turn = i - DEPTH, 0
        else:
            d = min(away, DEPTH - away)
            n = rows + (0 if i < DEPTH else DEPTH // 2) + d - 1
            turn = 0 if d == away else (HALO - d if right else d)
        outer, inner = [ref[n, :, lo : lo + LANES] for ref in (outer_ref, inner_ref)]
        tile = jnp.where(odd, inner, outer) if right else jnp.where(odd, outer, inner)
        return pltpu.roll(tile, turn, 0) if turn else tile

    for i in range(1, win - 1):
        for h in range(2):
            for c0, right in sides:
                f_ref[0, h, i, c0 : c0 + HALO] = edge(i, h * LANES, right) * inside_row(i, rows)

    needed = [i for i in range(1, win - 1) if reach_of(i, rows) < DEPTH - 1]
    for n, i in enumerate(needed):
        for side, (c0, right) in enumerate(sides):
            at = (2 * n + side) * HALO
            raw_ref[at : at + HALO, :] = edge(i, 2 * LANES, right)
    wide_ref[...] = widen(raw_ref[...], ex_ref[...])
    for n, i in enumerate(needed):
        for side, (c0, right) in enumerate(sides):
            at_col = col0 + c0 + sub
            seen = jnp.logical_and(at_col >= 0, at_col < total_cols)
            keep = jnp.where(seen, inside_row(i, rows) * (1.0 / SCALE), 0.0)
            for h in range(2):
                values = tile_coefficients(wide_ref, (2 * n + side) * HALO, h, keep)
                for c, one in enumerate(values):
                    halo_ref[c, h, i - 1, side * HALO : (side + 1) * HALO] = one

    coef = coefficients(mine_ref, halo_ref, cols)

    def read(k, h, i, t):
        n = own_tile(t, cols)
        if k == 0 and n is not None:
            return guess_ref[h, i, 8 * n : 8 * n + 8]
        return f_ref[k, h, i, 8 * t : 8 * t + 8]

    def load(k, i):
        return [[read(k, h, i, t) for t in range(tiles)] for h in range(2)]

    def apply(step, finish):
        west, mid = load(step - 1, step - 1), load(step - 1, step)
        for i in range(step, win - step):
            east = load(step - 1, i + 1)
            shown = tiles_within(DEPTH - step - reach_of(i, rows), cols)
            images = stencil_row(west, mid, east, coef, i - 1, shown)
            for (h, t), image in images.items():
                f_ref[step, h, i, 8 * t : 8 * t + 8] = finish(image, mid[h][t])
            west, mid = mid, east

    apply(1, lambda image, mid: -SCALE * image)
    fetch.wait()
    for q in range(R):
        i = cell_ref[0, q] - row0
        c = cell_ref[1, q] - col0
        seen = (i >= 1) & (i < win - 1) & (c >= 0) & (c < width)
        i = jnp.clip(i, 1, win - 2)
        c = jnp.clip(c, 0, width - 1)
        base = pl.multiple_of((c // 8) * 8, 8)
        gain = jnp.where(seen, source_gain, 0.0)
        spot = jnp.where((sub == c % 8) & (lane == R + q), gain, 0.0)
        f_ref[1, 0, i, pl.ds(base, 8)] += spot
    for step in range(2, DEPTH + 1):
        apply(step, lambda image, mid: image - SHIFT * mid)

    pieces = [
        (h, i, t) for h in range(2) for i in range(rows) for t in range(cols // 8)
    ]
    count = len(pieces)
    for k in range(VECS):
        for m, (h, i, t) in enumerate(pieces):
            c0 = HALO + 8 * t
            hi_ref[k, m], lo_ref[k, m] = split(f_ref[k + 1, h, DEPTH + i, c0 : c0 + 8])

    zero = jnp.zeros((8, LANES), jnp.float32)
    sums = {}
    for group in ([0, 1, 2, 3], [4, 5], [6]):
        pairs = [(i, j) for j in group for i in range(j + 1)]

        def add(m, carry, pairs=pairs):
            need = sorted({i for pair in pairs for i in pair})
            hi = {k: hi_ref[k, m] for k in need}
            lo = {k: lo_ref[k, m] for k in need}
            out = []
            for (i, j), (s, e) in zip(pairs, carry):
                s, miss = two_sum(s, hi[i] * hi[j])
                if i == j:
                    cross = 2.0 * (hi[i] * lo[j])
                else:
                    cross = hi[i] * lo[j] + lo[i] * hi[j]
                out.append((s, e + ((cross + lo[i] * lo[j]) + miss)))
            return tuple(out)

        done = lax.fori_loop(0, count, add, tuple((zero, zero) for _ in pairs), unroll=True)
        for pair, value in zip(pairs, done):
            sums[pair] = value

    def merge(a, b, axis, step):
        where = (sub if axis == 0 else lane) & step
        first = where == 0
        size = 8 if axis == 0 else LANES
        out = []
        for x, y in zip(a, b):
            kept = jnp.where(first, x, y)
            moved = jnp.where(first, y, x)
            if 2 * step == size:
                moved = pltpu.roll(moved, step, axis)
            else:
                moved = jnp.where(
                    first, pltpu.roll(moved, size - step, axis), pltpu.roll(moved, step, axis)
                )
            out.append((kept, moved))
        (s0, s1), (e0, e1) = out
        s, miss = two_sum(s0, s1)
        return s, (e0 + e1) + miss

    def tree(items, axis, steps):
        for step in steps:
            half = len(items) // 2
            items = [merge(items[n], items[n + half], axis, step) for n in range(half)]
        return items[0]

    columns = []
    for j in range(8):
        i_list = [sums.get((min(i, j), max(i, j)), (zero, zero)) for i in range(8)]
        columns.append(tree(i_list, 0, (4, 2, 1)) if j < VECS else (zero, zero))
    s, e = tree(columns, 1, (64, 32, 16))
    low = (lane & R) == 0
    s1 = jnp.where(low, pltpu.roll(s, LANES - R, 1), pltpu.roll(s, R, 1))
    e1 = jnp.where(low, pltpu.roll(e, LANES - R, 1), pltpu.roll(e, R, 1))
    s, miss = two_sum(s, s1)
    e = (e + e1) + miss
    s, e = quick_sum(s, e)
    chunk = jnp.where(low, s, e)
    for n in range(gram_ref.shape[0] // 8):
        gram_ref[8 * n : 8 * n + 8] = chunk


def finish_kernel(gram_ref, f_ref, guess_ref, mine_ref, halo_ref, x_ref, r_ref):
    rows, cols = x_ref.shape[:2]
    coef = coefficients(mine_ref, halo_ref, cols)
    tiles = (cols + 2 * HALO) // 8
    lane = lax.broadcasted_iota(jnp.int32, (8, LANES), 1)
    sub = lax.broadcasted_iota(jnp.int32, (8, LANES), 0)
    devices = gram_ref.shape[0] // 8
    ways = math.gcd(devices, 8)
    zero = jnp.zeros((8, LANES), jnp.float32)

    def plus(a, b):
        s, miss = two_sum(a[0], b[0])
        return s, (a[1] + b[1]) + miss

    def total(items):
        while len(items) > 1:
            half = len(items) // 2
            pairs = [plus(items[2 * n], items[2 * n + 1]) for n in range(half)]
            items = pairs + items[2 * half :]
        return items[0]

    def gather(n, carry):
        out = []
        for w, (s, e) in enumerate(carry):
            at = pl.multiple_of((n * ways + w) * 8, 8)
            s, miss = two_sum(s, gram_ref[pl.ds(at, 8), :])
            out.append((s, e + miss))
        return tuple(out)

    steps = devices // ways
    s, e = total(
        list(lax.fori_loop(0, steps, gather, ((zero, zero),) * ways, unroll=steps <= 8))
    )
    low = (lane & R) == 0
    g_hi = jnp.where(low, s, pltpu.roll(s, R, 1))
    g_lo = jnp.where(low, pltpu.roll(s, LANES - R, 1) + e, s + pltpu.roll(e, R, 1))
    g_hi, g_lo = quick_sum(g_hi, g_lo)

    def column(x, j):
        x = jnp.where(lane // (2 * R) == j, x, 0.0)
        for step in (64, 32, 16):
            x = x + pltpu.roll(x, step, 1)
        return x

    grams = [(column(g_hi, j), column(g_lo, j)) for j in range(VECS)]
    gram_splits = [split(g[0]) for g in grams]

    def product(a, b, a_split, b_split):
        p = a[0] * b[0]
        (ah, al), (bh, bl) = a_split, b_split
        e = (((ah * bh - p) + ah * bl) + al * bh) + al * bl
        return p, e + (a[0] * b[1] + a[1] * b[0])

    def minus(a, factor, b):
        p, e = two_prod(factor, b[0])
        s, miss = two_sum(a[0], -p)
        return quick_sum(s, (a[1] - (e + factor * b[1])) + miss)


    def list_image(p):
        out = [(SHIFT * p[0][0], SHIFT * p[0][1])]
        for k in range(1, len(p)):
            out.append(quick_sum(*plus((SHIFT * p[k][0], SHIFT * p[k][1]), p[k - 1])))
        return out + [p[-1]]

    def sub_image(p):
        moved = pltpu.roll(p[0], 1, 0), pltpu.roll(p[1], 1, 0)
        return quick_sum(*plus((SHIFT * p[0], SHIFT * p[1]), moved))

    def list_minus(a, factor, b):
        a = a + [(zero, zero)] * (len(b) - len(a))
        return [minus(x, factor, y) for x, y in zip(a, b)]

    def apply_gram(p):
        return quick_sum(
            *total([product(g, x, gs, split(x[0])) for g, gs, x in zip(grams, gram_splits, p)])
        )

    def dot(a, b):
        p, e = product(a, b, split(a[0]), split(b[0]))
        for step in (4, 2, 1):
            p, e = plus((p, e), (pltpu.roll(p, step, 0), pltpu.roll(e, step, 0)))
        return quick_sum(p, e)

    as_list = [(zero + 1.0, zero)]
    as_sub = (jnp.where(sub == 0, 1.0, 0.0), zero)
    gained = []
    for cycle in range(CYCLES):
        list1 = list_image(as_list)
        list2 = list_image(list1)
        sub1 = sub_image(as_sub)
        sub2 = sub_image(sub1)
        y0, y1, y2 = apply_gram(as_list), apply_gram(list1), apply_gram(list2)
        m00, m01, m02 = dot(as_sub, y0), dot(sub1, y0), dot(sub2, y0)
        m11, m12, m22 = dot(sub1, y1), dot(sub2, y1), dot(sub2, y2)
        alpha = m00[0] / m01[0]
        along = minus(m01, alpha, minus(plus(m02, m11), alpha, m12))
        power = minus(m11, alpha, minus((2.0 * m12[0], 2.0 * m12[1]), alpha, m22))
        omega = along[0] / power[0]
        if cycle + 1 < CYCLES:
            half_list = list_minus(as_list, alpha, list1)
            turn_list = list_minus(list1, alpha, list2)
            gained = gained + [zero] * (len(half_list) - len(gained))
            for k, one in enumerate(half_list):
                gained[k] = gained[k] + (omega / SCALE) * one[0]
            for k, one in enumerate(as_list):
                gained[k] = gained[k] + (alpha / SCALE) * one[0]
            as_list = list_minus(half_list, omega, turn_list)
            as_sub = minus(minus(as_sub, alpha, sub1), omega, minus(sub1, alpha, sub2))

    def combine(i, t, h):
        at = slice(8 * t, 8 * t + 8)
        out = as_list[0][0] * f_ref[1, h, i, at]
        for k in range(1, len(as_list)):
            out = out + as_list[k][0] * f_ref[k + 1, h, i, at]
        return out

    def grid(reach, make):
        out = {}
        for i in range(DEPTH - reach, DEPTH + rows + reach):
            shown = tiles_within(reach - reach_of(i, rows), cols)
            row = make(i, shown)
            out[i] = [[row.get((h, t), zero) for t in range(tiles)] for h in range(2)]
        return out

    residual = grid(
        2, lambda i, shown: {(h, t): combine(i, t, h) for h in range(2) for t in shown}
    )

    def image_row(values, i, shown):
        return stencil_row(values[i - 1], values[i], values[i + 1], coef, i - 1, shown)

    def half_row(i, shown):
        images = image_row(residual, i, shown)
        return {(h, t): residual[i][h][t] - alpha * image for (h, t), image in images.items()}

    half = grid(1, half_row)
    for i in range(DEPTH, DEPTH + rows):
        own = range(HALO // 8, (HALO + cols) // 8)
        for (h, t), turned in image_row(half, i, own).items():
            at = slice(8 * t, 8 * t + 8)
            out = (i - DEPTH, slice(8 * t - HALO, 8 * t - HALO + 8), slice(h * LANES, (h + 1) * LANES))
            x = gained[0] * f_ref[1, h, i, at]
            for k in range(1, len(gained)):
                x = x + gained[k] * f_ref[k + 1, h, i, at]
            mine = guess_ref[h, i, 8 * t - HALO : 8 * t - HALO + 8]
            x = (mine + x) + (alpha / SCALE) * residual[i][h][t]
            x_ref[out] = x + (omega / SCALE) * half[i][h][t]
            r_ref[out] = half[i][h][t] - omega * turned


def body(adjoint_guess, velocity, leaf_rate, canopy, solid, receptors):
    rows, cols, lanes = adjoint_guess.shape
    ngx, ngy = lax.axis_size("gx"), lax.axis_size("gy")
    devices = ngx * ngy
    width = cols + 2 * HALO
    win = rows + 2 * DEPTH
    vmem = pl.BlockSpec(memory_space=pltpu.VMEM)
    hbm = pl.BlockSpec(memory_space=pltpu.HBM)
    wide = lanes + 4 * NZ
    own, far_rows = pl.pallas_call(
        pack_kernel,
        out_shape=(
            pltpu.VMEM((rows, cols, wide), jnp.float32),
            pltpu.VMEM((DEPTH - rows, cols, wide), jnp.float32),
        ),
        in_specs=[hbm] * 5,
        out_specs=(vmem, vmem),
        scratch_shapes=[
            pltpu.VMEM(velocity.shape, jnp.float32),
            pltpu.VMEM(leaf_rate.shape, jnp.float32),
            pltpu.VMEM(canopy.shape, jnp.int32),
            pltpu.VMEM(solid.shape, jnp.int32),
            pltpu.SemaphoreType.DMA((5,)),
        ],
        compiler_params=pltpu.CompilerParams(vmem_limit_bytes=56 * 1024 * 1024),
        name="pack",
    )(adjoint_guess, velocity, leaf_rate, canopy, solid)
    def swap(x, axis, pairs):
        return lax.ppermute(x, axis, pairs + [(j, i) for i, j in pairs])

    place = lax.axis_index("gx")
    far = swap(far_rows, "gx", [(j, j + 2) for j in range(ngx - 2) if j % 4 < 2])
    pair = swap(own, "gx", [(j, j + 1) for j in range(0, ngx - 1, 2)])
    across = swap(own, "gx", [(j, j + 1) for j in range(1, ngx - 1, 2)])
    if ngx > 4:
        other = jnp.where(place % 4 < 2, own[: DEPTH - rows], own[2 * rows - DEPTH :])
        farther = swap(other, "gx", [(j, j + 2) for j in range(ngx - 2) if j % 4 >= 2])
    else:
        farther = jnp.zeros_like(far_rows)

    edge = pltpu.VMEM((rows + 2 * (DEPTH // 2), HALO, wide), jnp.float32)
    outer, inner = pl.pallas_call(
        edges_kernel,
        out_shape=(edge, edge),
        in_specs=[vmem] * 5,
        out_specs=(vmem, vmem),
        compiler_params=pltpu.CompilerParams(vmem_limit_bytes=8 * 1024 * 1024),
        name="edges",
    )(own, pair, across, far, farther)
    outer = swap(outer, "gy", [(j, j + 1) for j in range(1, ngy - 1, 2)])
    inner = swap(inner, "gy", [(j, j + 1) for j in range(0, ngy - 1, 2)])

    source_lane = jnp.arange(4 * NZ)[:, None]
    wide_lane = jnp.arange(4 * NZ * R)[None, :]
    spread = (source_lane == wide_lane // R).astype(jnp.bfloat16)
    spread = jnp.concatenate([spread] * 3, axis=0)
    guess, mine = pl.pallas_call(
        central_kernel,
        out_shape=(
            pltpu.VMEM((2, win, cols, LANES), jnp.float32),
            pltpu.VMEM((7, 2, win - 2, cols, LANES), jnp.float32),
        ),
        in_specs=[vmem] * 6,
        out_specs=(vmem, vmem),
        scratch_shapes=[
            pltpu.VMEM(((win - 2) * cols, LANES), jnp.float32),
            pltpu.VMEM(((win - 2) * cols, 8 * LANES), jnp.float32),
        ],
        compiler_params=pltpu.CompilerParams(vmem_limit_bytes=16 * 1024 * 1024),
        name="central",
    )(own, pair, across, far, farther, spread)

    total_cols = cols * ngy
    cells = jnp.stack([receptors // total_cols, receptors % total_cols])
    halo_rows = win - 4
    vectors = 2 * rows * cols // 8
    gram, basis, halo = pl.pallas_call(
        functools.partial(krylov_kernel, rows, cols),
        out_shape=(
            jax.ShapeDtypeStruct((devices * 8, LANES), jnp.float32),
            pltpu.VMEM((DEPTH + 1, 2, win, width, LANES), jnp.float32),
            pltpu.VMEM((7, 2, win - 2, 2 * HALO, LANES), jnp.float32),
        ),
        in_specs=[pl.BlockSpec(memory_space=pl.ANY)] + [vmem] * 5,
        out_specs=(vmem, vmem, vmem),
        scratch_shapes=[
            pltpu.VMEM((halo_rows * 2 * HALO, LANES), jnp.float32),
            pltpu.VMEM((halo_rows * 2 * HALO, 8 * LANES), jnp.float32),
            pltpu.VMEM((VECS, vectors, 8, LANES), jnp.float32),
            pltpu.VMEM((VECS, vectors, 8, LANES), jnp.float32),
            pltpu.SMEM((2, R), jnp.int32),
            pltpu.SemaphoreType.DMA(()),
        ],
        compiler_params=pltpu.CompilerParams(vmem_limit_bytes=24 * 1024 * 1024),
        name="krylov",
    )(cells, outer, inner, guess, mine, spread)
    everyone = lax.all_to_all(gram, ("gx", "gy"), 0, 0, tiled=True)
    out = jax.ShapeDtypeStruct((rows, cols, lanes), jnp.float32)
    return pl.pallas_call(
        finish_kernel,
        out_shape=(out, out),
        in_specs=[vmem] * 5,
        out_specs=(vmem, vmem),
        compiler_params=pltpu.CompilerParams(vmem_limit_bytes=16 * 1024 * 1024),
        name="finish",
    )(everyone, basis, guess, mine, halo)


def solution(mesh):
    return jax.shard_map(
        body,
        mesh=mesh,
        in_specs=(
            P("gx", "gy", None),
            P(None, "gx", "gy"),
            P("gx", "gy"),
            P("gx", "gy"),
            P("gx", "gy"),
            P(),
        ),
        out_specs=(P("gx", "gy", None), P("gx", "gy", None)),
        check_vma=False,
    )
```

```python
import functools
import math

import jax
import jax.numpy as jnp
from jax import lax
from jax.experimental import pallas as pl
from jax.experimental.pallas import tpu as pltpu
from jax.sharding import PartitionSpec as P

NZ = 32
R = 8
CYCLES = 3
DEPTH = 2 * CYCLES + 1
VECS = DEPTH
HALO = 8
SCALE = 16.0
SHIFT = 2.0
LANES = 128

horiz_diff = 4.0
vert_diff = 2.0
decay_rate = 3.5
penalty = 40.0
leaf_gain = 4.0
source_gain = 32.0


def two_sum(a, b):
    s = a + b
    t = s - a
    return s, (a - (s - t)) + (b - t)


def quick_sum(a, b):
    s = a + b
    return s, b - (s - a)


def split(a):
    c = a * 4097.0
    hi = c - (c - a)
    return hi, a - hi


def two_prod(a, b):
    p = a * b
    ah, al = split(a)
    bh, bl = split(b)
    return p, (((ah * bh - p) + ah * bl) + al * bh) + al * bl


def pack_kernel(
    guess_ref, velocity_ref, leaf_ref, canopy_ref, solid_ref, out_ref, far_ref,
    v_ref, l_ref, c_ref, s_ref, sem,
):
    copies = [
        pltpu.make_async_copy(velocity_ref, v_ref, sem.at[0]),
        pltpu.make_async_copy(leaf_ref, l_ref, sem.at[1]),
        pltpu.make_async_copy(canopy_ref, c_ref, sem.at[2]),
        pltpu.make_async_copy(solid_ref, s_ref, sem.at[3]),
        pltpu.make_async_copy(guess_ref, out_ref.at[:, :, pl.ds(0, NZ * R)], sem.at[4]),
    ]
    for copy in copies:
        copy.start()
    for copy in copies[:4]:
        copy.wait()
    rows, cols = guess_ref.shape[:2]
    lane = lax.broadcasted_iota(jnp.int32, (8, LANES), 1)
    sub = lax.broadcasted_iota(jnp.int32, (8, LANES), 0)
    reaction = penalty * s_ref[...].astype(jnp.float32) + leaf_gain * l_ref[...] * c_ref[
        ...
    ].astype(jnp.float32)
    fields = [v_ref[0], v_ref[1], v_ref[2], reaction]
    for x in range(rows):
        for t in range(cols // 8):
            base = 8 * t * NZ
            spread = []
            for field in fields:
                near = field[x : x + 1, base : base + LANES]
                far = field[x : x + 1, base + LANES : base + 2 * LANES]
                spread.append(
                    jnp.where(
                        sub < 4,
                        jnp.broadcast_to(near, (8, LANES)),
                        jnp.broadcast_to(far, (8, LANES)),
                    )
                )
            whole = None
            for d in range(4):
                mixed = spread[d]
                for s in range(1, 4):
                    mixed = jnp.where(sub % 4 == s, spread[(s + d) % 4], mixed)
                if d == 0:
                    whole = mixed
                else:
                    here = (lane // NZ - sub) % 4 == d
                    whole = jnp.where(here, pltpu.roll(mixed, NZ * d, 1), whole)
            out_ref[x, 8 * t : 8 * t + 8, NZ * R :] = whole
    copies[4].wait()
    count = far_ref.shape[0]
    first = jnp.where(lax.axis_index("gx") % 4 < 2, rows - count, 0)
    for x in range(count):
        far_ref[x] = out_ref[first + x]


def window_row(i, rows, a, own, even, odd, far, farther):
    at = i - DEPTH
    if 0 <= at < rows:
        return own(at)
    if -rows <= at < 0:
        return jnp.where(a % 2 == 1, even(at + rows), odd(at + rows))
    if rows <= at < 2 * rows:
        return jnp.where(a % 2 == 1, odd(at - rows), even(at - rows))
    if at < 0:
        return jnp.where(a % 4 >= 2, far(at + DEPTH), farther(at + DEPTH))
    return jnp.where(a % 4 >= 2, farther(at - 2 * rows), far(at - 2 * rows))


def edges_kernel(
    own_ref, pair_ref, across_ref, far_ref, farther_ref, outer_ref, inner_ref
):
    rows, cols, wide = own_ref.shape
    place = lax.axis_index("gx")
    odd = lax.axis_index("gy") % 2 == 1
    sub = lax.broadcasted_iota(jnp.int32, (8, wide), 0)
    refs = (own_ref, pair_ref, across_ref, far_ref, farther_ref)

    def edge(right):
        c0 = cols - HALO if right else 0
        blocks = [lambda x, ref=ref: ref[x, c0 : c0 + HALO, :] for ref in refs]
        tiles = [window_row(DEPTH + x, rows, place, *blocks) for x in range(rows)]
        for start, way in ((DEPTH, -1), (DEPTH + rows - 1, 1)):
            for d in range(1, DEPTH // 2 + 1):
                close = window_row(start + way * d, rows, place, *blocks)
                distant = window_row(start + way * (DEPTH - d), rows, place, *blocks)
                distant = pltpu.roll(distant, d if right else HALO - d, 0)
                if right:
                    kept = sub >= HALO - DEPTH + d
                else:
                    kept = sub < DEPTH - d
                tiles.append(jnp.where(kept, close, distant))
        return tiles

    for n, (left, right) in enumerate(zip(edge(False), edge(True))):
        outer_ref[n] = jnp.where(odd, right, left)
        inner_ref[n] = jnp.where(odd, left, right)


def reach_of(i, rows):
    return max(DEPTH - i, i - (DEPTH + rows - 1), 0)


def tiles_within(reach, cols):
    shown = []
    for t in range((cols + 2 * HALO) // 8):
        away = max(HALO - (8 * t + 7), 8 * t - (HALO + cols) + 1, 0)
        if away <= reach:
            shown.append(t)
    return shown


def stencil_row(west, mid, east, coef, at, shown):
    lane = lax.broadcasted_iota(jnp.int32, (8, LANES), 1)
    sub = lax.broadcasted_iota(jnp.int32, (8, LANES), 0)
    tiles = len(mid[0])
    ahead = [[pltpu.roll(m, 7, 0) for m in mid[h]] for h in range(2)]
    behind = [[pltpu.roll(m, 1, 0) for m in mid[h]] for h in range(2)]
    images = {}
    for t in shown:
        up = [pltpu.roll(mid[h][t], LANES - R, 1) for h in range(2)]
        down = [pltpu.roll(mid[h][t], R, 1) for h in range(2)]
        above = [jnp.where(lane < LANES - R, up[0], up[1]), up[1]]
        below = [down[0], jnp.where(lane >= R, down[1], down[0])]
        for h in range(2):
            north, south = ahead[h][t], behind[h][t]
            if t + 1 < tiles:
                north = jnp.where(sub < 7, north, ahead[h][t + 1])
            if t > 0:
                south = jnp.where(sub > 0, south, behind[h][t - 1])
            near = [mid[h][t], east[h][t], west[h][t], north, south, above[h], below[h]]
            terms = [coef(c, h, at, t) * near[c] for c in range(7)]
            image = (terms[0] - terms[1]) - (terms[2] + terms[3])
            images[h, t] = image - ((terms[4] + terms[5]) + terms[6])
    return images


def own_tile(t, cols):
    return t - HALO // 8 if HALO <= 8 * t < HALO + cols else None


def coefficients(own_ref, halo_ref, cols):
    def read(c, h, at, t):
        n = own_tile(t, cols)
        if n is not None:
            return own_ref[c, h, at, 8 * n : 8 * n + 8]
        side = 0 if 8 * t < HALO else 8
        return halo_ref[c, h, at, side : side + 8]

    return read


def inside_row(i, rows):
    at = lax.axis_index("gx") * rows - DEPTH + i
    ok = jnp.logical_and(at >= 0, at < rows * lax.axis_size("gx"))
    return jnp.where(ok, 1.0, 0.0)


def widen(raw, spread):
    first = raw.astype(jnp.bfloat16)
    rest = raw - first.astype(jnp.float32)
    second = rest.astype(jnp.bfloat16)
    third = (rest - second.astype(jnp.float32)).astype(jnp.bfloat16)
    pieces = jnp.concatenate([first, second, third], axis=1)
    return jnp.dot(pieces, spread, preferred_element_type=jnp.float32)


def tile_coefficients(wide_ref, at, h, keep):
    lane = lax.broadcasted_iota(jnp.int32, (8, LANES), 1)
    u, v, w, reaction = [
        wide_ref[at : at + 8, (2 * c + h) * LANES : (2 * c + h + 1) * LANES] for c in range(4)
    ]
    side = [
        horiz_diff + jnp.maximum(u, 0.0),
        horiz_diff + jnp.maximum(-u, 0.0),
        horiz_diff + jnp.maximum(v, 0.0),
        horiz_diff + jnp.maximum(-v, 0.0),
        vert_diff + jnp.maximum(w, 0.0),
        vert_diff + jnp.maximum(-w, 0.0),
    ]
    diag = decay_rate + reaction
    for one in side:
        diag = diag + one
    if h == 1:
        side[4] = jnp.where(lane < LANES - R, side[4], 0.0)
    else:
        side[5] = jnp.where(lane >= R, side[5], 0.0)
    return [one * keep for one in [diag] + side]


def central_kernel(
    own_ref, pair_ref, across_ref, far_ref, farther_ref, ex_ref, guess_ref, coef_ref,
    raw_ref, wide_ref,
):
    rows, cols, _ = own_ref.shape
    win = rows + 2 * DEPTH
    place = lax.axis_index("gx")
    refs = (own_ref, pair_ref, across_ref, far_ref, farther_ref)

    def middle(i, lo):
        blocks = [lambda x, ref=ref: ref[x, :, lo : lo + LANES] for ref in refs]
        return window_row(i, rows, place, *blocks)

    for i in range(win):
        for h in range(2):
            guess_ref[h, i] = middle(i, h * LANES) * inside_row(i, rows)
    for i in range(win - 2):
        raw_ref[i * cols : (i + 1) * cols, :] = middle(i + 1, 2 * LANES)
    wide_ref[...] = widen(raw_ref[...], ex_ref[...])
    for i in range(win - 2):
        keep = inside_row(i + 1, rows) * (1.0 / SCALE)
        for t in range(cols // 8):
            for h in range(2):
                values = tile_coefficients(wide_ref, i * cols + 8 * t, h, keep)
                for c, one in enumerate(values):
                    coef_ref[c, h, i, 8 * t : 8 * t + 8] = one


def krylov_kernel(
    rows, cols, rec_ref, outer_ref, inner_ref, guess_ref, mine_ref, ex_ref, gram_ref, f_ref,
    halo_ref, raw_ref, wide_ref, cell_ref, cell_sem,
):
    fetch = pltpu.make_async_copy(rec_ref, cell_ref, cell_sem)
    fetch.start()
    win = rows + 2 * DEPTH
    width = cols + 2 * HALO
    tiles = width // 8
    odd = lax.axis_index("gy") % 2 == 1
    total_cols = cols * lax.axis_size("gy")
    row0 = lax.axis_index("gx") * rows - DEPTH
    col0 = lax.axis_index("gy") * cols - HALO
    lane = lax.broadcasted_iota(jnp.int32, (8, LANES), 1)
    sub = lax.broadcasted_iota(jnp.int32, (8, LANES), 0)
    sides = ((0, True), (HALO + cols, False))

    def edge(i, lo, right):
        away = reach_of(i, rows)
        if away == 0:
            n, turn = i - DEPTH, 0
        else:
            d = min(away, DEPTH - away)
            n = rows + (0 if i < DEPTH else DEPTH // 2) + d - 1
            turn = 0 if d == away else (HALO - d if right else d)
        outer, inner = [ref[n, :, lo : lo + LANES] for ref in (outer_ref, inner_ref)]
        tile = jnp.where(odd, inner, outer) if right else jnp.where(odd, outer, inner)
        return pltpu.roll(tile, turn, 0) if turn else tile

    for i in range(1, win - 1):
        for h in range(2):
            for c0, right in sides:
                f_ref[0, h, i, c0 : c0 + HALO] = edge(i, h * LANES, right) * inside_row(i, rows)

    needed = [i for i in range(1, win - 1) if reach_of(i, rows) < DEPTH - 1]
    for n, i in enumerate(needed):
        for side, (c0, right) in enumerate(sides):
            at = (2 * n + side) * HALO
            raw_ref[at : at + HALO, :] = edge(i, 2 * LANES, right)
    wide_ref[...] = widen(raw_ref[...], ex_ref[...])
    for n, i in enumerate(needed):
        for side, (c0, right) in enumerate(sides):
            at_col = col0 + c0 + sub
            seen = jnp.logical_and(at_col >= 0, at_col < total_cols)
            keep = jnp.where(seen, inside_row(i, rows) * (1.0 / SCALE), 0.0)
            for h in range(2):
                values = tile_coefficients(wide_ref, (2 * n + side) * HALO, h, keep)
                for c, one in enumerate(values):
                    halo_ref[c, h, i - 1, side * HALO : (side + 1) * HALO] = one

    coef = coefficients(mine_ref, halo_ref, cols)

    def read(k, h, i, t):
        n = own_tile(t, cols)
        if k == 0 and n is not None:
            return guess_ref[h, i, 8 * n : 8 * n + 8]
        return f_ref[k, h, i, 8 * t : 8 * t + 8]

    def load(k, i):
        return [[read(k, h, i, t) for t in range(tiles)] for h in range(2)]

    def apply(step, finish):
        west, mid = load(step - 1, step - 1), load(step - 1, step)
        for i in range(step, win - step):
            east = load(step - 1, i + 1)
            shown = tiles_within(DEPTH - step - reach_of(i, rows), cols)
            images = stencil_row(west, mid, east, coef, i - 1, shown)
            for (h, t), image in images.items():
                f_ref[step, h, i, 8 * t : 8 * t + 8] = finish(image, mid[h][t])
            west, mid = mid, east

    apply(1, lambda image, mid: -SCALE * image)
    fetch.wait()
    for q in range(R):
        i = cell_ref[0, q] - row0
        c = cell_ref[1, q] - col0
        seen = (i >= 1) & (i < win - 1) & (c >= 0) & (c < width)
        i = jnp.clip(i, 1, win - 2)
        c = jnp.clip(c, 0, width - 1)
        base = pl.multiple_of((c // 8) * 8, 8)
        gain = jnp.where(seen, source_gain, 0.0)
        spot = jnp.where((sub == c % 8) & (lane == R + q), gain, 0.0)
        f_ref[1, 0, i, pl.ds(base, 8)] += spot
    for step in range(2, DEPTH + 1):
        apply(step, lambda image, mid: image - SHIFT * mid)

    pieces = [
        (h, i, t) for h in range(2) for i in range(rows) for t in range(cols // 8)
    ]
    zero = jnp.zeros((8, LANES), jnp.float32)
    sums = {}
    for group in ([0, 1, 2, 3], [4, 5], [6]):
        pairs = [(i, j) for j in group for i in range(j + 1)]

        done = [(zero, zero)] * len(pairs)
        for h, row, t in pieces:
            need = sorted({i for pair in pairs for i in pair})
            at = slice(HALO + 8 * t, HALO + 8 * t + 8)
            full = {k: f_ref[k + 1, h, DEPTH + row, at] for k in need}
            halves = {k: split(full[k]) for k in need}
            hi = {k: halves[k][0] for k in need}
            lo = {k: halves[k][1] for k in need}
            out = []
            for (i, j), (s, e) in zip(pairs, done):
                s, miss = two_sum(s, hi[i] * hi[j])
                if i == j:
                    cross = lo[j] * (hi[i] + full[i])
                else:
                    cross = hi[i] * lo[j] + lo[i] * full[j]
                out.append((s, e + (cross + miss)))
            done = out
        for pair, value in zip(pairs, done):
            sums[pair] = value

    def merge(a, b, axis, step):
        where = (sub if axis == 0 else lane) & step
        first = where == 0
        size = 8 if axis == 0 else LANES
        out = []
        for x, y in zip(a, b):
            kept = jnp.where(first, x, y)
            moved = jnp.where(first, y, x)
            if 2 * step == size:
                moved = pltpu.roll(moved, step, axis)
            else:
                moved = jnp.where(
                    first, pltpu.roll(moved, size - step, axis), pltpu.roll(moved, step, axis)
                )
            out.append((kept, moved))
        (s0, s1), (e0, e1) = out
        s, miss = two_sum(s0, s1)
        return s, (e0 + e1) + miss

    def tree(items, axis, steps):
        for step in steps:
            half = len(items) // 2
            items = [merge(items[n], items[n + half], axis, step) for n in range(half)]
        return items[0]

    columns = []
    for j in range(8):
        i_list = [sums.get((min(i, j), max(i, j)), (zero, zero)) for i in range(8)]
        columns.append(tree(i_list, 0, (4, 2, 1)) if j < VECS else (zero, zero))
    s, e = tree(columns, 1, (64, 32, 16))
    low = (lane & R) == 0
    s1 = jnp.where(low, pltpu.roll(s, LANES - R, 1), pltpu.roll(s, R, 1))
    e1 = jnp.where(low, pltpu.roll(e, LANES - R, 1), pltpu.roll(e, R, 1))
    s, miss = two_sum(s, s1)
    e = (e + e1) + miss
    s, e = quick_sum(s, e)
    chunk = jnp.where(low, s, e)
    folded = chunk
    for r, turn in ((1, 3), (2, 5), (3, 7)):
        other = pltpu.roll(pltpu.roll(chunk, turn, 0), 2 * R * (r + 1), 1)
        folded = jnp.where((sub == r) & (lane // (2 * R) < r), other, folded)
    for n in range(gram_ref.shape[0] // 4):
        gram_ref[4 * n : 4 * n + 4] = folded[:4]


def finish_kernel(gram_ref, f_ref, guess_ref, mine_ref, halo_ref, x_ref, r_ref):
    rows, cols = x_ref.shape[:2]
    coef = coefficients(mine_ref, halo_ref, cols)
    tiles = (cols + 2 * HALO) // 8
    lane = lax.broadcasted_iota(jnp.int32, (8, LANES), 1)
    sub = lax.broadcasted_iota(jnp.int32, (8, LANES), 0)
    pairs = gram_ref.shape[0] // 8
    ways = math.gcd(pairs, 8)
    zero = jnp.zeros((8, LANES), jnp.float32)

    def plus(a, b):
        s, miss = two_sum(a[0], b[0])
        return s, (a[1] + b[1]) + miss

    def total(items):
        while len(items) > 1:
            half = len(items) // 2
            pairs = [plus(items[2 * n], items[2 * n + 1]) for n in range(half)]
            items = pairs + items[2 * half :]
        return items[0]

    def gather(n, carry):
        out = []
        for w, (s, e) in enumerate(carry):
            at = pl.multiple_of((n * ways + w) * 8, 8)
            s, miss = two_sum(s, gram_ref[pl.ds(at, 8), :])
            out.append((s, e + miss))
        return tuple(out)

    steps = pairs // ways
    s, e = total(
        list(lax.fori_loop(0, steps, gather, ((zero, zero),) * ways, unroll=steps <= 8))
    )
    s, e = plus((s, e), (pltpu.roll(s, 4, 0), pltpu.roll(e, 4, 0)))
    low = (lane & R) == 0
    g_hi = jnp.where(low, s, pltpu.roll(s, R, 1))
    g_lo = jnp.where(low, pltpu.roll(s, LANES - R, 1) + e, s + pltpu.roll(e, R, 1))
    g_hi, g_lo = quick_sum(g_hi, g_lo)

    block = lane // (2 * R)

    def unfold(x):
        for i, turn in ((4, 1), (5, 3), (6, 5)):
            x = jnp.where(sub == i, pltpu.roll(pltpu.roll(x, turn, 0), 2 * R * i, 1), x)
        return x

    def column(x, j):
        turned = jnp.where(block == sub, jnp.broadcast_to(x[j : j + 1], x.shape), 0.0)
        x = jnp.where(sub <= j, jnp.where(block == j, x, 0.0), turned)
        for step in (64, 32, 16):
            x = x + pltpu.roll(x, step, 1)
        return jnp.where(sub < VECS, x, 0.0)

    g_hi, g_lo = unfold(g_hi), unfold(g_lo)
    grams = [(column(g_hi, j), column(g_lo, j)) for j in range(VECS)]
    gram_splits = [split(g[0]) for g in grams]

    def product(a, b, a_split, b_split):
        p = a[0] * b[0]
        (ah, al), (bh, bl) = a_split, b_split
        e = (((ah * bh - p) + ah * bl) + al * bh) + al * bl
        return p, e + (a[0] * b[1] + a[1] * b[0])

    def minus(a, factor, b):
        p, e = two_prod(factor, b[0])
        s, miss = two_sum(a[0], -p)
        return quick_sum(s, (a[1] - (e + factor * b[1])) + miss)


    def list_image(p):
        out = [(SHIFT * p[0][0], SHIFT * p[0][1])]
        for k in range(1, len(p)):
            out.append(quick_sum(*plus((SHIFT * p[k][0], SHIFT * p[k][1]), p[k - 1])))
        return out + [p[-1]]

    def sub_image(p):
        moved = pltpu.roll(p[0], 1, 0), pltpu.roll(p[1], 1, 0)
        return quick_sum(*plus((SHIFT * p[0], SHIFT * p[1]), moved))

    def list_minus(a, factor, b):
        a = a + [(zero, zero)] * (len(b) - len(a))
        return [minus(x, factor, y) for x, y in zip(a, b)]

    def apply_gram(p):
        return quick_sum(
            *total([product(g, x, gs, split(x[0])) for g, gs, x in zip(grams, gram_splits, p)])
        )

    def dot(a, b):
        p, e = product(a, b, split(a[0]), split(b[0]))
        for step in (4, 2, 1):
            p, e = plus((p, e), (pltpu.roll(p, step, 0), pltpu.roll(e, step, 0)))
        return quick_sum(p, e)

    as_list = [(zero + 1.0, zero)]
    as_sub = (jnp.where(sub == 0, 1.0, 0.0), zero)
    gained = []
    for cycle in range(CYCLES):
        list1 = list_image(as_list)
        list2 = list_image(list1)
        sub1 = sub_image(as_sub)
        sub2 = sub_image(sub1)
        y0, y1, y2 = apply_gram(as_list), apply_gram(list1), apply_gram(list2)
        m00, m01, m02 = dot(as_sub, y0), dot(sub1, y0), dot(sub2, y0)
        m11, m12, m22 = dot(sub1, y1), dot(sub2, y1), dot(sub2, y2)
        alpha = m00[0] / m01[0]
        along = minus(m01, alpha, minus(plus(m02, m11), alpha, m12))
        power = minus(m11, alpha, minus((2.0 * m12[0], 2.0 * m12[1]), alpha, m22))
        omega = along[0] / power[0]
        if cycle + 1 < CYCLES:
            half_list = list_minus(as_list, alpha, list1)
            turn_list = list_minus(list1, alpha, list2)
            gained = gained + [zero] * (len(half_list) - len(gained))
            for k, one in enumerate(half_list):
                gained[k] = gained[k] + (omega / SCALE) * one[0]
            for k, one in enumerate(as_list):
                gained[k] = gained[k] + (alpha / SCALE) * one[0]
            as_list = list_minus(half_list, omega, turn_list)
            as_sub = minus(minus(as_sub, alpha, sub1), omega, minus(sub1, alpha, sub2))

    def combine(i, t, h):
        at = slice(8 * t, 8 * t + 8)
        out = as_list[0][0] * f_ref[1, h, i, at]
        for k in range(1, len(as_list)):
            out = out + as_list[k][0] * f_ref[k + 1, h, i, at]
        return out

    def grid(reach, make):
        out = {}
        for i in range(DEPTH - reach, DEPTH + rows + reach):
            shown = tiles_within(reach - reach_of(i, rows), cols)
            row = make(i, shown)
            out[i] = [[row.get((h, t), zero) for t in range(tiles)] for h in range(2)]
        return out

    residual = grid(
        2, lambda i, shown: {(h, t): combine(i, t, h) for h in range(2) for t in shown}
    )

    def image_row(values, i, shown):
        return stencil_row(values[i - 1], values[i], values[i + 1], coef, i - 1, shown)

    def half_row(i, shown):
        images = image_row(residual, i, shown)
        return {(h, t): residual[i][h][t] - alpha * image for (h, t), image in images.items()}

    half = grid(1, half_row)
    for i in range(DEPTH, DEPTH + rows):
        own = range(HALO // 8, (HALO + cols) // 8)
        for (h, t), turned in image_row(half, i, own).items():
            at = slice(8 * t, 8 * t + 8)
            out = (i - DEPTH, slice(8 * t - HALO, 8 * t - HALO + 8), slice(h * LANES, (h + 1) * LANES))
            x = gained[0] * f_ref[1, h, i, at]
            for k in range(1, len(gained)):
                x = x + gained[k] * f_ref[k + 1, h, i, at]
            mine = guess_ref[h, i, 8 * t - HALO : 8 * t - HALO + 8]
            x = (mine + x) + (alpha / SCALE) * residual[i][h][t]
            x_ref[out] = x + (omega / SCALE) * half[i][h][t]
            r_ref[out] = half[i][h][t] - omega * turned


def body(adjoint_guess, velocity, leaf_rate, canopy, solid, receptors):
    rows, cols, lanes = adjoint_guess.shape
    ngx, ngy = lax.axis_size("gx"), lax.axis_size("gy")
    devices = ngx * ngy
    width = cols + 2 * HALO
    win = rows + 2 * DEPTH
    vmem = pl.BlockSpec(memory_space=pltpu.VMEM)
    hbm = pl.BlockSpec(memory_space=pltpu.HBM)
    wide = lanes + 4 * NZ
    own, far_rows = pl.pallas_call(
        pack_kernel,
        out_shape=(
            pltpu.VMEM((rows, cols, wide), jnp.float32),
            pltpu.VMEM((DEPTH - rows, cols, wide), jnp.float32),
        ),
        in_specs=[hbm] * 5,
        out_specs=(vmem, vmem),
        scratch_shapes=[
            pltpu.VMEM(velocity.shape, jnp.float32),
            pltpu.VMEM(leaf_rate.shape, jnp.float32),
            pltpu.VMEM(canopy.shape, jnp.int32),
            pltpu.VMEM(solid.shape, jnp.int32),
            pltpu.SemaphoreType.DMA((5,)),
        ],
        compiler_params=pltpu.CompilerParams(vmem_limit_bytes=56 * 1024 * 1024),
        name="pack",
    )(adjoint_guess, velocity, leaf_rate, canopy, solid)
    def swap(x, axis, pairs):
        return lax.ppermute(x, axis, pairs + [(j, i) for i, j in pairs])

    place = lax.axis_index("gx")
    far = swap(far_rows, "gx", [(j, j + 2) for j in range(ngx - 2) if j % 4 < 2])
    pair = swap(own, "gx", [(j, j + 1) for j in range(0, ngx - 1, 2)])
    across = swap(own, "gx", [(j, j + 1) for j in range(1, ngx - 1, 2)])
    if ngx > 4:
        other = jnp.where(place % 4 < 2, own[: DEPTH - rows], own[2 * rows - DEPTH :])
        farther = swap(other, "gx", [(j, j + 2) for j in range(ngx - 2) if j % 4 >= 2])
    else:
        farther = jnp.zeros_like(far_rows)

    edge = pltpu.VMEM((rows + 2 * (DEPTH // 2), HALO, wide), jnp.float32)
    outer, inner = pl.pallas_call(
        edges_kernel,
        out_shape=(edge, edge),
        in_specs=[vmem] * 5,
        out_specs=(vmem, vmem),
        compiler_params=pltpu.CompilerParams(vmem_limit_bytes=8 * 1024 * 1024),
        name="edges",
    )(own, pair, across, far, farther)
    outer = swap(outer, "gy", [(j, j + 1) for j in range(1, ngy - 1, 2)])
    inner = swap(inner, "gy", [(j, j + 1) for j in range(0, ngy - 1, 2)])

    source_lane = jnp.arange(4 * NZ)[:, None]
    wide_lane = jnp.arange(4 * NZ * R)[None, :]
    spread = (source_lane == wide_lane // R).astype(jnp.bfloat16)
    spread = jnp.concatenate([spread] * 3, axis=0)
    guess, mine = pl.pallas_call(
        central_kernel,
        out_shape=(
            pltpu.VMEM((2, win, cols, LANES), jnp.float32),
            pltpu.VMEM((7, 2, win - 2, cols, LANES), jnp.float32),
        ),
        in_specs=[vmem] * 6,
        out_specs=(vmem, vmem),
        scratch_shapes=[
            pltpu.VMEM(((win - 2) * cols, LANES), jnp.float32),
            pltpu.VMEM(((win - 2) * cols, 8 * LANES), jnp.float32),
        ],
        compiler_params=pltpu.CompilerParams(vmem_limit_bytes=16 * 1024 * 1024),
        name="central",
    )(own, pair, across, far, farther, spread)

    total_cols = cols * ngy
    cells = jnp.stack([receptors // total_cols, receptors % total_cols])
    halo_rows = win - 4
    gram, basis, halo = pl.pallas_call(
        functools.partial(krylov_kernel, rows, cols),
        out_shape=(
            jax.ShapeDtypeStruct((devices * 4, LANES), jnp.float32),
            pltpu.VMEM((DEPTH + 1, 2, win, width, LANES), jnp.float32),
            pltpu.VMEM((7, 2, win - 2, 2 * HALO, LANES), jnp.float32),
        ),
        in_specs=[pl.BlockSpec(memory_space=pl.ANY)] + [vmem] * 5,
        out_specs=(vmem, vmem, vmem),
        scratch_shapes=[
            pltpu.VMEM((halo_rows * 2 * HALO, LANES), jnp.float32),
            pltpu.VMEM((halo_rows * 2 * HALO, 8 * LANES), jnp.float32),
            pltpu.SMEM((2, R), jnp.int32),
            pltpu.SemaphoreType.DMA(()),
        ],
        compiler_params=pltpu.CompilerParams(vmem_limit_bytes=24 * 1024 * 1024),
        name="krylov",
    )(cells, outer, inner, guess, mine, spread)
    everyone = lax.all_to_all(gram, ("gx", "gy"), 0, 0, tiled=True)
    out = jax.ShapeDtypeStruct((rows, cols, lanes), jnp.float32)
    return pl.pallas_call(
        finish_kernel,
        out_shape=(out, out),
        in_specs=[vmem] * 5,
        out_specs=(vmem, vmem),
        compiler_params=pltpu.CompilerParams(vmem_limit_bytes=16 * 1024 * 1024),
        name="finish",
    )(everyone, basis, guess, mine, halo)


def solution(mesh):
    return jax.shard_map(
        body,
        mesh=mesh,
        in_specs=(
            P("gx", "gy", None),
            P(None, "gx", "gy"),
            P("gx", "gy"),
            P("gx", "gy"),
            P("gx", "gy"),
            P(),
        ),
        out_specs=(P("gx", "gy", None), P("gx", "gy", None)),
        check_vma=False,
    )
```

```python
import functools
import math

import jax
import jax.numpy as jnp
from jax import lax
from jax.experimental import pallas as pl
from jax.experimental.pallas import tpu as pltpu
from jax.sharding import PartitionSpec as P

NZ = 32
R = 8
CYCLES = 3
DEPTH = 2 * CYCLES + 1
VECS = DEPTH
HALO = 8
SCALE = 16.0
SHIFT = 2.0
LANES = 128

horiz_diff = 4.0
vert_diff = 2.0
decay_rate = 3.5
penalty = 40.0
leaf_gain = 4.0
source_gain = 32.0


def two_sum(a, b):
    s = a + b
    t = s - a
    return s, (a - (s - t)) + (b - t)


def quick_sum(a, b):
    s = a + b
    return s, b - (s - a)


def split(a):
    c = a * 4097.0
    hi = c - (c - a)
    return hi, a - hi


def two_prod(a, b):
    p = a * b
    ah, al = split(a)
    bh, bl = split(b)
    return p, (((ah * bh - p) + ah * bl) + al * bh) + al * bl


def pack_kernel(
    guess_ref, velocity_ref, leaf_ref, canopy_ref, solid_ref, out_ref, far_ref,
    v_ref, l_ref, c_ref, s_ref, sem,
):
    copies = [
        pltpu.make_async_copy(velocity_ref, v_ref, sem.at[0]),
        pltpu.make_async_copy(leaf_ref, l_ref, sem.at[1]),
        pltpu.make_async_copy(canopy_ref, c_ref, sem.at[2]),
        pltpu.make_async_copy(solid_ref, s_ref, sem.at[3]),
        pltpu.make_async_copy(guess_ref, out_ref.at[:, :, pl.ds(0, NZ * R)], sem.at[4]),
    ]
    for copy in copies:
        copy.start()
    for copy in copies[:4]:
        copy.wait()
    rows, cols = guess_ref.shape[:2]
    lane = lax.broadcasted_iota(jnp.int32, (8, LANES), 1)
    sub = lax.broadcasted_iota(jnp.int32, (8, LANES), 0)
    reaction = penalty * s_ref[...].astype(jnp.float32) + leaf_gain * l_ref[...] * c_ref[
        ...
    ].astype(jnp.float32)
    fields = [v_ref[0], v_ref[1], v_ref[2], reaction]
    for x in range(rows):
        for t in range(cols // 8):
            base = 8 * t * NZ
            spread = []
            for field in fields:
                near = field[x : x + 1, base : base + LANES]
                far = field[x : x + 1, base + LANES : base + 2 * LANES]
                spread.append(
                    jnp.where(
                        sub < 4,
                        jnp.broadcast_to(near, (8, LANES)),
                        jnp.broadcast_to(far, (8, LANES)),
                    )
                )
            whole = None
            for d in range(4):
                mixed = spread[d]
                for s in range(1, 4):
                    mixed = jnp.where(sub % 4 == s, spread[(s + d) % 4], mixed)
                if d == 0:
                    whole = mixed
                else:
                    here = (lane // NZ - sub) % 4 == d
                    whole = jnp.where(here, pltpu.roll(mixed, NZ * d, 1), whole)
            out_ref[x, 8 * t : 8 * t + 8, NZ * R :] = whole
    copies[4].wait()
    count = far_ref.shape[0]
    first = jnp.where(lax.axis_index("gx") % 4 < 2, rows - count, 0)
    for x in range(count):
        far_ref[x] = out_ref[first + x]


def window_row(i, rows, a, own, even, odd, far, farther):
    at = i - DEPTH
    if 0 <= at < rows:
        return own(at)
    if -rows <= at < 0:
        return jnp.where(a % 2 == 1, even(at + rows), odd(at + rows))
    if rows <= at < 2 * rows:
        return jnp.where(a % 2 == 1, odd(at - rows), even(at - rows))
    if at < 0:
        return jnp.where(a % 4 >= 2, far(at + DEPTH), farther(at + DEPTH))
    return jnp.where(a % 4 >= 2, farther(at - 2 * rows), far(at - 2 * rows))


def sides_kernel(own_ref, outer_ref, inner_ref):
    cols = own_ref.shape[1]
    odd = lax.axis_index("gy") % 2 == 1
    for n in range(own_ref.shape[0]):
        left, right = own_ref[n, :HALO, :], own_ref[n, cols - HALO :, :]
        outer_ref[n] = jnp.where(odd, right, left)
        inner_ref[n] = jnp.where(odd, left, right)


def edges_kernel(
    own_ref, pair_ref, across_ref, far_ref, farther_ref, outer_ref, inner_ref
):
    rows, cols, wide = own_ref.shape
    place = lax.axis_index("gx")
    odd = lax.axis_index("gy") % 2 == 1
    sub = lax.broadcasted_iota(jnp.int32, (8, wide), 0)
    refs = (own_ref, pair_ref, across_ref, far_ref, farther_ref)

    def edge(right):
        c0 = cols - HALO if right else 0
        blocks = [lambda x, ref=ref: ref[x, c0 : c0 + HALO, :] for ref in refs]
        tiles = []
        for start, way in ((DEPTH, -1), (DEPTH + rows - 1, 1)):
            for d in range(1, DEPTH // 2 + 1):
                close = window_row(start + way * d, rows, place, *blocks)
                distant = window_row(start + way * (DEPTH - d), rows, place, *blocks)
                distant = pltpu.roll(distant, d if right else HALO - d, 0)
                if right:
                    kept = sub >= HALO - DEPTH + d
                else:
                    kept = sub < DEPTH - d
                tiles.append(jnp.where(kept, close, distant))
        return tiles

    for n, (left, right) in enumerate(zip(edge(False), edge(True))):
        outer_ref[n] = jnp.where(odd, right, left)
        inner_ref[n] = jnp.where(odd, left, right)


def reach_of(i, rows):
    return max(DEPTH - i, i - (DEPTH + rows - 1), 0)


def tiles_within(reach, cols):
    shown = []
    for t in range((cols + 2 * HALO) // 8):
        away = max(HALO - (8 * t + 7), 8 * t - (HALO + cols) + 1, 0)
        if away <= reach:
            shown.append(t)
    return shown


def stencil_row(west, mid, east, coef, at, shown):
    lane = lax.broadcasted_iota(jnp.int32, (8, LANES), 1)
    sub = lax.broadcasted_iota(jnp.int32, (8, LANES), 0)
    tiles = len(mid[0])
    ahead = [[pltpu.roll(m, 7, 0) for m in mid[h]] for h in range(2)]
    behind = [[pltpu.roll(m, 1, 0) for m in mid[h]] for h in range(2)]
    images = {}
    for t in shown:
        up = [pltpu.roll(mid[h][t], LANES - R, 1) for h in range(2)]
        down = [pltpu.roll(mid[h][t], R, 1) for h in range(2)]
        above = [jnp.where(lane < LANES - R, up[0], up[1]), up[1]]
        below = [down[0], jnp.where(lane >= R, down[1], down[0])]
        for h in range(2):
            north, south = ahead[h][t], behind[h][t]
            if t + 1 < tiles:
                north = jnp.where(sub < 7, north, ahead[h][t + 1])
            if t > 0:
                south = jnp.where(sub > 0, south, behind[h][t - 1])
            near = [mid[h][t], east[h][t], west[h][t], north, south, above[h], below[h]]
            terms = [coef(c, h, at, t) * near[c] for c in range(7)]
            image = (terms[0] - terms[1]) - (terms[2] + terms[3])
            images[h, t] = image - ((terms[4] + terms[5]) + terms[6])
    return images


def own_tile(t, cols):
    return t - HALO // 8 if HALO <= 8 * t < HALO + cols else None


def coefficients(own_ref, halo_ref, cols):
    def read(c, h, at, t):
        n = own_tile(t, cols)
        if n is not None:
            return own_ref[c, h, at, 8 * n : 8 * n + 8]
        side = 0 if 8 * t < HALO else 8
        return halo_ref[c, h, at, side : side + 8]

    return read


def inside_row(i, rows):
    at = lax.axis_index("gx") * rows - DEPTH + i
    ok = jnp.logical_and(at >= 0, at < rows * lax.axis_size("gx"))
    return jnp.where(ok, 1.0, 0.0)


def widen(raw, spread):
    first = raw.astype(jnp.bfloat16)
    rest = raw - first.astype(jnp.float32)
    second = rest.astype(jnp.bfloat16)
    third = (rest - second.astype(jnp.float32)).astype(jnp.bfloat16)
    pieces = jnp.concatenate([first, second, third], axis=1)
    return jnp.dot(pieces, spread, preferred_element_type=jnp.float32)


def tile_coefficients(wide_ref, at, h, keep):
    lane = lax.broadcasted_iota(jnp.int32, (8, LANES), 1)
    u, v, w, reaction = [
        wide_ref[at : at + 8, (2 * c + h) * LANES : (2 * c + h + 1) * LANES] for c in range(4)
    ]
    side = [
        horiz_diff + jnp.maximum(u, 0.0),
        horiz_diff + jnp.maximum(-u, 0.0),
        horiz_diff + jnp.maximum(v, 0.0),
        horiz_diff + jnp.maximum(-v, 0.0),
        vert_diff + jnp.maximum(w, 0.0),
        vert_diff + jnp.maximum(-w, 0.0),
    ]
    diag = decay_rate + reaction
    for one in side:
        diag = diag + one
    if h == 1:
        side[4] = jnp.where(lane < LANES - R, side[4], 0.0)
    else:
        side[5] = jnp.where(lane >= R, side[5], 0.0)
    return [one * keep for one in [diag] + side]


def central_kernel(
    own_ref, pair_ref, across_ref, far_ref, farther_ref, ex_ref, guess_ref, coef_ref,
    raw_ref, wide_ref,
):
    rows, cols, _ = own_ref.shape
    win = rows + 2 * DEPTH
    place = lax.axis_index("gx")
    refs = (own_ref, pair_ref, across_ref, far_ref, farther_ref)

    def middle(i, lo):
        blocks = [lambda x, ref=ref: ref[x, :, lo : lo + LANES] for ref in refs]
        return window_row(i, rows, place, *blocks)

    for i in range(win):
        for h in range(2):
            guess_ref[h, i] = middle(i, h * LANES) * inside_row(i, rows)
    for i in range(win - 2):
        raw_ref[i * cols : (i + 1) * cols, :] = middle(i + 1, 2 * LANES)
    wide_ref[...] = widen(raw_ref[...], ex_ref[...])
    for i in range(win - 2):
        keep = inside_row(i + 1, rows) * (1.0 / SCALE)
        for t in range(cols // 8):
            for h in range(2):
                values = tile_coefficients(wide_ref, i * cols + 8 * t, h, keep)
                for c, one in enumerate(values):
                    coef_ref[c, h, i, 8 * t : 8 * t + 8] = one


def krylov_kernel(
    rows, cols, rec_ref, outer_own_ref, inner_own_ref, outer_ref, inner_ref, guess_ref, mine_ref, ex_ref, gram_ref, f_ref,
    halo_ref, raw_ref, wide_ref, cell_ref, cell_sem,
):
    fetch = pltpu.make_async_copy(rec_ref, cell_ref, cell_sem)
    fetch.start()
    win = rows + 2 * DEPTH
    width = cols + 2 * HALO
    tiles = width // 8
    odd = lax.axis_index("gy") % 2 == 1
    total_cols = cols * lax.axis_size("gy")
    row0 = lax.axis_index("gx") * rows - DEPTH
    col0 = lax.axis_index("gy") * cols - HALO
    lane = lax.broadcasted_iota(jnp.int32, (8, LANES), 1)
    sub = lax.broadcasted_iota(jnp.int32, (8, LANES), 0)
    sides = ((0, True), (HALO + cols, False))

    def edge(i, lo, right):
        away = reach_of(i, rows)
        refs = outer_ref, inner_ref
        if away == 0:
            refs = outer_own_ref, inner_own_ref
            n, turn = i - DEPTH, 0
        else:
            d = min(away, DEPTH - away)
            n = (0 if i < DEPTH else DEPTH // 2) + d - 1
            turn = 0 if d == away else (HALO - d if right else d)
        outer, inner = [ref[n, :, lo : lo + LANES] for ref in refs]
        tile = jnp.where(odd, inner, outer) if right else jnp.where(odd, outer, inner)
        return pltpu.roll(tile, turn, 0) if turn else tile

    for i in range(1, win - 1):
        for h in range(2):
            for c0, right in sides:
                f_ref[0, h, i, c0 : c0 + HALO] = edge(i, h * LANES, right) * inside_row(i, rows)

    needed = [i for i in range(1, win - 1) if reach_of(i, rows) < DEPTH - 1]
    for n, i in enumerate(needed):
        for side, (c0, right) in enumerate(sides):
            at = (2 * n + side) * HALO
            raw_ref[at : at + HALO, :] = edge(i, 2 * LANES, right)
    wide_ref[...] = widen(raw_ref[...], ex_ref[...])
    for n, i in enumerate(needed):
        for side, (c0, right) in enumerate(sides):
            at_col = col0 + c0 + sub
            seen = jnp.logical_and(at_col >= 0, at_col < total_cols)
            keep = jnp.where(seen, inside_row(i, rows) * (1.0 / SCALE), 0.0)
            for h in range(2):
                values = tile_coefficients(wide_ref, (2 * n + side) * HALO, h, keep)
                for c, one in enumerate(values):
                    halo_ref[c, h, i - 1, side * HALO : (side + 1) * HALO] = one

    coef = coefficients(mine_ref, halo_ref, cols)

    def read(k, h, i, t):
        n = own_tile(t, cols)
        if k == 0 and n is not None:
            return guess_ref[h, i, 8 * n : 8 * n + 8]
        return f_ref[k, h, i, 8 * t : 8 * t + 8]

    def load(k, i):
        return [[read(k, h, i, t) for t in range(tiles)] for h in range(2)]

    def apply(step, finish):
        west, mid = load(step - 1, step - 1), load(step - 1, step)
        for i in range(step, win - step):
            east = load(step - 1, i + 1)
            shown = tiles_within(DEPTH - step - reach_of(i, rows), cols)
            images = stencil_row(west, mid, east, coef, i - 1, shown)
            for (h, t), image in images.items():
                f_ref[step, h, i, 8 * t : 8 * t + 8] = finish(image, mid[h][t])
            west, mid = mid, east

    apply(1, lambda image, mid: -SCALE * image)
    fetch.wait()
    for q in range(R):
        i = cell_ref[0, q] - row0
        c = cell_ref[1, q] - col0
        seen = (i >= 1) & (i < win - 1) & (c >= 0) & (c < width)
        i = jnp.clip(i, 1, win - 2)
        c = jnp.clip(c, 0, width - 1)
        base = pl.multiple_of((c // 8) * 8, 8)
        gain = jnp.where(seen, source_gain, 0.0)
        spot = jnp.where((sub == c % 8) & (lane == R + q), gain, 0.0)
        f_ref[1, 0, i, pl.ds(base, 8)] += spot
    for step in range(2, DEPTH + 1):
        apply(step, lambda image, mid: image - SHIFT * mid)

    pieces = [
        (h, i, t) for h in range(2) for i in range(rows) for t in range(cols // 8)
    ]
    zero = jnp.zeros((8, LANES), jnp.float32)
    sums = {}
    for group in ([0, 1, 2, 3], [4, 5], [6]):
        pairs = [(i, j) for j in group for i in range(j + 1)]

        done = [(zero, zero)] * len(pairs)
        for h, row, t in pieces:
            need = sorted({i for pair in pairs for i in pair})
            at = slice(HALO + 8 * t, HALO + 8 * t + 8)
            full = {k: f_ref[k + 1, h, DEPTH + row, at] for k in need}
            halves = {k: split(full[k]) for k in need}
            hi = {k: halves[k][0] for k in need}
            lo = {k: halves[k][1] for k in need}
            out = []
            for (i, j), (s, e) in zip(pairs, done):
                s, miss = two_sum(s, hi[i] * hi[j])
                if i == j:
                    cross = lo[j] * (hi[i] + full[i])
                else:
                    cross = hi[i] * lo[j] + lo[i] * full[j]
                out.append((s, e + (cross + miss)))
            done = out
        for pair, value in zip(pairs, done):
            sums[pair] = value

    def merge(a, b, axis, step):
        where = (sub if axis == 0 else lane) & step
        first = where == 0
        size = 8 if axis == 0 else LANES
        out = []
        for x, y in zip(a, b):
            kept = jnp.where(first, x, y)
            moved = jnp.where(first, y, x)
            if 2 * step == size:
                moved = pltpu.roll(moved, step, axis)
            else:
                moved = jnp.where(
                    first, pltpu.roll(moved, size - step, axis), pltpu.roll(moved, step, axis)
                )
            out.append((kept, moved))
        (s0, s1), (e0, e1) = out
        s, miss = two_sum(s0, s1)
        return s, (e0 + e1) + miss

    def tree(items, axis, steps):
        for step in steps:
            half = len(items) // 2
            items = [merge(items[n], items[n + half], axis, step) for n in range(half)]
        return items[0]

    columns = []
    for j in range(8):
        i_list = [sums.get((min(i, j), max(i, j)), (zero, zero)) for i in range(8)]
        columns.append(tree(i_list, 0, (4, 2, 1)) if j < VECS else (zero, zero))
    s, e = tree(columns, 1, (64, 32, 16))
    low = (lane & R) == 0
    s1 = jnp.where(low, pltpu.roll(s, LANES - R, 1), pltpu.roll(s, R, 1))
    e1 = jnp.where(low, pltpu.roll(e, LANES - R, 1), pltpu.roll(e, R, 1))
    s, miss = two_sum(s, s1)
    e = (e + e1) + miss
    s, e = quick_sum(s, e)
    chunk = jnp.where(low, s, e)
    folded = chunk
    for r, turn in ((1, 3), (2, 5), (3, 7)):
        other = pltpu.roll(pltpu.roll(chunk, turn, 0), 2 * R * (r + 1), 1)
        folded = jnp.where((sub == r) & (lane // (2 * R) < r), other, folded)
    for n in range(gram_ref.shape[0] // 4):
        gram_ref[4 * n : 4 * n + 4] = folded[:4]


def finish_kernel(gram_ref, f_ref, guess_ref, mine_ref, halo_ref, x_ref, r_ref):
    rows, cols = x_ref.shape[:2]
    coef = coefficients(mine_ref, halo_ref, cols)
    tiles = (cols + 2 * HALO) // 8
    lane = lax.broadcasted_iota(jnp.int32, (8, LANES), 1)
    sub = lax.broadcasted_iota(jnp.int32, (8, LANES), 0)
    pairs = gram_ref.shape[0] // 8
    ways = math.gcd(pairs, 8)
    zero = jnp.zeros((8, LANES), jnp.float32)

    def plus(a, b):
        s, miss = two_sum(a[0], b[0])
        return s, (a[1] + b[1]) + miss

    def total(items):
        while len(items) > 1:
            half = len(items) // 2
            pairs = [plus(items[2 * n], items[2 * n + 1]) for n in range(half)]
            items = pairs + items[2 * half :]
        return items[0]

    def gather(n, carry):
        out = []
        for w, (s, e) in enumerate(carry):
            at = pl.multiple_of((n * ways + w) * 8, 8)
            s, miss = two_sum(s, gram_ref[pl.ds(at, 8), :])
            out.append((s, e + miss))
        return tuple(out)

    steps = pairs // ways
    s, e = total(
        list(lax.fori_loop(0, steps, gather, ((zero, zero),) * ways, unroll=steps <= 8))
    )
    s, e = plus((s, e), (pltpu.roll(s, 4, 0), pltpu.roll(e, 4, 0)))
    low = (lane & R) == 0
    g_hi = jnp.where(low, s, pltpu.roll(s, R, 1))
    g_lo = jnp.where(low, pltpu.roll(s, LANES - R, 1) + e, s + pltpu.roll(e, R, 1))
    g_hi, g_lo = quick_sum(g_hi, g_lo)

    block = lane // (2 * R)

    def unfold(x):
        for i, turn in ((4, 1), (5, 3), (6, 5)):
            x = jnp.where(sub == i, pltpu.roll(pltpu.roll(x, turn, 0), 2 * R * i, 1), x)
        return x

    def column(x, j):
        turned = jnp.where(block == sub, jnp.broadcast_to(x[j : j + 1], x.shape), 0.0)
        x = jnp.where(sub <= j, jnp.where(block == j, x, 0.0), turned)
        for step in (64, 32, 16):
            x = x + pltpu.roll(x, step, 1)
        return jnp.where(sub < VECS, x, 0.0)

    g_hi, g_lo = unfold(g_hi), unfold(g_lo)
    grams = [(column(g_hi, j), column(g_lo, j)) for j in range(VECS)]
    gram_splits = [split(g[0]) for g in grams]

    def product(a, b, a_split, b_split):
        p = a[0] * b[0]
        (ah, al), (bh, bl) = a_split, b_split
        e = (((ah * bh - p) + ah * bl) + al * bh) + al * bl
        return p, e + (a[0] * b[1] + a[1] * b[0])

    def minus(a, factor, b):
        p, e = two_prod(factor, b[0])
        s, miss = two_sum(a[0], -p)
        return quick_sum(s, (a[1] - (e + factor * b[1])) + miss)


    def list_image(p):
        out = [(SHIFT * p[0][0], SHIFT * p[0][1])]
        for k in range(1, len(p)):
            out.append(quick_sum(*plus((SHIFT * p[k][0], SHIFT * p[k][1]), p[k - 1])))
        return out + [p[-1]]

    def sub_image(p):
        moved = pltpu.roll(p[0], 1, 0), pltpu.roll(p[1], 1, 0)
        return quick_sum(*plus((SHIFT * p[0], SHIFT * p[1]), moved))

    def list_minus(a, factor, b):
        a = a + [(zero, zero)] * (len(b) - len(a))
        return [minus(x, factor, y) for x, y in zip(a, b)]

    def apply_gram(p):
        return quick_sum(
            *total([product(g, x, gs, split(x[0])) for g, gs, x in zip(grams, gram_splits, p)])
        )

    def dot(a, b):
        p, e = product(a, b, split(a[0]), split(b[0]))
        for step in (4, 2, 1):
            p, e = plus((p, e), (pltpu.roll(p, step, 0), pltpu.roll(e, step, 0)))
        return quick_sum(p, e)

    as_list = [(zero + 1.0, zero)]
    as_sub = (jnp.where(sub == 0, 1.0, 0.0), zero)
    gained = []
    for cycle in range(CYCLES):
        list1 = list_image(as_list)
        list2 = list_image(list1)
        sub1 = sub_image(as_sub)
        sub2 = sub_image(sub1)
        y0, y1, y2 = apply_gram(as_list), apply_gram(list1), apply_gram(list2)
        m00, m01, m02 = dot(as_sub, y0), dot(sub1, y0), dot(sub2, y0)
        m11, m12, m22 = dot(sub1, y1), dot(sub2, y1), dot(sub2, y2)
        alpha = m00[0] / m01[0]
        along = minus(m01, alpha, minus(plus(m02, m11), alpha, m12))
        power = minus(m11, alpha, minus((2.0 * m12[0], 2.0 * m12[1]), alpha, m22))
        omega = along[0] / power[0]
        if cycle + 1 < CYCLES:
            half_list = list_minus(as_list, alpha, list1)
            turn_list = list_minus(list1, alpha, list2)
            gained = gained + [zero] * (len(half_list) - len(gained))
            for k, one in enumerate(half_list):
                gained[k] = gained[k] + (omega / SCALE) * one[0]
            for k, one in enumerate(as_list):
                gained[k] = gained[k] + (alpha / SCALE) * one[0]
            as_list = list_minus(half_list, omega, turn_list)
            as_sub = minus(minus(as_sub, alpha, sub1), omega, minus(sub1, alpha, sub2))

    def combine(i, t, h):
        at = slice(8 * t, 8 * t + 8)
        out = as_list[0][0] * f_ref[1, h, i, at]
        for k in range(1, len(as_list)):
            out = out + as_list[k][0] * f_ref[k + 1, h, i, at]
        return out

    def grid(reach, make):
        out = {}
        for i in range(DEPTH - reach, DEPTH + rows + reach):
            shown = tiles_within(reach - reach_of(i, rows), cols)
            row = make(i, shown)
            out[i] = [[row.get((h, t), zero) for t in range(tiles)] for h in range(2)]
        return out

    residual = grid(
        2, lambda i, shown: {(h, t): combine(i, t, h) for h in range(2) for t in shown}
    )

    def image_row(values, i, shown):
        return stencil_row(values[i - 1], values[i], values[i + 1], coef, i - 1, shown)

    def half_row(i, shown):
        images = image_row(residual, i, shown)
        return {(h, t): residual[i][h][t] - alpha * image for (h, t), image in images.items()}

    half = grid(1, half_row)
    for i in range(DEPTH, DEPTH + rows):
        own = range(HALO // 8, (HALO + cols) // 8)
        for (h, t), turned in image_row(half, i, own).items():
            at = slice(8 * t, 8 * t + 8)
            out = (i - DEPTH, slice(8 * t - HALO, 8 * t - HALO + 8), slice(h * LANES, (h + 1) * LANES))
            x = gained[0] * f_ref[1, h, i, at]
            for k in range(1, len(gained)):
                x = x + gained[k] * f_ref[k + 1, h, i, at]
            mine = guess_ref[h, i, 8 * t - HALO : 8 * t - HALO + 8]
            x = (mine + x) + (alpha / SCALE) * residual[i][h][t]
            x_ref[out] = x + (omega / SCALE) * half[i][h][t]
            r_ref[out] = half[i][h][t] - omega * turned


def body(adjoint_guess, velocity, leaf_rate, canopy, solid, receptors):
    rows, cols, lanes = adjoint_guess.shape
    ngx, ngy = lax.axis_size("gx"), lax.axis_size("gy")
    devices = ngx * ngy
    width = cols + 2 * HALO
    win = rows + 2 * DEPTH
    vmem = pl.BlockSpec(memory_space=pltpu.VMEM)
    hbm = pl.BlockSpec(memory_space=pltpu.HBM)
    wide = lanes + 4 * NZ
    own, far_rows = pl.pallas_call(
        pack_kernel,
        out_shape=(
            pltpu.VMEM((rows, cols, wide), jnp.float32),
            pltpu.VMEM((DEPTH - rows, cols, wide), jnp.float32),
        ),
        in_specs=[hbm] * 5,
        out_specs=(vmem, vmem),
        scratch_shapes=[
            pltpu.VMEM(velocity.shape, jnp.float32),
            pltpu.VMEM(leaf_rate.shape, jnp.float32),
            pltpu.VMEM(canopy.shape, jnp.int32),
            pltpu.VMEM(solid.shape, jnp.int32),
            pltpu.SemaphoreType.DMA((5,)),
        ],
        compiler_params=pltpu.CompilerParams(vmem_limit_bytes=56 * 1024 * 1024),
        name="pack",
    )(adjoint_guess, velocity, leaf_rate, canopy, solid)
    def swap(x, axis, pairs):
        return lax.ppermute(x, axis, pairs + [(j, i) for i, j in pairs])

    place = lax.axis_index("gx")
    far = swap(far_rows, "gx", [(j, j + 2) for j in range(ngx - 2) if j % 4 < 2])
    pair = swap(own, "gx", [(j, j + 1) for j in range(0, ngx - 1, 2)])
    across = swap(own, "gx", [(j, j + 1) for j in range(1, ngx - 1, 2)])
    if ngx > 4:
        other = jnp.where(place % 4 < 2, own[: DEPTH - rows], own[2 * rows - DEPTH :])
        farther = swap(other, "gx", [(j, j + 2) for j in range(ngx - 2) if j % 4 >= 2])
    else:
        farther = jnp.zeros_like(far_rows)

    def exchange_edges(kernel, tiles, name, *blocks):
        edge = pltpu.VMEM((tiles, HALO, wide), jnp.float32)
        outer, inner = pl.pallas_call(
            kernel,
            out_shape=(edge, edge),
            in_specs=[vmem] * len(blocks),
            out_specs=(vmem, vmem),
            compiler_params=pltpu.CompilerParams(vmem_limit_bytes=8 * 1024 * 1024),
            name=name,
        )(*blocks)
        return (
            swap(outer, "gy", [(j, j + 1) for j in range(1, ngy - 1, 2)]),
            swap(inner, "gy", [(j, j + 1) for j in range(0, ngy - 1, 2)]),
        )

    outer_own, inner_own = exchange_edges(sides_kernel, rows, "sides", own)
    outer, inner = exchange_edges(
        edges_kernel, 2 * (DEPTH // 2), "edges", own, pair, across, far, farther
    )

    source_lane = jnp.arange(4 * NZ)[:, None]
    wide_lane = jnp.arange(4 * NZ * R)[None, :]
    spread = (source_lane == wide_lane // R).astype(jnp.bfloat16)
    spread = jnp.concatenate([spread] * 3, axis=0)
    guess, mine = pl.pallas_call(
        central_kernel,
        out_shape=(
            pltpu.VMEM((2, win, cols, LANES), jnp.float32),
            pltpu.VMEM((7, 2, win - 2, cols, LANES), jnp.float32),
        ),
        in_specs=[vmem] * 6,
        out_specs=(vmem, vmem),
        scratch_shapes=[
            pltpu.VMEM(((win - 2) * cols, LANES), jnp.float32),
            pltpu.VMEM(((win - 2) * cols, 8 * LANES), jnp.float32),
        ],
        compiler_params=pltpu.CompilerParams(vmem_limit_bytes=16 * 1024 * 1024),
        name="central",
    )(own, pair, across, far, farther, spread)

    total_cols = cols * ngy
    cells = jnp.stack([receptors // total_cols, receptors % total_cols])
    halo_rows = win - 4
    gram, basis, halo = pl.pallas_call(
        functools.partial(krylov_kernel, rows, cols),
        out_shape=(
            jax.ShapeDtypeStruct((devices * 4, LANES), jnp.float32),
            pltpu.VMEM((DEPTH + 1, 2, win, width, LANES), jnp.float32),
            pltpu.VMEM((7, 2, win - 2, 2 * HALO, LANES), jnp.float32),
        ),
        in_specs=[pl.BlockSpec(memory_space=pl.ANY)] + [vmem] * 7,
        out_specs=(vmem, vmem, vmem),
        scratch_shapes=[
            pltpu.VMEM((halo_rows * 2 * HALO, LANES), jnp.float32),
            pltpu.VMEM((halo_rows * 2 * HALO, 8 * LANES), jnp.float32),
            pltpu.SMEM((2, R), jnp.int32),
            pltpu.SemaphoreType.DMA(()),
        ],
        compiler_params=pltpu.CompilerParams(vmem_limit_bytes=24 * 1024 * 1024),
        name="krylov",
    )(cells, outer_own, inner_own, outer, inner, guess, mine, spread)
    everyone = lax.all_to_all(gram, ("gx", "gy"), 0, 0, tiled=True)
    out = jax.ShapeDtypeStruct((rows, cols, lanes), jnp.float32)
    return pl.pallas_call(
        finish_kernel,
        out_shape=(out, out),
        in_specs=[vmem] * 5,
        out_specs=(vmem, vmem),
        compiler_params=pltpu.CompilerParams(vmem_limit_bytes=16 * 1024 * 1024),
        name="finish",
    )(everyone, basis, guess, mine, halo)


def solution(mesh):
    return jax.shard_map(
        body,
        mesh=mesh,
        in_specs=(
            P("gx", "gy", None),
            P(None, "gx", "gy"),
            P("gx", "gy"),
            P("gx", "gy"),
            P("gx", "gy"),
            P(),
        ),
        out_specs=(P("gx", "gy", None), P("gx", "gy", None)),
        check_vma=False,
    )
```

```python
import functools
import math

import jax
import jax.numpy as jnp
from jax import lax
from jax.experimental import pallas as pl
from jax.experimental.pallas import tpu as pltpu
from jax.sharding import PartitionSpec as P

NZ = 32
R = 8
CYCLES = 3
DEPTH = 2 * CYCLES + 1
VECS = DEPTH
HALO = 8
SCALE = 16.0
SHIFT = 2.0
LANES = 128

horiz_diff = 4.0
vert_diff = 2.0
decay_rate = 3.5
penalty = 40.0
leaf_gain = 4.0
source_gain = 32.0


def two_sum(a, b):
    s = a + b
    t = s - a
    return s, (a - (s - t)) + (b - t)


def quick_sum(a, b):
    s = a + b
    return s, b - (s - a)


def split(a):
    c = a * 4097.0
    hi = c - (c - a)
    return hi, a - hi


def two_prod(a, b):
    p = a * b
    ah, al = split(a)
    bh, bl = split(b)
    return p, (((ah * bh - p) + ah * bl) + al * bh) + al * bl


def pack_kernel(
    guess_ref, velocity_ref, leaf_ref, canopy_ref, solid_ref, out_ref, far_ref,
    v_ref, l_ref, c_ref, s_ref, sem,
):
    copies = [
        pltpu.make_async_copy(velocity_ref, v_ref, sem.at[0]),
        pltpu.make_async_copy(leaf_ref, l_ref, sem.at[1]),
        pltpu.make_async_copy(canopy_ref, c_ref, sem.at[2]),
        pltpu.make_async_copy(solid_ref, s_ref, sem.at[3]),
        pltpu.make_async_copy(guess_ref, out_ref.at[:, :, pl.ds(0, NZ * R)], sem.at[4]),
    ]
    for copy in copies:
        copy.start()
    for copy in copies[:4]:
        copy.wait()
    rows, cols = guess_ref.shape[:2]
    lane = lax.broadcasted_iota(jnp.int32, (8, LANES), 1)
    sub = lax.broadcasted_iota(jnp.int32, (8, LANES), 0)
    reaction = penalty * s_ref[...].astype(jnp.float32) + leaf_gain * l_ref[...] * c_ref[
        ...
    ].astype(jnp.float32)
    fields = [v_ref[0], v_ref[1], v_ref[2], reaction]
    for x in range(rows):
        for t in range(cols // 8):
            base = 8 * t * NZ
            spread = []
            for field in fields:
                near = field[x : x + 1, base : base + LANES]
                far = field[x : x + 1, base + LANES : base + 2 * LANES]
                spread.append(
                    jnp.where(
                        sub < 4,
                        jnp.broadcast_to(near, (8, LANES)),
                        jnp.broadcast_to(far, (8, LANES)),
                    )
                )
            whole = None
            for d in range(4):
                mixed = spread[d]
                for s in range(1, 4):
                    mixed = jnp.where(sub % 4 == s, spread[(s + d) % 4], mixed)
                if d == 0:
                    whole = mixed
                else:
                    here = (lane // NZ - sub) % 4 == d
                    whole = jnp.where(here, pltpu.roll(mixed, NZ * d, 1), whole)
            out_ref[x, 8 * t : 8 * t + 8, NZ * R :] = whole
    copies[4].wait()
    count = far_ref.shape[0]
    first = jnp.where(lax.axis_index("gx") % 4 < 2, rows - count, 0)
    for x in range(count):
        far_ref[x] = out_ref[first + x]


def window_row(i, rows, a, own, even, odd, far, farther):
    at = i - DEPTH
    if 0 <= at < rows:
        return own(at)
    if -rows <= at < 0:
        return jnp.where(a % 2 == 1, even(at + rows), odd(at + rows))
    if rows <= at < 2 * rows:
        return jnp.where(a % 2 == 1, odd(at - rows), even(at - rows))
    if at < 0:
        return jnp.where(a % 4 >= 2, far(at + DEPTH), farther(at + DEPTH))
    return jnp.where(a % 4 >= 2, farther(at - 2 * rows), far(at - 2 * rows))


def sides_kernel(own_ref, outer_ref, inner_ref):
    cols = own_ref.shape[1]
    odd = lax.axis_index("gy") % 2 == 1
    for n in range(own_ref.shape[0]):
        left, right = own_ref[n, :HALO, :], own_ref[n, cols - HALO :, :]
        outer_ref[n] = jnp.where(odd, right, left)
        inner_ref[n] = jnp.where(odd, left, right)


def edges_kernel(
    own_ref, pair_ref, across_ref, far_ref, farther_ref, outer_ref, inner_ref
):
    rows, cols, wide = own_ref.shape
    place = lax.axis_index("gx")
    odd = lax.axis_index("gy") % 2 == 1
    sub = lax.broadcasted_iota(jnp.int32, (8, wide), 0)
    refs = (own_ref, pair_ref, across_ref, far_ref, farther_ref)

    def edge(right):
        c0 = cols - HALO if right else 0
        blocks = [lambda x, ref=ref: ref[x, c0 : c0 + HALO, :] for ref in refs]
        tiles = []
        for start, way in ((DEPTH, -1), (DEPTH + rows - 1, 1)):
            for d in range(1, DEPTH // 2 + 1):
                close = window_row(start + way * d, rows, place, *blocks)
                distant = window_row(start + way * (DEPTH - d), rows, place, *blocks)
                distant = pltpu.roll(distant, d if right else HALO - d, 0)
                if right:
                    kept = sub >= HALO - DEPTH + d
                else:
                    kept = sub < DEPTH - d
                tiles.append(jnp.where(kept, close, distant))
        return tiles

    for n, (left, right) in enumerate(zip(edge(False), edge(True))):
        outer_ref[n] = jnp.where(odd, right, left)
        inner_ref[n] = jnp.where(odd, left, right)


def reach_of(i, rows):
    return max(DEPTH - i, i - (DEPTH + rows - 1), 0)


def tiles_within(reach, cols):
    shown = []
    for t in range((cols + 2 * HALO) // 8):
        away = max(HALO - (8 * t + 7), 8 * t - (HALO + cols) + 1, 0)
        if away <= reach:
            shown.append(t)
    return shown


def stencil_row(west, mid, east, coef, at, shown):
    lane = lax.broadcasted_iota(jnp.int32, (8, LANES), 1)
    sub = lax.broadcasted_iota(jnp.int32, (8, LANES), 0)
    tiles = len(mid[0])
    ahead = [[pltpu.roll(m, 7, 0) for m in mid[h]] for h in range(2)]
    behind = [[pltpu.roll(m, 1, 0) for m in mid[h]] for h in range(2)]
    images = {}
    for t in shown:
        up = [pltpu.roll(mid[h][t], LANES - R, 1) for h in range(2)]
        down = [pltpu.roll(mid[h][t], R, 1) for h in range(2)]
        above = [jnp.where(lane < LANES - R, up[0], up[1]), up[1]]
        below = [down[0], jnp.where(lane >= R, down[1], down[0])]
        for h in range(2):
            north, south = ahead[h][t], behind[h][t]
            if t + 1 < tiles:
                north = jnp.where(sub < 7, north, ahead[h][t + 1])
            if t > 0:
                south = jnp.where(sub > 0, south, behind[h][t - 1])
            near = [mid[h][t], east[h][t], west[h][t], north, south, above[h], below[h]]
            terms = [coef(c, h, at, t) * near[c] for c in range(7)]
            image = (terms[0] - terms[1]) - (terms[2] + terms[3])
            images[h, t] = image - ((terms[4] + terms[5]) + terms[6])
    return images


def own_tile(t, cols):
    return t - HALO // 8 if HALO <= 8 * t < HALO + cols else None


def coefficients(own_ref, halo_ref, cols):
    def read(c, h, at, t):
        n = own_tile(t, cols)
        if n is not None:
            return own_ref[c, h, at, 8 * n : 8 * n + 8]
        side = 0 if 8 * t < HALO else 8
        return halo_ref[c, h, at, side : side + 8]

    return read


def inside_row(i, rows):
    at = lax.axis_index("gx") * rows - DEPTH + i
    ok = jnp.logical_and(at >= 0, at < rows * lax.axis_size("gx"))
    return jnp.where(ok, 1.0, 0.0)


def widen(raw, spread):
    first = raw.astype(jnp.bfloat16)
    rest = raw - first.astype(jnp.float32)
    second = rest.astype(jnp.bfloat16)
    third = (rest - second.astype(jnp.float32)).astype(jnp.bfloat16)
    pieces = jnp.concatenate([first, second, third], axis=1)
    return jnp.dot(pieces, spread, preferred_element_type=jnp.float32)


def tile_coefficients(wide_ref, at, h, keep):
    lane = lax.broadcasted_iota(jnp.int32, (8, LANES), 1)
    u, v, w, reaction = [
        wide_ref[at : at + 8, (2 * c + h) * LANES : (2 * c + h + 1) * LANES] for c in range(4)
    ]
    side = [
        horiz_diff + jnp.maximum(u, 0.0),
        horiz_diff + jnp.maximum(-u, 0.0),
        horiz_diff + jnp.maximum(v, 0.0),
        horiz_diff + jnp.maximum(-v, 0.0),
        vert_diff + jnp.maximum(w, 0.0),
        vert_diff + jnp.maximum(-w, 0.0),
    ]
    diag = decay_rate + reaction
    for one in side:
        diag = diag + one
    if h == 1:
        side[4] = jnp.where(lane < LANES - R, side[4], 0.0)
    else:
        side[5] = jnp.where(lane >= R, side[5], 0.0)
    return [one * keep for one in [diag] + side]


def central_kernel(
    own_ref, pair_ref, across_ref, far_ref, farther_ref, ex_ref, guess_ref, coef_ref,
    raw_ref, wide_ref,
):
    rows, cols, _ = own_ref.shape
    win = rows + 2 * DEPTH
    place = lax.axis_index("gx")
    refs = (own_ref, pair_ref, across_ref, far_ref, farther_ref)

    def middle(i, lo):
        blocks = [lambda x, ref=ref: ref[x, :, lo : lo + LANES] for ref in refs]
        return window_row(i, rows, place, *blocks)

    for i in range(win):
        for h in range(2):
            guess_ref[h, i] = middle(i, h * LANES) * inside_row(i, rows)
    for i in range(win - 2):
        raw_ref[i * cols : (i + 1) * cols, :] = middle(i + 1, 2 * LANES)
    wide_ref[...] = widen(raw_ref[...], ex_ref[...])
    for i in range(win - 2):
        keep = inside_row(i + 1, rows) * (1.0 / SCALE)
        for t in range(cols // 8):
            for h in range(2):
                values = tile_coefficients(wide_ref, i * cols + 8 * t, h, keep)
                for c, one in enumerate(values):
                    coef_ref[c, h, i, 8 * t : 8 * t + 8] = one


def krylov_kernel(
    rows, cols, rec_ref, outer_own_ref, inner_own_ref, outer_ref, inner_ref, guess_ref, mine_ref, ex_ref, gram_ref, f_ref,
    halo_ref, raw_ref, wide_ref, cell_ref, cell_sem,
):
    fetch = pltpu.make_async_copy(rec_ref, cell_ref, cell_sem)
    fetch.start()
    win = rows + 2 * DEPTH
    width = cols + 2 * HALO
    tiles = width // 8
    odd = lax.axis_index("gy") % 2 == 1
    total_cols = cols * lax.axis_size("gy")
    row0 = lax.axis_index("gx") * rows - DEPTH
    col0 = lax.axis_index("gy") * cols - HALO
    lane = lax.broadcasted_iota(jnp.int32, (8, LANES), 1)
    sub = lax.broadcasted_iota(jnp.int32, (8, LANES), 0)
    sides = ((0, True), (HALO + cols, False))

    def edge(i, lo, right):
        away = reach_of(i, rows)
        refs = outer_ref, inner_ref
        if away == 0:
            refs = outer_own_ref, inner_own_ref
            n, turn = i - DEPTH, 0
        else:
            d = min(away, DEPTH - away)
            n = (0 if i < DEPTH else DEPTH // 2) + d - 1
            turn = 0 if d == away else (HALO - d if right else d)
        outer, inner = [ref[n, :, lo : lo + LANES] for ref in refs]
        tile = jnp.where(odd, inner, outer) if right else jnp.where(odd, outer, inner)
        return pltpu.roll(tile, turn, 0) if turn else tile

    for i in range(1, win - 1):
        for h in range(2):
            for c0, right in sides:
                f_ref[0, h, i, c0 : c0 + HALO] = edge(i, h * LANES, right) * inside_row(i, rows)

    needed = [i for i in range(1, win - 1) if reach_of(i, rows) < DEPTH - 1]
    for n, i in enumerate(needed):
        for side, (c0, right) in enumerate(sides):
            at = (2 * n + side) * HALO
            raw_ref[at : at + HALO, :] = edge(i, 2 * LANES, right)
    wide_ref[...] = widen(raw_ref[...], ex_ref[...])
    for n, i in enumerate(needed):
        for side, (c0, right) in enumerate(sides):
            at_col = col0 + c0 + sub
            seen = jnp.logical_and(at_col >= 0, at_col < total_cols)
            keep = jnp.where(seen, inside_row(i, rows) * (1.0 / SCALE), 0.0)
            for h in range(2):
                values = tile_coefficients(wide_ref, (2 * n + side) * HALO, h, keep)
                for c, one in enumerate(values):
                    halo_ref[c, h, i - 1, side * HALO : (side + 1) * HALO] = one

    coef = coefficients(mine_ref, halo_ref, cols)

    def read(k, h, i, t):
        n = own_tile(t, cols)
        if k == 0 and n is not None:
            return guess_ref[h, i, 8 * n : 8 * n + 8]
        return f_ref[k, h, i, 8 * t : 8 * t + 8]

    def load(k, i):
        return [[read(k, h, i, t) for t in range(tiles)] for h in range(2)]

    def apply(step, finish):
        west, mid = load(step - 1, step - 1), load(step - 1, step)
        for i in range(step, win - step):
            east = load(step - 1, i + 1)
            shown = tiles_within(DEPTH - step - reach_of(i, rows), cols)
            images = stencil_row(west, mid, east, coef, i - 1, shown)
            for (h, t), image in images.items():
                f_ref[step, h, i, 8 * t : 8 * t + 8] = finish(image, mid[h][t])
            west, mid = mid, east

    apply(1, lambda image, mid: -SCALE * image)
    fetch.wait()
    for q in range(R):
        i = cell_ref[0, q] - row0
        c = cell_ref[1, q] - col0
        seen = (i >= 1) & (i < win - 1) & (c >= 0) & (c < width)
        i = jnp.clip(i, 1, win - 2)
        c = jnp.clip(c, 0, width - 1)
        base = pl.multiple_of((c // 8) * 8, 8)
        gain = jnp.where(seen, source_gain, 0.0)
        spot = jnp.where((sub == c % 8) & (lane == R + q), gain, 0.0)
        f_ref[1, 0, i, pl.ds(base, 8)] += spot
    for step in range(2, DEPTH + 1):
        apply(step, lambda image, mid: image - SHIFT * mid)

    pieces = [
        (h, i, t) for h in range(2) for i in range(rows) for t in range(cols // 8)
    ]
    zero = jnp.zeros((8, LANES), jnp.float32)
    sums = {}
    for group in ([0, 1, 2, 3, 4], [5, 6]):
        pairs = [(i, j) for j in group for i in range(j + 1)]

        done = [(zero, zero)] * len(pairs)
        for h, row, t in pieces:
            need = sorted({i for pair in pairs for i in pair})
            at = slice(HALO + 8 * t, HALO + 8 * t + 8)
            full = {k: f_ref[k + 1, h, DEPTH + row, at] for k in need}
            halves = {k: split(full[k]) for k in need}
            hi = {k: halves[k][0] for k in need}
            lo = {k: halves[k][1] for k in need}
            out = []
            for (i, j), (s, e) in zip(pairs, done):
                s, miss = two_sum(s, hi[i] * hi[j])
                if i == j:
                    cross = lo[j] * (hi[i] + full[i])
                else:
                    cross = hi[i] * lo[j] + lo[i] * full[j]
                out.append((s, e + (cross + miss)))
            done = out
        for pair, value in zip(pairs, done):
            sums[pair] = value

    def merge(a, b, axis, step):
        where = (sub if axis == 0 else lane) & step
        first = where == 0
        size = 8 if axis == 0 else LANES
        out = []
        for x, y in zip(a, b):
            kept = jnp.where(first, x, y)
            moved = jnp.where(first, y, x)
            if 2 * step == size:
                moved = pltpu.roll(moved, step, axis)
            else:
                moved = jnp.where(
                    first, pltpu.roll(moved, size - step, axis), pltpu.roll(moved, step, axis)
                )
            out.append((kept, moved))
        (s0, s1), (e0, e1) = out
        s, miss = two_sum(s0, s1)
        return s, (e0 + e1) + miss

    def tree(items, axis, steps):
        for step in steps:
            half = len(items) // 2
            items = [merge(items[n], items[n + half], axis, step) for n in range(half)]
        return items[0]

    columns = []
    for j in range(8):
        i_list = [sums.get((min(i, j), max(i, j)), (zero, zero)) for i in range(8)]
        columns.append(tree(i_list, 0, (4, 2, 1)) if j < VECS else (zero, zero))
    s, e = tree(columns, 1, (64, 32, 16))
    low = (lane & R) == 0
    s1 = jnp.where(low, pltpu.roll(s, LANES - R, 1), pltpu.roll(s, R, 1))
    e1 = jnp.where(low, pltpu.roll(e, LANES - R, 1), pltpu.roll(e, R, 1))
    s, miss = two_sum(s, s1)
    e = (e + e1) + miss
    s, e = quick_sum(s, e)
    chunk = jnp.where(low, s, e)
    folded = chunk
    for r, turn in ((1, 3), (2, 5), (3, 7)):
        other = pltpu.roll(pltpu.roll(chunk, turn, 0), 2 * R * (r + 1), 1)
        folded = jnp.where((sub == r) & (lane // (2 * R) < r), other, folded)
    for n in range(gram_ref.shape[0] // 4):
        gram_ref[4 * n : 4 * n + 4] = folded[:4]


def finish_kernel(gram_ref, f_ref, guess_ref, mine_ref, halo_ref, x_ref, r_ref):
    rows, cols = x_ref.shape[:2]
    coef = coefficients(mine_ref, halo_ref, cols)
    tiles = (cols + 2 * HALO) // 8
    lane = lax.broadcasted_iota(jnp.int32, (8, LANES), 1)
    sub = lax.broadcasted_iota(jnp.int32, (8, LANES), 0)
    pairs = gram_ref.shape[0] // 8
    ways = math.gcd(pairs, 8)
    zero = jnp.zeros((8, LANES), jnp.float32)

    def plus(a, b):
        s, miss = two_sum(a[0], b[0])
        return s, (a[1] + b[1]) + miss

    def total(items):
        while len(items) > 1:
            half = len(items) // 2
            pairs = [plus(items[2 * n], items[2 * n + 1]) for n in range(half)]
            items = pairs + items[2 * half :]
        return items[0]

    def gather(n, carry):
        out = []
        for w, (s, e) in enumerate(carry):
            at = pl.multiple_of((n * ways + w) * 8, 8)
            s, miss = two_sum(s, gram_ref[pl.ds(at, 8), :])
            out.append((s, e + miss))
        return tuple(out)

    steps = pairs // ways
    s, e = total(
        list(lax.fori_loop(0, steps, gather, ((zero, zero),) * ways, unroll=steps <= 8))
    )
    s, e = plus((s, e), (pltpu.roll(s, 4, 0), pltpu.roll(e, 4, 0)))
    low = (lane & R) == 0
    g_hi = jnp.where(low, s, pltpu.roll(s, R, 1))
    g_lo = jnp.where(low, pltpu.roll(s, LANES - R, 1) + e, s + pltpu.roll(e, R, 1))
    g_hi, g_lo = quick_sum(g_hi, g_lo)

    block = lane // (2 * R)

    def unfold(x):
        for i, turn in ((4, 1), (5, 3), (6, 5)):
            x = jnp.where(sub == i, pltpu.roll(pltpu.roll(x, turn, 0), 2 * R * i, 1), x)
        return x

    def column(x, j):
        turned = jnp.where(block == sub, jnp.broadcast_to(x[j : j + 1], x.shape), 0.0)
        x = jnp.where(sub <= j, jnp.where(block == j, x, 0.0), turned)
        for step in (64, 32, 16):
            x = x + pltpu.roll(x, step, 1)
        return jnp.where(sub < VECS, x, 0.0)

    g_hi, g_lo = unfold(g_hi), unfold(g_lo)
    grams = [(column(g_hi, j), column(g_lo, j)) for j in range(VECS)]
    gram_splits = [split(g[0]) for g in grams]

    def product(a, b, a_split, b_split):
        p = a[0] * b[0]
        (ah, al), (bh, bl) = a_split, b_split
        e = (((ah * bh - p) + ah * bl) + al * bh) + al * bl
        return p, e + (a[0] * b[1] + a[1] * b[0])

    def minus(a, factor, b):
        p, e = two_prod(factor, b[0])
        s, miss = two_sum(a[0], -p)
        return quick_sum(s, (a[1] - (e + factor * b[1])) + miss)


    def list_image(p):
        out = [(SHIFT * p[0][0], SHIFT * p[0][1])]
        for k in range(1, len(p)):
            out.append(quick_sum(*plus((SHIFT * p[k][0], SHIFT * p[k][1]), p[k - 1])))
        return out + [p[-1]]

    def sub_image(p):
        moved = pltpu.roll(p[0], 1, 0), pltpu.roll(p[1], 1, 0)
        return quick_sum(*plus((SHIFT * p[0], SHIFT * p[1]), moved))

    def list_minus(a, factor, b):
        a = a + [(zero, zero)] * (len(b) - len(a))
        return [minus(x, factor, y) for x, y in zip(a, b)]

    def apply_gram(p):
        return quick_sum(
            *total([product(g, x, gs, split(x[0])) for g, gs, x in zip(grams, gram_splits, p)])
        )

    def dot(a, b):
        p, e = product(a, b, split(a[0]), split(b[0]))
        for step in (4, 2, 1):
            p, e = plus((p, e), (pltpu.roll(p, step, 0), pltpu.roll(e, step, 0)))
        return quick_sum(p, e)

    as_list = [(zero + 1.0, zero)]
    as_sub = (jnp.where(sub == 0, 1.0, 0.0), zero)
    gained = []
    for cycle in range(CYCLES):
        list1 = list_image(as_list)
        list2 = list_image(list1)
        sub1 = sub_image(as_sub)
        sub2 = sub_image(sub1)
        y0, y1, y2 = apply_gram(as_list), apply_gram(list1), apply_gram(list2)
        m00, m01, m02 = dot(as_sub, y0), dot(sub1, y0), dot(sub2, y0)
        m11, m12, m22 = dot(sub1, y1), dot(sub2, y1), dot(sub2, y2)
        alpha = m00[0] / m01[0]
        along = minus(m01, alpha, minus(plus(m02, m11), alpha, m12))
        power = minus(m11, alpha, minus((2.0 * m12[0], 2.0 * m12[1]), alpha, m22))
        omega = along[0] / power[0]
        if cycle + 1 < CYCLES:
            half_list = list_minus(as_list, alpha, list1)
            turn_list = list_minus(list1, alpha, list2)
            gained = gained + [zero] * (len(half_list) - len(gained))
            for k, one in enumerate(half_list):
                gained[k] = gained[k] + (omega * (1.0 / SCALE)) * one[0]
            for k, one in enumerate(as_list):
                gained[k] = gained[k] + (alpha * (1.0 / SCALE)) * one[0]
            as_list = list_minus(half_list, omega, turn_list)
            as_sub = minus(minus(as_sub, alpha, sub1), omega, minus(sub1, alpha, sub2))

    def combine(i, t, h):
        at = slice(8 * t, 8 * t + 8)
        out = as_list[0][0] * f_ref[1, h, i, at]
        for k in range(1, len(as_list)):
            out = out + as_list[k][0] * f_ref[k + 1, h, i, at]
        return out

    def grid(reach, make):
        out = {}
        for i in range(DEPTH - reach, DEPTH + rows + reach):
            shown = tiles_within(reach - reach_of(i, rows), cols)
            row = make(i, shown)
            out[i] = [[row.get((h, t), zero) for t in range(tiles)] for h in range(2)]
        return out

    residual = grid(
        2, lambda i, shown: {(h, t): combine(i, t, h) for h in range(2) for t in shown}
    )

    def image_row(values, i, shown):
        return stencil_row(values[i - 1], values[i], values[i + 1], coef, i - 1, shown)

    def half_row(i, shown):
        images = image_row(residual, i, shown)
        return {(h, t): residual[i][h][t] - alpha * image for (h, t), image in images.items()}

    half = grid(1, half_row)
    for i in range(DEPTH, DEPTH + rows):
        own = range(HALO // 8, (HALO + cols) // 8)
        for (h, t), turned in image_row(half, i, own).items():
            at = slice(8 * t, 8 * t + 8)
            out = (i - DEPTH, slice(8 * t - HALO, 8 * t - HALO + 8), slice(h * LANES, (h + 1) * LANES))
            x = gained[0] * f_ref[1, h, i, at]
            for k in range(1, len(gained)):
                x = x + gained[k] * f_ref[k + 1, h, i, at]
            mine = guess_ref[h, i, 8 * t - HALO : 8 * t - HALO + 8]
            x = (mine + x) + (alpha * (1.0 / SCALE)) * residual[i][h][t]
            x_ref[out] = x + (omega * (1.0 / SCALE)) * half[i][h][t]
            r_ref[out] = half[i][h][t] - omega * turned


def body(adjoint_guess, velocity, leaf_rate, canopy, solid, receptors):
    rows, cols, lanes = adjoint_guess.shape
    ngx, ngy = lax.axis_size("gx"), lax.axis_size("gy")
    devices = ngx * ngy
    width = cols + 2 * HALO
    win = rows + 2 * DEPTH
    vmem = pl.BlockSpec(memory_space=pltpu.VMEM)
    hbm = pl.BlockSpec(memory_space=pltpu.HBM)
    wide = lanes + 4 * NZ
    own, far_rows = pl.pallas_call(
        pack_kernel,
        out_shape=(
            pltpu.VMEM((rows, cols, wide), jnp.float32),
            pltpu.VMEM((DEPTH - rows, cols, wide), jnp.float32),
        ),
        in_specs=[hbm] * 5,
        out_specs=(vmem, vmem),
        scratch_shapes=[
            pltpu.VMEM(velocity.shape, jnp.float32),
            pltpu.VMEM(leaf_rate.shape, jnp.float32),
            pltpu.VMEM(canopy.shape, jnp.int32),
            pltpu.VMEM(solid.shape, jnp.int32),
            pltpu.SemaphoreType.DMA((5,)),
        ],
        compiler_params=pltpu.CompilerParams(vmem_limit_bytes=56 * 1024 * 1024),
        name="pack",
    )(adjoint_guess, velocity, leaf_rate, canopy, solid)
    def swap(x, axis, pairs):
        return lax.ppermute(x, axis, pairs + [(j, i) for i, j in pairs])

    place = lax.axis_index("gx")
    far = swap(far_rows, "gx", [(j, j + 2) for j in range(ngx - 2) if j % 4 < 2])
    pair = swap(own, "gx", [(j, j + 1) for j in range(0, ngx - 1, 2)])
    across = swap(own, "gx", [(j, j + 1) for j in range(1, ngx - 1, 2)])
    if ngx > 4:
        other = jnp.where(place % 4 < 2, own[: DEPTH - rows], own[2 * rows - DEPTH :])
        farther = swap(other, "gx", [(j, j + 2) for j in range(ngx - 2) if j % 4 >= 2])
    else:
        farther = jnp.zeros_like(far_rows)

    def exchange_edges(kernel, tiles, name, *blocks):
        edge = pltpu.VMEM((tiles, HALO, wide), jnp.float32)
        outer, inner = pl.pallas_call(
            kernel,
            out_shape=(edge, edge),
            in_specs=[vmem] * len(blocks),
            out_specs=(vmem, vmem),
            compiler_params=pltpu.CompilerParams(vmem_limit_bytes=8 * 1024 * 1024),
            name=name,
        )(*blocks)
        return (
            swap(outer, "gy", [(j, j + 1) for j in range(1, ngy - 1, 2)]),
            swap(inner, "gy", [(j, j + 1) for j in range(0, ngy - 1, 2)]),
        )

    outer_own, inner_own = exchange_edges(sides_kernel, rows, "sides", own)
    outer, inner = exchange_edges(
        edges_kernel, 2 * (DEPTH // 2), "edges", own, pair, across, far, farther
    )

    source_lane = jnp.arange(4 * NZ)[:, None]
    wide_lane = jnp.arange(4 * NZ * R)[None, :]
    spread = (source_lane == wide_lane // R).astype(jnp.bfloat16)
    spread = jnp.concatenate([spread] * 3, axis=0)
    guess, mine = pl.pallas_call(
        central_kernel,
        out_shape=(
            pltpu.VMEM((2, win, cols, LANES), jnp.float32),
            pltpu.VMEM((7, 2, win - 2, cols, LANES), jnp.float32),
        ),
        in_specs=[vmem] * 6,
        out_specs=(vmem, vmem),
        scratch_shapes=[
            pltpu.VMEM(((win - 2) * cols, LANES), jnp.float32),
            pltpu.VMEM(((win - 2) * cols, 8 * LANES), jnp.float32),
        ],
        compiler_params=pltpu.CompilerParams(vmem_limit_bytes=16 * 1024 * 1024),
        name="central",
    )(own, pair, across, far, farther, spread)

    total_cols = cols * ngy
    cells = jnp.stack([receptors // total_cols, receptors % total_cols])
    halo_rows = win - 4
    gram, basis, halo = pl.pallas_call(
        functools.partial(krylov_kernel, rows, cols),
        out_shape=(
            jax.ShapeDtypeStruct((devices * 4, LANES), jnp.float32),
            pltpu.VMEM((DEPTH + 1, 2, win, width, LANES), jnp.float32),
            pltpu.VMEM((7, 2, win - 2, 2 * HALO, LANES), jnp.float32),
        ),
        in_specs=[pl.BlockSpec(memory_space=pl.ANY)] + [vmem] * 7,
        out_specs=(vmem, vmem, vmem),
        scratch_shapes=[
            pltpu.VMEM((halo_rows * 2 * HALO, LANES), jnp.float32),
            pltpu.VMEM((halo_rows * 2 * HALO, 8 * LANES), jnp.float32),
            pltpu.SMEM((2, R), jnp.int32),
            pltpu.SemaphoreType.DMA(()),
        ],
        compiler_params=pltpu.CompilerParams(vmem_limit_bytes=24 * 1024 * 1024),
        name="krylov",
    )(cells, outer_own, inner_own, outer, inner, guess, mine, spread)
    everyone = lax.all_to_all(gram, ("gx", "gy"), 0, 0, tiled=True)
    out = jax.ShapeDtypeStruct((rows, cols, lanes), jnp.float32)
    return pl.pallas_call(
        finish_kernel,
        out_shape=(out, out),
        in_specs=[vmem] * 5,
        out_specs=(vmem, vmem),
        compiler_params=pltpu.CompilerParams(vmem_limit_bytes=16 * 1024 * 1024),
        name="finish",
    )(everyone, basis, guess, mine, halo)


def solution(mesh):
    return jax.shard_map(
        body,
        mesh=mesh,
        in_specs=(
            P("gx", "gy", None),
            P(None, "gx", "gy"),
            P("gx", "gy"),
            P("gx", "gy"),
            P("gx", "gy"),
            P(),
        ),
        out_specs=(P("gx", "gy", None), P("gx", "gy", None)),
        check_vma=False,
    )
```
